32 devices in a mesh: grid: 8 (over z, y), tile: 4 (over x, core).
Axes of the slice: x: 2, y: 2, z: 4, core: 2. Of those that a mesh axis runs over, the one named last changes fastest.
Arguments:
- basis_values: bfloat16 [768, 256, 128], P(('grid', 'tile')), may hold values from -6 to 6
- blocks: int32 [768, 2], P(('grid', 'tile')), may hold values from 0 to 47, as said below
- counts: int32 [768], P(('grid', 'tile')), may hold values from 1 to 256, as said below
- weighted_potential: float32 [768, 256], P(('grid', 'tile')), may hold values from -0.12 to 0.12
- xc_kernel: float32 [768, 256], P(('grid', 'tile')), may hold values from -0.002 to -0.0002
- occ_coef: bfloat16 [8192, 512], P('grid'), may hold values from -0.5 to 0.5
- virt_coef: bfloat16 [8192, 7680], P('grid', 'tile'), may hold values from -0.0625 to 0.0625
- occ_energy: float32 [512], replicated, may hold values from -2 to -0.5
- virt_energy: float32 [7680], P('tile'), may hold values from 0.3 to 8
Outputs:
- response_coef: bfloat16 [8192, 512], P('grid')
- response_potential: float32 [768, 256], P(('grid', 'tile'))
The draws below stay inside these ranges and needn't reach their ends.
Inputs may be any that keep to these rules, and one draw needn't show every extreme that they name: Each row names 2 different blocks of the window of 48 blocks around the batch's region. The live points of batch b are its first counts[b] slots; every device holds at least one full batch.
All inputs are finite; a program needn't handle non-finite values.
Results may differ from the reference program's by a relative error of at most 0.0061.
Values may be sent and summed in bfloat16 or wider, within the bound.
No kernel may reach another device: no remote copies, remote signals or barrier semaphores. Data moves between devices by JAX's collectives and lax.ppermute only.
A program may use at most 128 MiB of HBM per device.

```python
import math
import jax
import jax.numpy as jnp
from jax import lax

NB = 8192
NOCC = 512
BB = 64
KB = 2
PTS = 256
NBATCH = 24
NV = 7680
NBLK = 128
BLK = 16
BATCHES = 768
N_GRID = 8
N_TILE = 4


def draw_blocks(key, part):
    keys = jax.random.split(jax.random.fold_in(key, 11), BATCHES)
    orders = jax.vmap(lambda single: jax.random.permutation(single, 3 * BLK))(keys)
    return orders[:, :KB].astype(jnp.int32)


def draw_counts(key, part):
    first_key, second_key, third_key = jax.random.split(jax.random.fold_in(key, 23), 3)
    groups = BATCHES // NBATCH
    caps = jax.random.randint(first_key, (groups,), PTS // 4, PTS + 1)
    cap_each = jnp.repeat(caps, NBATCH, total_repeat_length=BATCHES)
    lowest = jnp.maximum(cap_each // 2, 1)
    fraction = jax.random.randint(second_key, (BATCHES,), 0, 1 << 20)
    chosen = lowest + fraction * (cap_each - lowest + 1) // (1 << 20)
    picked = jax.random.randint(third_key, (groups,), 0, NBATCH)
    slot = jnp.arange(BATCHES, dtype=jnp.int32) % NBATCH
    full_slot = slot == jnp.repeat(picked, NBATCH, total_repeat_length=BATCHES)
    return jnp.where(full_slot, PTS, chosen).astype(jnp.int32)


def levels(own_key, shape, cuts, least, high):
    loudness, own = 1.0, jax.random.fold_in(own_key, 6)
    for dim, shards_of in cuts:
        steps = jnp.exp(jax.random.uniform(jax.random.fold_in(own, dim), (shards_of,), jnp.float32, least / len(cuts), high / len(cuts)))
        loudness = loudness * jnp.repeat(steps, shape[dim] // shards_of).reshape([-1 if axis == dim else 1 for axis in range(len(shape))])
    return loudness


def noise(rng, dims, deviation, limit, pieces=(), held_as=jnp.bfloat16):
    entries = jax.random.normal(rng, dims, jnp.float32) * deviation
    if len(pieces) > 0:
        entries = levels(rng, dims, pieces, -0.22, 0.18) * entries
    return jnp.clip(entries, min=-limit, max=limit).astype(held_as)


def setup_inputs(seed: int = 0) -> dict:
    seeds = jax.random.split(jax.random.key(seed), 10)
    return {
        "basis_values": noise(seeds[0], (BATCHES, PTS, KB * BB), 1.0, 6.0, ((0, 32),)),
        "blocks": draw_blocks(jax.random.fold_in(seeds[9], 71), 0),
        "counts": draw_counts(jax.random.fold_in(seeds[9], 71), 0),
        "weighted_potential": noise(seeds[3], (BATCHES, PTS), 0.02, 0.12, ((0, 32),), jnp.float32),
        "xc_kernel": jnp.clip(-0.002 + 0.0018000001 * jax.random.uniform(seeds[4], (BATCHES, PTS), jnp.float32) ** levels(seeds[4], (BATCHES, PTS), ((0, 32),), -0.2, 0.2), -0.002, -0.0002),
        "occ_coef": noise(seeds[5], (NB, NOCC), (KB * BB) ** -0.5, 0.5, ((0, 8),)),
        "virt_coef": noise(seeds[6], (NB, NV), NB ** -0.5, 0.0625, ((0, 8), (1, 4))),
        "occ_energy": jnp.clip(jax.random.uniform(seeds[7], (NOCC,), jnp.float32, -2.0, -0.5), -2.0, -0.5),
        "virt_energy": jnp.clip(jnp.exp(math.log(8.0) - 3.2834143 * jax.random.uniform(seeds[8], (NV,), jnp.float32) ** levels(seeds[8], (NV,), ((0, 4),), -0.2, 0.2)), 0.3, 8.0),
    }


def basis_rows(region, blocks_here):
    first_block = (region * BLK - BLK + blocks_here) % NBLK
    offsets = jnp.arange(BB, dtype=jnp.int32)
    rows_index = first_block[:, :, None] * BB + offsets[None, None, :]
    return rows_index.reshape(blocks_here.shape[0], KB * BB).astype(jnp.int32)


def reference(basis_values, blocks, counts, weighted_potential, xc_kernel, occ_coef, virt_coef, occ_energy, virt_energy):
    per_region = N_TILE * NBATCH
    values_split = basis_values.reshape(N_GRID, per_region, PTS, KB * BB)
    blocks_split = blocks.reshape(N_GRID, per_region, KB)
    counts_split = counts.reshape(N_GRID, per_region)
    potential_split = weighted_potential.reshape(N_GRID, per_region, PTS)
    kernel_split = xc_kernel.reshape(N_GRID, per_region, PTS)
    regions = jnp.arange(N_GRID, dtype=jnp.int32)
    point_index = jnp.arange(PTS, dtype=jnp.int32)
    occ_float = occ_coef.astype(jnp.float32)

    def integrate(ham_sum, inputs):
        region, values_here, blocks_here, counts_here, potential_here = inputs
        rows_index = basis_rows(region, blocks_here)
        values_float = values_here.astype(jnp.float32)
        occ_rows = occ_float[rows_index]
        occ_values = jnp.einsum("bpk,bko->bpo", values_float, occ_rows)
        live_mask = point_index[None, :] < counts_here[:, None]
        weights = jnp.where(live_mask, potential_here, jnp.zeros_like(potential_here))
        scaled = (weights[:, :, None] * occ_values).astype(jnp.bfloat16)
        scaled = lax.optimization_barrier(scaled).astype(jnp.float32)
        contrib = jnp.einsum("bpk,bpo->bko", values_float, scaled)
        ham_sum = ham_sum.at[rows_index.reshape(-1)].add(contrib.reshape(-1, NOCC))
        return ham_sum, None

    ham_sum, unused = lax.scan(integrate, jnp.zeros((NB, NOCC), jnp.float32),
                               (regions, values_split, blocks_split, counts_split, potential_split))
    ham_occ = ham_sum.astype(jnp.bfloat16)
    virt_ham = jnp.dot(virt_coef.T, ham_occ, preferred_element_type=jnp.float32)
    rotation = (virt_ham / (occ_energy[None, :] - virt_energy[:, None])).astype(jnp.bfloat16)
    response_coef = jnp.dot(virt_coef, rotation, preferred_element_type=jnp.float32).astype(jnp.bfloat16)
    coef_float = response_coef.astype(jnp.float32)

    def respond(carry, inputs):
        region, values_here, blocks_here, counts_here, kernel_here = inputs
        rows_index = basis_rows(region, blocks_here)
        values_float = values_here.astype(jnp.float32)
        occ_values = jnp.einsum("bpk,bko->bpo", values_float, occ_float[rows_index])
        resp_values = jnp.einsum("bpk,bko->bpo", values_float, coef_float[rows_index])
        density = 4.0 * jnp.sum(occ_values * resp_values, axis=2)
        live_mask = point_index[None, :] < counts_here[:, None]
        result = jnp.where(live_mask, kernel_here * density, jnp.zeros_like(density))
        return carry, result

    unused_carry, potential_out = lax.scan(respond, jnp.zeros((), jnp.float32),
                                           (regions, values_split, blocks_split, counts_split, kernel_split))
    return response_coef, potential_out.reshape(BATCHES, PTS)
```

```python
import functools

import jax
import jax.numpy as jnp
from jax import lax
from jax.experimental import pallas as pl
from jax.experimental.pallas import tpu as pltpu
from jax.sharding import PartitionSpec as P

VMEM = pl.BlockSpec(memory_space=pltpu.VMEM)
SMEM = pl.BlockSpec(memory_space=pltpu.SMEM)
LIMIT = 40 * 1024 * 1024
LANES = 128
F32 = jnp.float32
BF16 = jnp.bfloat16
NT = (((1,), (1,)), ((), ()))


def params():
    return pltpu.CompilerParams(vmem_limit_bytes=LIMIT)


def split_dot(full, other, dims):
    high = full.astype(BF16)
    low = (full - high.astype(F32)).astype(BF16)
    return lax.dot_general(high, other, dims, preferred_element_type=F32) + lax.dot_general(
        low, other, dims, preferred_element_type=F32
    )


def integrate_kernel(basis_ref, weights_ref, out_ref):
    def step(b, carry):
        values = basis_ref[b]
        weighted = values.astype(F32).T * weights_ref[b]
        out_ref[b] = split_dot(weighted, values, (((1,), (0,)), ((), ()))).astype(BF16)
        return carry

    lax.fori_loop(0, basis_ref.shape[0], step, 0, unroll=4)


def integrate(basis_values, weights):
    nbatch, points, columns = basis_values.shape
    return pl.pallas_call(
        integrate_kernel,
        out_shape=jax.ShapeDtypeStruct((nbatch, columns, columns), BF16),
        in_specs=[VMEM, VMEM],
        out_specs=VMEM,
        compiler_params=params(),
        cost_estimate=pl.CostEstimate(
            flops=4 * nbatch * points * columns * columns,
            bytes_accessed=basis_values.size * 2 + nbatch * columns * columns * 2,
            transcendentals=0,
        ),
    )(basis_values, weights.reshape(nbatch, 1, points))


def apply_kernel(pieces, per_batch, rows, *refs):
    block_refs, ham_refs = refs[:pieces], refs[pieces : 2 * pieces]
    before_ref, own_ref, after_ref = refs[2 * pieces : 2 * pieces + 3]
    out_before, out_own, out_after = refs[2 * pieces + 3 : 2 * pieces + 6]
    window, total = refs[2 * pieces + 6 :]
    region = own_ref.shape[0]
    window[:region] = before_ref[...]
    window[region : 2 * region] = own_ref[...]
    window[2 * region :] = after_ref[...]
    total[...] = jnp.zeros_like(total)
    nbatch = ham_refs[0].shape[0]

    def step(b, carry):
        places, products = [], []
        for p in range(pieces):
            place = [
                pl.ds(pl.multiple_of(block_refs[p][b, j] * rows, rows), rows)
                for j in range(per_batch)
            ]
            picked = jnp.concatenate([window[at, :] for at in place], axis=0)
            products.append(jnp.dot(ham_refs[p][b], picked, preferred_element_type=F32))
            places.append(place)
        for place, product in zip(places, products):
            for j, at in enumerate(place):
                total[at, :] += product[j * rows : (j + 1) * rows]
        return carry

    lax.fori_loop(0, nbatch, step, 0, unroll=2)
    out_before[...] = total[:region].astype(BF16)
    out_own[...] = total[region : 2 * region]
    out_after[...] = total[2 * region :].astype(BF16)


def apply_window(blocks, hams, before, own, after):
    pieces, per_batch = len(hams), blocks[0].shape[1]
    nbatch, columns = hams[0].shape[:2]
    region, width = own.shape
    return pl.pallas_call(
        functools.partial(apply_kernel, pieces, per_batch, columns // per_batch),
        out_shape=[
            jax.ShapeDtypeStruct((region, width), BF16),
            jax.ShapeDtypeStruct((region, width), F32),
            jax.ShapeDtypeStruct((region, width), BF16),
        ],
        in_specs=[SMEM] * pieces + [VMEM] * (pieces + 3),
        out_specs=[VMEM] * 3,
        scratch_shapes=[
            pltpu.VMEM((3 * region, width), BF16),
            pltpu.VMEM((3 * region, width), F32),
        ],
        compiler_params=params(),
        cost_estimate=pl.CostEstimate(
            flops=2 * pieces * nbatch * columns * columns * width,
            bytes_accessed=pieces * nbatch * columns * columns * 2 + 14 * region * width,
            transcendentals=0,
        ),
    )(*blocks, *hams, before, own, after)


def overlap_kernel(pieces, per_batch, rows, *refs):
    block_refs = refs[:pieces]
    occ_refs = refs[pieces : pieces + 6]
    resp_refs = refs[pieces + 6 : pieces + 12]
    out_refs = refs[pieces + 12 : 2 * pieces + 12]
    occ, resp = refs[2 * pieces + 12 :]
    region, width = occ_refs[0].shape
    for target, sources in ((occ, occ_refs), (resp, resp_refs)):
        for i, source in enumerate(sources):
            side, part = i // 2, i % 2
            target[side * region : (side + 1) * region, part * width : (part + 1) * width] = (
                source[...]
            )
    nbatch = out_refs[0].shape[0]

    def step(b, carry):
        for p in range(pieces):
            place = [
                pl.ds(pl.multiple_of(block_refs[p][b, j] * rows, rows), rows)
                for j in range(per_batch)
            ]
            left = jnp.concatenate([resp[at, :] for at in place], axis=0)
            right = jnp.concatenate([occ[at, :] for at in place], axis=0)
            product = lax.dot_general(left, right, NT, preferred_element_type=F32)
            out_refs[p][b] = product.astype(out_refs[p].dtype)
        return carry

    lax.fori_loop(0, nbatch, step, 0, unroll=2)


def overlaps(blocks, columns, occ_parts, resp_parts, types):
    pieces = len(blocks)
    nbatch, per_batch = blocks[0].shape
    region, width = occ_parts[0].shape
    return pl.pallas_call(
        functools.partial(overlap_kernel, pieces, per_batch, columns // per_batch),
        out_shape=[jax.ShapeDtypeStruct((nbatch, columns, columns), kind) for kind in types],
        in_specs=[SMEM] * pieces + [VMEM] * 12,
        out_specs=[VMEM] * pieces,
        scratch_shapes=[pltpu.VMEM((3 * region, 2 * width), BF16)] * 2,
        compiler_params=params(),
        cost_estimate=pl.CostEstimate(
            flops=4 * pieces * nbatch * columns * columns * width,
            bytes_accessed=24 * region * width + pieces * nbatch * columns * columns * 3,
            transcendentals=0,
        ),
    )(*blocks, *occ_parts, *resp_parts)


def density_kernel(basis_ref, first_ref, second_ref, scale_ref, out_ref):
    def step(b, carry):
        values = basis_ref[b]
        overlap = first_ref[b] + second_ref[b].astype(F32)
        product = split_dot(overlap, values, NT)
        density = jnp.sum(product * values.astype(F32).T, axis=0, keepdims=True)
        out_ref[b] = scale_ref[b] * density
        return carry

    lax.fori_loop(0, basis_ref.shape[0], step, 0, unroll=4)


def density(basis_values, first, second, scale):
    nbatch, points, columns = basis_values.shape
    out = pl.pallas_call(
        density_kernel,
        out_shape=jax.ShapeDtypeStruct((nbatch, 1, points), F32),
        in_specs=[VMEM] * 4,
        out_specs=VMEM,
        compiler_params=params(),
        cost_estimate=pl.CostEstimate(
            flops=4 * nbatch * points * columns * columns,
            bytes_accessed=basis_values.size * 2 + nbatch * columns * columns * 6,
            transcendentals=0,
        ),
    )(basis_values, first, second, scale.reshape(nbatch, 1, points))
    return out.reshape(nbatch, points)


def flip(array, axis, mask):
    return lax.ppermute(array, axis, [(i, i ^ mask) for i in range(lax.axis_size(axis))])


def neighbours(array):
    size = lax.axis_size("grid")
    before = lax.ppermute(array, "grid", [(i, (i + 1) % size) for i in range(size)])
    after = lax.ppermute(array, "grid", [((i + 1) % size, i) for i in range(size)])
    return before, after


def column_part(array, index, width):
    return lax.dynamic_slice_in_dim(array, index * width, width, 1)


def rotate(part, occ_energy, virt_energy):
    size = lax.axis_size("grid")
    if size != 8:
        total = lax.psum(part, "grid")
        return (total / (occ_energy[:, None] - virt_energy[None, :])).astype(BF16)
    index = lax.axis_index("grid")
    half = part.shape[0] // 2
    side, place = index % 2, index // 2
    keep = lax.dynamic_slice_in_dim(part, side * half, half, 0)
    send = lax.dynamic_slice_in_dim(part, (1 - side) * half, half, 0).astype(BF16)
    total = keep + flip(send, "grid", 1).astype(F32)
    inward = [(0, 2), (1, 3), (6, 4), (7, 5)]
    across = [(2, 4), (3, 5), (4, 2), (5, 3)]
    outward = [(j, i) for i, j in inward]
    total = total + lax.ppermute(total.astype(BF16), "grid", inward).astype(F32)
    total = total + lax.ppermute(total.astype(BF16), "grid", across).astype(F32)
    energy = lax.dynamic_slice_in_dim(occ_energy, side * half, half, 0)
    own = (total / (energy[:, None] - virt_energy[None, :])).astype(BF16)
    outer = (place == 0) | (place == 3)
    own = jnp.where(outer, lax.ppermute(own, "grid", outward), own)
    other = flip(own, "grid", 1)
    low, high = jnp.where(side == 0, own, other), jnp.where(side == 0, other, own)
    return jnp.concatenate([low, high], axis=0)


def per_device(
    basis_values,
    blocks,
    counts,
    weighted_potential,
    xc_kernel,
    occ_coef,
    virt_coef,
    occ_energy,
    virt_energy,
):
    nbatch, points, columns = basis_values.shape
    region, occ_count = occ_coef.shape
    width = occ_count // lax.axis_size("tile")
    tile = lax.axis_index("tile")
    chip, core = tile // 2, tile % 2
    quarter = 2 * core + chip
    live_mask = lax.broadcasted_iota(jnp.int32, (nbatch, points), 1) < counts[:, None]

    occ_own = column_part(occ_coef, quarter, width)
    occ_before, occ_after = neighbours(occ_own)

    blocks_near = flip(blocks, "tile", 1)
    blocks_far = flip(blocks, "tile", 2)
    blocks_last = flip(blocks_far, "tile", 1)
    ham = integrate(basis_values, jnp.where(live_mask, weighted_potential, 0.0))
    ham_far = flip(ham, "tile", 2)
    ham_near = flip(ham, "tile", 1)
    ham_last = flip(ham_far, "tile", 1)
    virt_near = flip(virt_coef, "tile", 1)
    energy_near = flip(virt_energy, "tile", 1)

    to_before, own_sum, to_after = apply_window(
        [blocks, blocks_near, blocks_far, blocks_last],
        [ham, ham_near, ham_far, ham_last],
        occ_before,
        occ_own,
        occ_after,
    )
    size = lax.axis_size("grid")
    from_before = lax.ppermute(to_after, "grid", [(i, (i + 1) % size) for i in range(size)])
    from_after = lax.ppermute(to_before, "grid", [((i + 1) % size, i) for i in range(size)])
    ham_own = (own_sum + from_before.astype(F32) + from_after.astype(F32)).astype(BF16)
    ham_half = jnp.concatenate([ham_own, flip(ham_own, "tile", 2)], axis=1)

    occ_far = column_part(occ_coef, quarter ^ 1, width)
    late_before, late_after, _ = lax.optimization_barrier((occ_before, occ_after, ham_half))
    before_far, after_far = flip(late_before, "tile", 2), flip(late_after, "tile", 2)

    energy_half = jnp.concatenate(
        [
            lax.dynamic_slice_in_dim(occ_energy, quarter * width, width, 0),
            lax.dynamic_slice_in_dim(occ_energy, (quarter ^ 1) * width, width, 0),
        ]
    )
    tile_virt = virt_coef.shape[1]
    cut = -(-tile_virt // (2 * LANES)) * LANES
    coef_part = None
    for virt, energy in ((virt_coef, virt_energy), (virt_near, energy_near)):
        for start, stop in ((0, cut), (cut, tile_virt)):
            columns_slice = virt[:, start:stop]
            part = lax.dot_general(
                ham_half, columns_slice, (((0,), (0,)), ((), ())), preferred_element_type=F32
            )
            rotation = rotate(part, energy_half, energy[start:stop])
            term = lax.dot_general(columns_slice, rotation, NT, preferred_element_type=F32)
            coef_part = term if coef_part is None else coef_part + term
    coef_far = flip(coef_part[:, width:].astype(BF16), "tile", 2)
    resp_own = (coef_part[:, :width] + coef_far.astype(F32)).astype(BF16)

    resp_before, resp_after = neighbours(resp_own)
    resp_far = flip(resp_own, "tile", 2)
    resp_before_far, resp_after_far = flip(resp_before, "tile", 2), flip(resp_after, "tile", 2)
    first = chip == 0
    half = jnp.concatenate(
        [jnp.where(first, resp_own, resp_far), jnp.where(first, resp_far, resp_own)], axis=1
    )
    half_near = flip(half, "tile", 1)
    first = core == 0
    response_coef = jnp.concatenate(
        [jnp.where(first, half, half_near), jnp.where(first, half_near, half)], axis=1
    )

    overlap_own, overlap_near = overlaps(
        [blocks, blocks_near],
        columns,
        [occ_before, before_far, occ_own, occ_far, occ_after, after_far],
        [resp_before, resp_before_far, resp_own, resp_far, resp_after, resp_after_far],
        [F32, BF16],
    )
    scale = jnp.where(live_mask, 4.0 * xc_kernel, 0.0)
    response_potential = density(basis_values, overlap_own, flip(overlap_near, "tile", 1), scale)
    return (response_coef, response_potential)


def solution(mesh):
    in_specs = (
        P(("grid", "tile"), None, None),
        P(("grid", "tile"), None),
        P(("grid", "tile")),
        P(("grid", "tile"), None),
        P(("grid", "tile"), None),
        P("grid", None),
        P("grid", "tile"),
        P(),
        P("tile"),
    )
    out_specs = (P("grid", None), P(("grid", "tile"), None))
    return jax.shard_map(
        per_device, mesh=mesh, in_specs=in_specs, out_specs=out_specs, check_vma=False
    )
```

```python
import functools

import jax
import jax.numpy as jnp
from jax import lax
from jax.experimental import pallas as pl
from jax.experimental.pallas import tpu as pltpu
from jax.sharding import PartitionSpec as P

VMEM = pl.BlockSpec(memory_space=pltpu.VMEM)
SMEM = pl.BlockSpec(memory_space=pltpu.SMEM)
LIMIT = 40 * 1024 * 1024
F32 = jnp.float32
BF16 = jnp.bfloat16
NT = (((1,), (1,)), ((), ()))


def params():
    return pltpu.CompilerParams(vmem_limit_bytes=LIMIT)


def split_dot(full, other, dims):
    high = full.astype(BF16)
    low = (full - high.astype(F32)).astype(BF16)
    return lax.dot_general(high, other, dims, preferred_element_type=F32) + lax.dot_general(
        low, other, dims, preferred_element_type=F32
    )


def triangle(size):
    rows = lax.broadcasted_iota(jnp.int32, (size, size), 0)
    return rows, lax.broadcasted_iota(jnp.int32, (size, size), 1)


def integrate_kernel(basis_ref, weights_ref, full_ref, packed_ref, diagonal):
    nbatch = basis_ref.shape[0]
    half = basis_ref.shape[2] // 2
    row, column = triangle(half)
    diagonal[...] = jnp.zeros_like(diagonal)

    def step(b, carry):
        values = basis_ref[b]
        weighted = values.astype(F32).T * weights_ref[b]
        ham = split_dot(weighted, values, (((1,), (0,)), ((), ())))
        full_ref[b] = ham.astype(BF16)
        last = ham[half:, half:]
        mixed = jnp.where(row >= column, ham[:half, :half], last)
        packed = jnp.concatenate([ham[:half, half:], mixed], axis=1)
        packed_ref[pl.ds(pl.multiple_of(b * half, half), half), :] = packed.astype(BF16)
        line = jnp.sum(jnp.where(row == column, last, 0.0), axis=0, keepdims=True)
        diagonal[pl.ds(b, 1), :] = jnp.concatenate([line, jnp.zeros_like(line)], axis=1)
        return carry

    lax.fori_loop(0, nbatch, step, 0, unroll=4)
    packed_ref[nbatch * half :, :] = diagonal[...].astype(BF16)


def padded_rows(nbatch):
    return -(-nbatch // 32) * 32


def integrate(basis_values, weights):
    nbatch, points, columns = basis_values.shape
    extra = padded_rows(nbatch)
    return pl.pallas_call(
        integrate_kernel,
        out_shape=[
            jax.ShapeDtypeStruct((nbatch, columns, columns), BF16),
            jax.ShapeDtypeStruct((nbatch * columns // 2 + extra, columns), BF16),
        ],
        in_specs=[VMEM, VMEM],
        out_specs=[VMEM, VMEM],
        scratch_shapes=[pltpu.VMEM((extra, columns), F32)],
        compiler_params=params(),
        cost_estimate=pl.CostEstimate(
            flops=4 * nbatch * points * columns * columns,
            bytes_accessed=basis_values.size * 2 + nbatch * columns * columns * 3,
            transcendentals=0,
        ),
    )(basis_values, weights.reshape(nbatch, 1, points))


def unpack_kernel(packed_ref, full_ref, diagonal):
    nbatch = full_ref.shape[0]
    half = full_ref.shape[1] // 2
    row, column = triangle(half)
    diagonal[...] = packed_ref[nbatch * half :, :].astype(F32)

    def step(b, carry):
        packed = packed_ref[pl.ds(pl.multiple_of(b * half, half), half), :].astype(F32)
        turned = packed.T
        mixed, mixed_turned = packed[:, half:], turned[half:]
        first = jnp.where(row >= column, mixed, mixed_turned)
        last = jnp.where(row < column, mixed, mixed_turned)
        last = jnp.where(row == column, diagonal[pl.ds(b, 1), :][:, :half], last)
        upper = jnp.concatenate([first, packed[:, :half]], axis=1)
        lower = jnp.concatenate([turned[:half], last], axis=1)
        full_ref[b] = jnp.concatenate([upper, lower], axis=0).astype(BF16)
        return carry

    lax.fori_loop(0, nbatch, step, 0, unroll=4)


def unpack(packed, nbatch, columns):
    return pl.pallas_call(
        unpack_kernel,
        out_shape=jax.ShapeDtypeStruct((nbatch, columns, columns), BF16),
        in_specs=[VMEM],
        out_specs=VMEM,
        scratch_shapes=[pltpu.VMEM((padded_rows(nbatch), columns), F32)],
        compiler_params=params(),
        cost_estimate=pl.CostEstimate(
            flops=nbatch * columns * columns * 4,
            bytes_accessed=nbatch * columns * columns * 3,
            transcendentals=0,
        ),
    )(packed)


def apply_kernel(pieces, per_batch, rows, *refs):
    block_refs, ham_refs = refs[:pieces], refs[pieces : 2 * pieces]
    before_ref, own_ref, after_ref = refs[2 * pieces : 2 * pieces + 3]
    out_before, out_own, out_after = refs[2 * pieces + 3 : 2 * pieces + 6]
    window, total = refs[2 * pieces + 6 :]
    region = own_ref.shape[0]
    window[:region] = before_ref[...]
    window[region : 2 * region] = own_ref[...]
    window[2 * region :] = after_ref[...]
    total[...] = jnp.zeros_like(total)
    nbatch = ham_refs[0].shape[0]

    def step(b, carry):
        places, products = [], []
        for p in range(pieces):
            place = [
                pl.ds(pl.multiple_of(block_refs[p][b, j] * rows, rows), rows)
                for j in range(per_batch)
            ]
            picked = jnp.concatenate([window[at, :] for at in place], axis=0)
            products.append(jnp.dot(ham_refs[p][b], picked, preferred_element_type=F32))
            places.append(place)
        for place, product in zip(places, products):
            for j, at in enumerate(place):
                total[at, :] += product[j * rows : (j + 1) * rows]
        return carry

    lax.fori_loop(0, nbatch, step, 0, unroll=2)
    out_before[...] = total[:region].astype(BF16)
    out_own[...] = total[region : 2 * region]
    out_after[...] = total[2 * region :].astype(BF16)


def apply_window(blocks, hams, before, own, after):
    pieces, per_batch = len(hams), blocks[0].shape[1]
    nbatch, columns = hams[0].shape[:2]
    region, width = own.shape
    return pl.pallas_call(
        functools.partial(apply_kernel, pieces, per_batch, columns // per_batch),
        out_shape=[
            jax.ShapeDtypeStruct((region, width), BF16),
            jax.ShapeDtypeStruct((region, width), F32),
            jax.ShapeDtypeStruct((region, width), BF16),
        ],
        in_specs=[SMEM] * pieces + [VMEM] * (pieces + 3),
        out_specs=[VMEM] * 3,
        scratch_shapes=[
            pltpu.VMEM((3 * region, width), BF16),
            pltpu.VMEM((3 * region, width), F32),
        ],
        compiler_params=params(),
        cost_estimate=pl.CostEstimate(
            flops=2 * pieces * nbatch * columns * columns * width,
            bytes_accessed=pieces * nbatch * columns * columns * 2 + 14 * region * width,
            transcendentals=0,
        ),
    )(*blocks, *hams, before, own, after)


def overlap_kernel(pieces, per_batch, rows, *refs):
    block_refs = refs[:pieces]
    occ_refs = refs[pieces : pieces + 6]
    resp_refs = refs[pieces + 6 : pieces + 12]
    out_refs = refs[pieces + 12 : 2 * pieces + 12]
    occ, resp = refs[2 * pieces + 12 :]
    region, width = occ_refs[0].shape
    for target, sources in ((occ, occ_refs), (resp, resp_refs)):
        for i, source in enumerate(sources):
            side, part = i // 2, i % 2
            target[side * region : (side + 1) * region, part * width : (part + 1) * width] = (
                source[...]
            )
    nbatch = out_refs[0].shape[0]

    def step(b, carry):
        for p in range(pieces):
            place = [
                pl.ds(pl.multiple_of(block_refs[p][b, j] * rows, rows), rows)
                for j in range(per_batch)
            ]
            left = jnp.concatenate([resp[at, :] for at in place], axis=0)
            right = jnp.concatenate([occ[at, :] for at in place], axis=0)
            product = lax.dot_general(left, right, NT, preferred_element_type=F32)
            out_refs[p][b] = product.astype(out_refs[p].dtype)
        return carry

    lax.fori_loop(0, nbatch, step, 0, unroll=2)


def overlaps(blocks, columns, occ_parts, resp_parts, types):
    pieces = len(blocks)
    nbatch, per_batch = blocks[0].shape
    region, width = occ_parts[0].shape
    return pl.pallas_call(
        functools.partial(overlap_kernel, pieces, per_batch, columns // per_batch),
        out_shape=[jax.ShapeDtypeStruct((nbatch, columns, columns), kind) for kind in types],
        in_specs=[SMEM] * pieces + [VMEM] * 12,
        out_specs=[VMEM] * pieces,
        scratch_shapes=[pltpu.VMEM((3 * region, 2 * width), BF16)] * 2,
        compiler_params=params(),
        cost_estimate=pl.CostEstimate(
            flops=4 * pieces * nbatch * columns * columns * width,
            bytes_accessed=24 * region * width + pieces * nbatch * columns * columns * 3,
            transcendentals=0,
        ),
    )(*blocks, *occ_parts, *resp_parts)


def density_kernel(basis_ref, first_ref, second_ref, scale_ref, out_ref):
    def step(b, carry):
        values = basis_ref[b]
        overlap = first_ref[b] + second_ref[b].astype(F32)
        product = split_dot(overlap, values, NT)
        density = jnp.sum(product * values.astype(F32).T, axis=0, keepdims=True)
        out_ref[b] = scale_ref[b] * density
        return carry

    lax.fori_loop(0, basis_ref.shape[0], step, 0, unroll=4)


def density(basis_values, first, second, scale):
    nbatch, points, columns = basis_values.shape
    out = pl.pallas_call(
        density_kernel,
        out_shape=jax.ShapeDtypeStruct((nbatch, 1, points), F32),
        in_specs=[VMEM] * 4,
        out_specs=VMEM,
        compiler_params=params(),
        cost_estimate=pl.CostEstimate(
            flops=4 * nbatch * points * columns * columns,
            bytes_accessed=basis_values.size * 2 + nbatch * columns * columns * 6,
            transcendentals=0,
        ),
    )(basis_values, first, second, scale.reshape(nbatch, 1, points))
    return out.reshape(nbatch, points)


def flip(array, axis, mask):
    return lax.ppermute(array, axis, [(i, i ^ mask) for i in range(lax.axis_size(axis))])


def neighbours(array):
    size = lax.axis_size("grid")
    before = lax.ppermute(array, "grid", [(i, (i + 1) % size) for i in range(size)])
    after = lax.ppermute(array, "grid", [((i + 1) % size, i) for i in range(size)])
    return before, after


def column_part(array, index, width):
    return lax.dynamic_slice_in_dim(array, index * width, width, 1)


def rotate(part, occ_energy, virt_energy):
    size = lax.axis_size("grid")
    if size != 8:
        total = lax.psum(part, "grid")
        return (total / (occ_energy[:, None] - virt_energy[None, :])).astype(BF16)
    index = lax.axis_index("grid")
    half = part.shape[0] // 2
    side, place = index % 2, index // 2
    keep = lax.dynamic_slice_in_dim(part, side * half, half, 0)
    send = lax.dynamic_slice_in_dim(part, (1 - side) * half, half, 0).astype(BF16)
    total = keep + flip(send, "grid", 1).astype(F32)
    inward = [(0, 2), (1, 3), (6, 4), (7, 5)]
    across = [(2, 4), (3, 5), (4, 2), (5, 3)]
    outward = [(j, i) for i, j in inward]
    total = total + lax.ppermute(total.astype(BF16), "grid", inward).astype(F32)
    total = total + lax.ppermute(total.astype(BF16), "grid", across).astype(F32)
    energy = lax.dynamic_slice_in_dim(occ_energy, side * half, half, 0)
    own = (total / (energy[:, None] - virt_energy[None, :])).astype(BF16)
    outer = (place == 0) | (place == 3)
    own = jnp.where(outer, lax.ppermute(own, "grid", outward), own)
    other = flip(own, "grid", 1)
    low, high = jnp.where(side == 0, own, other), jnp.where(side == 0, other, own)
    return jnp.concatenate([low, high], axis=0)


def per_device(
    basis_values,
    blocks,
    counts,
    weighted_potential,
    xc_kernel,
    occ_coef,
    virt_coef,
    occ_energy,
    virt_energy,
):
    nbatch, points, columns = basis_values.shape
    region, occ_count = occ_coef.shape
    width = occ_count // lax.axis_size("tile")
    tile = lax.axis_index("tile")
    chip, core = tile // 2, tile % 2
    quarter = 2 * core + chip
    live_mask = lax.broadcasted_iota(jnp.int32, (nbatch, points), 1) < counts[:, None]

    occ_own = column_part(occ_coef, quarter, width)
    occ_before, occ_after = neighbours(occ_own)

    blocks_near = flip(blocks, "tile", 1)
    blocks_far = flip(blocks, "tile", 2)
    blocks_last = flip(blocks_far, "tile", 1)
    weights = jnp.where(live_mask, weighted_potential, 0.0)
    ham, ham_packed = integrate(basis_values, weights)
    ham_near = flip(ham, "tile", 1)
    ham_far = unpack(flip(ham_packed, "tile", 2), nbatch, columns)
    ham_far, occ_before, occ_after = lax.optimization_barrier((ham_far, occ_before, occ_after))
    ham_last = flip(ham_far, "tile", 1)
    virt_near = flip(virt_coef, "tile", 1)
    energy_near = flip(virt_energy, "tile", 1)

    to_before, own_sum, to_after = apply_window(
        [blocks, blocks_near, blocks_far, blocks_last],
        [ham, ham_near, ham_far, ham_last],
        occ_before,
        occ_own,
        occ_after,
    )
    size = lax.axis_size("grid")
    from_before = lax.ppermute(to_after, "grid", [(i, (i + 1) % size) for i in range(size)])
    from_after = lax.ppermute(to_before, "grid", [((i + 1) % size, i) for i in range(size)])
    ham_own = (own_sum + from_before.astype(F32) + from_after.astype(F32)).astype(BF16)
    ham_sums = [ham_own, flip(ham_own, "tile", 2)]

    occ_far = column_part(occ_coef, quarter ^ 1, width)
    late_before, late_after, _ = lax.optimization_barrier((occ_before, occ_after, ham_sums[1]))
    before_far, after_far = flip(late_before, "tile", 2), flip(late_after, "tile", 2)

    levels = [
        lax.dynamic_slice_in_dim(occ_energy, place * width, width, 0)
        for place in (quarter, quarter ^ 1)
    ]
    virtuals = [(virt_coef, virt_energy), (virt_near, energy_near)]
    coefs = [None, None]
    for part, share in ((0, 0), (1, 0), (1, 1), (0, 1)):
        virt, energy = virtuals[share]
        virt_ham = lax.dot_general(
            ham_sums[part], virt, (((0,), (0,)), ((), ())), preferred_element_type=F32
        )
        rotation = rotate(virt_ham, levels[part], energy)
        term = lax.dot_general(virt, rotation, NT, preferred_element_type=F32)
        coefs[part] = term if coefs[part] is None else coefs[part] + term
    coef_far = flip(coefs[1].astype(BF16), "tile", 2)
    resp_own = (coefs[0] + coef_far.astype(F32)).astype(BF16)

    resp_before, resp_after = neighbours(resp_own)
    resp_far = flip(resp_own, "tile", 2)
    resp_before_far, resp_after_far = flip(resp_before, "tile", 2), flip(resp_after, "tile", 2)
    first = chip == 0
    half = jnp.concatenate(
        [jnp.where(first, resp_own, resp_far), jnp.where(first, resp_far, resp_own)], axis=1
    )
    half_near = flip(half, "tile", 1)
    first = core == 0
    response_coef = jnp.concatenate(
        [jnp.where(first, half, half_near), jnp.where(first, half_near, half)], axis=1
    )

    overlap_own, overlap_near = overlaps(
        [blocks, blocks_near],
        columns,
        [occ_before, before_far, occ_own, occ_far, occ_after, after_far],
        [resp_before, resp_before_far, resp_own, resp_far, resp_after, resp_after_far],
        [F32, BF16],
    )
    scale = jnp.where(live_mask, 4.0 * xc_kernel, 0.0)
    response_potential = density(basis_values, overlap_own, flip(overlap_near, "tile", 1), scale)
    return (response_coef, response_potential)


def solution(mesh):
    in_specs = (
        P(("grid", "tile"), None, None),
        P(("grid", "tile"), None),
        P(("grid", "tile")),
        P(("grid", "tile"), None),
        P(("grid", "tile"), None),
        P("grid", None),
        P("grid", "tile"),
        P(),
        P("tile"),
    )
    out_specs = (P("grid", None), P(("grid", "tile"), None))
    return jax.shard_map(
        per_device, mesh=mesh, in_specs=in_specs, out_specs=out_specs, check_vma=False
    )
```

```python
import functools

import jax
import jax.numpy as jnp
from jax import lax
from jax.experimental import pallas as pl
from jax.experimental.pallas import tpu as pltpu
from jax.sharding import PartitionSpec as P

VMEM = pl.BlockSpec(memory_space=pltpu.VMEM)
SMEM = pl.BlockSpec(memory_space=pltpu.SMEM)
LIMIT = 40 * 1024 * 1024
F32 = jnp.float32
BF16 = jnp.bfloat16
NT = (((1,), (1,)), ((), ()))


def params():
    return pltpu.CompilerParams(vmem_limit_bytes=LIMIT)


def split_dot(full, other, dims):
    high = full.astype(BF16)
    low = (full - high.astype(F32)).astype(BF16)
    return lax.dot_general(high, other, dims, preferred_element_type=F32) + lax.dot_general(
        low, other, dims, preferred_element_type=F32
    )


def triangle(size):
    rows = lax.broadcasted_iota(jnp.int32, (size, size), 0)
    return rows, lax.broadcasted_iota(jnp.int32, (size, size), 1)


def integrate_kernel(start, basis_ref, weights_ref, full_ref, packed_ref, diagonal):
    nbatch = full_ref.shape[0]
    half = full_ref.shape[2] // 2
    row, column = triangle(half)
    diagonal[...] = jnp.zeros_like(diagonal)

    def step(b, carry):
        values = basis_ref[start + b]
        weighted = values.astype(F32).T * weights_ref[start + b]
        ham = split_dot(weighted, values, (((1,), (0,)), ((), ())))
        full_ref[b] = ham.astype(BF16)
        last = ham[half:, half:]
        mixed = jnp.where(row >= column, ham[:half, :half], last)
        packed = jnp.concatenate([ham[:half, half:], mixed], axis=1)
        packed_ref[pl.ds(pl.multiple_of(b * half, half), half), :] = packed.astype(BF16)
        line = jnp.sum(jnp.where(row == column, last, 0.0), axis=0, keepdims=True)
        diagonal[pl.ds(b, 1), :] = jnp.concatenate([line, jnp.zeros_like(line)], axis=1)
        return carry

    lax.fori_loop(0, nbatch, step, 0, unroll=4)
    packed_ref[nbatch * half :, :] = diagonal[...].astype(BF16)


def padded_rows(nbatch):
    return -(-nbatch // 32) * 32


def integrate(basis_values, weights, start, stop):
    _, points, columns = basis_values.shape
    nbatch = stop - start
    extra = padded_rows(nbatch)
    return pl.pallas_call(
        functools.partial(integrate_kernel, start),
        out_shape=[
            jax.ShapeDtypeStruct((nbatch, columns, columns), BF16),
            jax.ShapeDtypeStruct((nbatch * columns // 2 + extra, columns), BF16),
        ],
        in_specs=[VMEM, VMEM],
        out_specs=[VMEM, VMEM],
        scratch_shapes=[pltpu.VMEM((extra, columns), F32)],
        compiler_params=params(),
        cost_estimate=pl.CostEstimate(
            flops=4 * nbatch * points * columns * columns,
            bytes_accessed=nbatch * columns * (points * 2 + columns * 3),
            transcendentals=0,
        ),
    )(basis_values, weights.reshape(-1, 1, points))


def unpack_kernel(packed_ref, full_ref, diagonal):
    nbatch = full_ref.shape[0]
    half = full_ref.shape[1] // 2
    row, column = triangle(half)
    diagonal[...] = packed_ref[nbatch * half :, :].astype(F32)

    def step(b, carry):
        packed = packed_ref[pl.ds(pl.multiple_of(b * half, half), half), :].astype(F32)
        turned = packed.T
        mixed, mixed_turned = packed[:, half:], turned[half:]
        first = jnp.where(row >= column, mixed, mixed_turned)
        last = jnp.where(row < column, mixed, mixed_turned)
        last = jnp.where(row == column, diagonal[pl.ds(b, 1), :][:, :half], last)
        upper = jnp.concatenate([first, packed[:, :half]], axis=1)
        lower = jnp.concatenate([turned[:half], last], axis=1)
        full_ref[b] = jnp.concatenate([upper, lower], axis=0).astype(BF16)
        return carry

    lax.fori_loop(0, nbatch, step, 0, unroll=4)


def unpack(packed, nbatch, columns):
    return pl.pallas_call(
        unpack_kernel,
        out_shape=jax.ShapeDtypeStruct((nbatch, columns, columns), BF16),
        in_specs=[VMEM],
        out_specs=VMEM,
        scratch_shapes=[pltpu.VMEM((padded_rows(nbatch), columns), F32)],
        compiler_params=params(),
        cost_estimate=pl.CostEstimate(
            flops=nbatch * columns * columns * 4,
            bytes_accessed=nbatch * columns * columns * 3,
            transcendentals=0,
        ),
    )(packed)


def apply_kernel(pieces, per_batch, rows, *refs):
    block_refs, ham_refs = refs[:pieces], refs[pieces : 2 * pieces]
    before_ref, own_ref, after_ref = refs[2 * pieces : 2 * pieces + 3]
    out_before, out_own, out_after = refs[2 * pieces + 3 : 2 * pieces + 6]
    window, total = refs[2 * pieces + 6 :]
    region = own_ref.shape[0]
    window[:region] = before_ref[...]
    window[region : 2 * region] = own_ref[...]
    window[2 * region :] = after_ref[...]
    total[...] = jnp.zeros_like(total)
    nbatch = ham_refs[0].shape[0]

    def step(b, carry):
        places, products = [], []
        for p in range(pieces):
            place = [
                pl.ds(pl.multiple_of(block_refs[p][b, j] * rows, rows), rows)
                for j in range(per_batch)
            ]
            picked = jnp.concatenate([window[at, :] for at in place], axis=0)
            products.append(jnp.dot(ham_refs[p][b], picked, preferred_element_type=F32))
            places.append(place)
        for place, product in zip(places, products):
            for j, at in enumerate(place):
                total[at, :] += product[j * rows : (j + 1) * rows]
        return carry

    lax.fori_loop(0, nbatch, step, 0, unroll=2)
    out_before[...] = total[:region].astype(BF16)
    out_own[...] = total[region : 2 * region]
    out_after[...] = total[2 * region :].astype(BF16)


def apply_window(blocks, hams, before, own, after):
    pieces, per_batch = len(hams), blocks[0].shape[1]
    nbatch, columns = hams[0].shape[:2]
    region, width = own.shape
    return pl.pallas_call(
        functools.partial(apply_kernel, pieces, per_batch, columns // per_batch),
        out_shape=[
            jax.ShapeDtypeStruct((region, width), BF16),
            jax.ShapeDtypeStruct((region, width), F32),
            jax.ShapeDtypeStruct((region, width), BF16),
        ],
        in_specs=[SMEM] * pieces + [VMEM] * (pieces + 3),
        out_specs=[VMEM] * 3,
        scratch_shapes=[
            pltpu.VMEM((3 * region, width), BF16),
            pltpu.VMEM((3 * region, width), F32),
        ],
        compiler_params=params(),
        cost_estimate=pl.CostEstimate(
            flops=2 * pieces * nbatch * columns * columns * width,
            bytes_accessed=pieces * nbatch * columns * columns * 2 + 14 * region * width,
            transcendentals=0,
        ),
    )(*blocks, *hams, before, own, after)


def overlap_kernel(pieces, per_batch, rows, *refs):
    block_refs = refs[:pieces]
    occ_refs = refs[pieces : pieces + 6]
    resp_refs = refs[pieces + 6 : pieces + 12]
    out_refs = refs[pieces + 12 : 2 * pieces + 12]
    occ, resp = refs[2 * pieces + 12 :]
    region, width = occ_refs[0].shape
    for target, sources in ((occ, occ_refs), (resp, resp_refs)):
        for i, source in enumerate(sources):
            side, part = i // 2, i % 2
            target[side * region : (side + 1) * region, part * width : (part + 1) * width] = (
                source[...]
            )
    nbatch = out_refs[0].shape[0]

    def step(b, carry):
        for p in range(pieces):
            place = [
                pl.ds(pl.multiple_of(block_refs[p][b, j] * rows, rows), rows)
                for j in range(per_batch)
            ]
            left = jnp.concatenate([resp[at, :] for at in place], axis=0)
            right = jnp.concatenate([occ[at, :] for at in place], axis=0)
            product = lax.dot_general(left, right, NT, preferred_element_type=F32)
            out_refs[p][b] = product.astype(out_refs[p].dtype)
        return carry

    lax.fori_loop(0, nbatch, step, 0, unroll=2)


def overlaps(blocks, columns, occ_parts, resp_parts, types):
    pieces = len(blocks)
    nbatch, per_batch = blocks[0].shape
    region, width = occ_parts[0].shape
    return pl.pallas_call(
        functools.partial(overlap_kernel, pieces, per_batch, columns // per_batch),
        out_shape=[jax.ShapeDtypeStruct((nbatch, columns, columns), kind) for kind in types],
        in_specs=[SMEM] * pieces + [VMEM] * 12,
        out_specs=[VMEM] * pieces,
        scratch_shapes=[pltpu.VMEM((3 * region, 2 * width), BF16)] * 2,
        compiler_params=params(),
        cost_estimate=pl.CostEstimate(
            flops=4 * pieces * nbatch * columns * columns * width,
            bytes_accessed=24 * region * width + pieces * nbatch * columns * columns * 3,
            transcendentals=0,
        ),
    )(*blocks, *occ_parts, *resp_parts)


def density_kernel(basis_ref, first_ref, second_ref, scale_ref, out_ref):
    def step(b, carry):
        values = basis_ref[b]
        overlap = first_ref[b] + second_ref[b].astype(F32)
        product = split_dot(overlap, values, NT)
        density = jnp.sum(product * values.astype(F32).T, axis=0, keepdims=True)
        out_ref[b] = scale_ref[b] * density
        return carry

    lax.fori_loop(0, basis_ref.shape[0], step, 0, unroll=4)


def density(basis_values, first, second, scale):
    nbatch, points, columns = basis_values.shape
    out = pl.pallas_call(
        density_kernel,
        out_shape=jax.ShapeDtypeStruct((nbatch, 1, points), F32),
        in_specs=[VMEM] * 4,
        out_specs=VMEM,
        compiler_params=params(),
        cost_estimate=pl.CostEstimate(
            flops=4 * nbatch * points * columns * columns,
            bytes_accessed=basis_values.size * 2 + nbatch * columns * columns * 6,
            transcendentals=0,
        ),
    )(basis_values, first, second, scale.reshape(nbatch, 1, points))
    return out.reshape(nbatch, points)


def flip(array, axis, mask):
    return lax.ppermute(array, axis, [(i, i ^ mask) for i in range(lax.axis_size(axis))])


def neighbours(array):
    size = lax.axis_size("grid")
    before = lax.ppermute(array, "grid", [(i, (i + 1) % size) for i in range(size)])
    after = lax.ppermute(array, "grid", [((i + 1) % size, i) for i in range(size)])
    return before, after


def column_part(array, index, width):
    return lax.dynamic_slice_in_dim(array, index * width, width, 1)


def rotations(parts, levels, energies, ties, finish):
    count, size = len(parts), lax.axis_size("grid")
    if size != 8:
        for k, part in enumerate(parts):
            total = lax.psum(part, "grid")
            finish(k, (total / (levels[k][:, None] - energies[k][None, :])).astype(BF16))
        return
    index = lax.axis_index("grid")
    half = parts[0].shape[0] // 2
    side, place = index % 2, index // 2
    outer = (place == 0) | (place == 3)
    inward = [(0, 2), (1, 3), (6, 4), (7, 5)]
    outward = [(j, i) for i, j in inward]
    across = [(2, 4), (3, 5), (4, 2), (5, 3)]
    sums, turned, done = {}, {}, {}
    for slot in range(count + 4):
        moved = {}
        if slot < count:
            send = lax.dynamic_slice_in_dim(parts[slot], (1 - side) * half, half, 0)
            moved["first"] = flip(send.astype(BF16), "grid", 1)
        if 0 <= slot - 4:
            moved["last"] = flip(turned[slot - 4], "grid", 1)
        coming, going = slot - 1, slot - 3
        if 0 <= coming < count and 0 <= going < count:
            payload = jnp.where(outer, sums[coming].astype(BF16), turned[going])
            moved["ends"] = lax.ppermute(payload, "grid", inward + outward)
        elif 0 <= coming < count:
            moved["ends"] = lax.ppermute(sums[coming].astype(BF16), "grid", inward)
        elif 0 <= going < count:
            moved["ends"] = lax.ppermute(turned[going], "grid", outward)
        if 0 <= slot - 2 < count:
            moved["middle"] = lax.ppermute(sums[slot - 2].astype(BF16), "grid", across)
        moved, _ = lax.optimization_barrier((moved, ties.pop(slot, ())))
        if "first" in moved:
            keep = lax.dynamic_slice_in_dim(parts[slot], side * half, half, 0)
            sums[slot] = keep + moved["first"].astype(F32)
        if 0 <= going < count:
            turned[going] = jnp.where(outer, moved["ends"], turned[going])
        if 0 <= coming < count:
            sums[coming] = sums[coming] + moved["ends"].astype(F32)
        if "middle" in moved:
            k = slot - 2
            level = lax.dynamic_slice_in_dim(levels[k], side * half, half, 0)
            total = sums[k] + moved["middle"].astype(F32)
            turned[k] = (total / (level[:, None] - energies[k][None, :])).astype(BF16)
        if "last" in moved:
            own, other = turned[slot - 4], moved["last"]
            low, high = jnp.where(side == 0, own, other), jnp.where(side == 0, other, own)
            tie = finish(slot - 4, jnp.concatenate([low, high], axis=0))
            if slot + 2 < count + 4:
                ties.setdefault(slot + 1, []).append(tie)


def per_device(
    basis_values,
    blocks,
    counts,
    weighted_potential,
    xc_kernel,
    occ_coef,
    virt_coef,
    occ_energy,
    virt_energy,
):
    nbatch, points, columns = basis_values.shape
    region, occ_count = occ_coef.shape
    width = occ_count // lax.axis_size("tile")
    tile = lax.axis_index("tile")
    chip, core = tile // 2, tile % 2
    quarter = 2 * core + chip
    live_mask = lax.broadcasted_iota(jnp.int32, (nbatch, points), 1) < counts[:, None]

    occ_own = column_part(occ_coef, quarter, width)
    occ_before, occ_after = neighbours(occ_own)

    weights = jnp.where(live_mask, weighted_potential, 0.0)
    weights, occ_own = lax.optimization_barrier((weights, occ_own))
    middle = -(-nbatch // 2)
    lists = [blocks, flip(blocks, "tile", 1), flip(blocks, "tile", 2)]
    lists.append(flip(lists[2], "tile", 1))
    fulls, arrived = [], []
    for start, stop in ((0, middle), (middle, nbatch)):
        full, packed = integrate(basis_values, weights, start, stop)
        fulls.append(full)
        arrived.append(flip(packed, "tile", 2))
    lists, arrived[1], occ_before, occ_after = lax.optimization_barrier(
        (lists, arrived[1], occ_before, occ_after)
    )
    hams, places = [], []
    for i, (start, stop) in enumerate(((0, middle), (middle, nbatch))):
        far = unpack(arrived[i], stop - start, columns)
        hams += [fulls[i], flip(fulls[i], "tile", 1), far, flip(far, "tile", 1)]
        places += [array[start:stop] for array in lists]
    blocks_near = lists[1]
    virt_near = flip(virt_coef, "tile", 1)
    energy_near = flip(virt_energy, "tile", 1)

    to_before, own_sum, to_after = apply_window(
        places,
        hams,
        occ_before,
        occ_own,
        occ_after,
    )
    size = lax.axis_size("grid")
    from_before = lax.ppermute(to_after, "grid", [(i, (i + 1) % size) for i in range(size)])
    from_after = lax.ppermute(to_before, "grid", [((i + 1) % size, i) for i in range(size)])
    ham_own = (own_sum + from_before.astype(F32) + from_after.astype(F32)).astype(BF16)
    ham_sums = [ham_own, flip(ham_own, "tile", 2)]

    occ_far = column_part(occ_coef, quarter ^ 1, width)
    late_before, late_after, _ = lax.optimization_barrier((occ_before, occ_after, ham_sums[1]))
    before_far, after_far = flip(late_before, "tile", 2), flip(late_after, "tile", 2)

    levels = [
        lax.dynamic_slice_in_dim(occ_energy, place * width, width, 0)
        for place in (quarter, quarter ^ 1)
    ]
    virtuals = [(virt_coef, virt_energy), (virt_near, energy_near)]
    coefs = [None, None]
    order = ((0, 0), (1, 0), (1, 1), (0, 1))

    def finish(k, rotation):
        part, share = order[k]
        term = lax.dot_general(virtuals[share][0], rotation, NT, preferred_element_type=F32)
        coefs[part] = term if coefs[part] is None else coefs[part] + term
        return term

    rotations(
        [
            lax.dot_general(
                ham_sums[part],
                virtuals[share][0],
                (((0,), (0,)), ((), ())),
                preferred_element_type=F32,
            )
            for part, share in order
        ],
        [levels[part] for part, share in order],
        [virtuals[share][1] for part, share in order],
        {3: [before_far, after_far]},
        finish,
    )
    coef_far = flip(coefs[1].astype(BF16), "tile", 2)
    resp_own = (coefs[0] + coef_far.astype(F32)).astype(BF16)

    resp_before, resp_after = neighbours(resp_own)
    resp_far, resp_before, resp_after = lax.optimization_barrier(
        (flip(resp_own, "tile", 2), resp_before, resp_after)
    )
    resp_before_far, resp_after_far = flip(resp_before, "tile", 2), flip(resp_after, "tile", 2)
    first = chip == 0
    half = jnp.concatenate(
        [jnp.where(first, resp_own, resp_far), jnp.where(first, resp_far, resp_own)], axis=1
    )
    half_near = flip(half, "tile", 1)
    first = core == 0
    response_coef = jnp.concatenate(
        [jnp.where(first, half, half_near), jnp.where(first, half_near, half)], axis=1
    )

    lists, response_coef = lax.optimization_barrier(([blocks, blocks_near], response_coef))
    overlap_own, overlap_near = overlaps(
        lists,
        columns,
        [occ_before, before_far, occ_own, occ_far, occ_after, after_far],
        [resp_before, resp_before_far, resp_own, resp_far, resp_after, resp_after_far],
        [F32, BF16],
    )
    scale = jnp.where(live_mask, 4.0 * xc_kernel, 0.0)
    response_potential = density(basis_values, overlap_own, flip(overlap_near, "tile", 1), scale)
    return (response_coef, response_potential)


def solution(mesh):
    in_specs = (
        P(("grid", "tile"), None, None),
        P(("grid", "tile"), None),
        P(("grid", "tile")),
        P(("grid", "tile"), None),
        P(("grid", "tile"), None),
        P("grid", None),
        P("grid", "tile"),
        P(),
        P("tile"),
    )
    out_specs = (P("grid", None), P(("grid", "tile"), None))
    return jax.shard_map(
        per_device, mesh=mesh, in_specs=in_specs, out_specs=out_specs, check_vma=False
    )
```

```python
import functools

import jax
import jax.numpy as jnp
from jax import lax
from jax.experimental import pallas as pl
from jax.experimental.pallas import tpu as pltpu
from jax.sharding import PartitionSpec as P

VMEM = pl.BlockSpec(memory_space=pltpu.VMEM)
SMEM = pl.BlockSpec(memory_space=pltpu.SMEM)
HBM = pl.BlockSpec(memory_space=pl.ANY)
MIB = 1024 * 1024
F32 = jnp.float32
BF16 = jnp.bfloat16
NT = (((1,), (1,)), ((), ()))


def params(mib=20):
    return pltpu.CompilerParams(vmem_limit_bytes=mib * MIB)


def split_dot(full, other, dims):
    high = full.astype(BF16)
    low = (full - high.astype(F32)).astype(BF16)
    return lax.dot_general(high, other, dims, preferred_element_type=F32) + lax.dot_general(
        low, other, dims, preferred_element_type=F32
    )


def triangle(size):
    rows = lax.broadcasted_iota(jnp.int32, (size, size), 0)
    return rows, lax.broadcasted_iota(jnp.int32, (size, size), 1)


def live_row(values_ref, counts_ref, b):
    row = values_ref[pl.ds(b, 1), :]
    points = lax.broadcasted_iota(jnp.int32, row.shape, 1)
    return jnp.where(points < counts_ref[b], row, 0.0)


def integrate_kernel(start, counts_ref, basis_ref, weights_ref, full_ref, packed_ref, diagonal):
    steps, here = pl.num_programs(0), basis_ref.shape[0]
    half = full_ref.shape[2] // 2
    row, column = triangle(half)
    now = pl.program_id(0)

    @pl.when(now == 0)
    def _():
        diagonal[...] = jnp.zeros_like(diagonal)

    for b in range(here):
        place = now * here + b
        values = basis_ref[b]
        weighted = values.astype(F32).T * live_row(weights_ref, counts_ref, start + place)
        ham = split_dot(weighted, values, (((1,), (0,)), ((), ())))
        full_ref[b] = ham.astype(BF16)
        last = ham[half:, half:]
        mixed = jnp.where(row >= column, ham[:half, :half], last)
        packed = jnp.concatenate([ham[:half, half:], mixed], axis=1)
        packed_ref[pl.ds(pl.multiple_of(place * half, half), half), :] = packed.astype(BF16)
        line = jnp.sum(jnp.where(row == column, last, 0.0), axis=0, keepdims=True)
        diagonal[pl.ds(place, 1), :] = jnp.concatenate([line, jnp.zeros_like(line)], axis=1)

    @pl.when(now == steps - 1)
    def _():
        packed_ref[steps * here * half :, :] = diagonal[...].astype(BF16)


def padded_rows(nbatch):
    return -(-nbatch // 32) * 32


def step_size(nbatch, most):
    return max(k for k in range(1, most + 1) if nbatch % k == 0)


def integrate(basis_values, counts, weights, start, stop):
    _, points, columns = basis_values.shape
    nbatch = stop - start
    here = step_size(nbatch, 4)
    rows = nbatch * columns // 2 + padded_rows(nbatch)
    first = start // here
    return pl.pallas_call(
        functools.partial(integrate_kernel, start),
        grid=(nbatch // here,),
        out_shape=[
            jax.ShapeDtypeStruct((nbatch, columns, columns), BF16),
            jax.ShapeDtypeStruct((rows, columns), BF16),
        ],
        in_specs=[
            SMEM,
            pl.BlockSpec((here, points, columns), lambda i: (first + i, 0, 0)),
            pl.BlockSpec(weights.shape, lambda i: (0, 0)),
        ],
        out_specs=[
            pl.BlockSpec((here, columns, columns), lambda i: (i, 0, 0)),
            pl.BlockSpec((rows, columns), lambda i: (0, 0)),
        ],
        scratch_shapes=[pltpu.VMEM((padded_rows(nbatch), columns), F32)],
        compiler_params=params(60),
        cost_estimate=pl.CostEstimate(
            flops=4 * nbatch * points * columns * columns,
            bytes_accessed=nbatch * columns * (points * 2 + columns * 3),
            transcendentals=0,
        ),
    )(counts, basis_values, weights)


def unpack_kernel(packed_ref, full_ref, diagonal):
    nbatch = full_ref.shape[0]
    half = full_ref.shape[1] // 2
    row, column = triangle(half)
    diagonal[...] = packed_ref[nbatch * half :, :].astype(F32)

    def step(b, carry):
        packed = packed_ref[pl.ds(pl.multiple_of(b * half, half), half), :].astype(F32)
        turned = packed.T
        mixed, mixed_turned = packed[:, half:], turned[half:]
        first = jnp.where(row >= column, mixed, mixed_turned)
        last = jnp.where(row < column, mixed, mixed_turned)
        last = jnp.where(row == column, diagonal[pl.ds(b, 1), :][:, :half], last)
        upper = jnp.concatenate([first, packed[:, :half]], axis=1)
        lower = jnp.concatenate([turned[:half], last], axis=1)
        full_ref[b] = jnp.concatenate([upper, lower], axis=0).astype(BF16)
        return carry

    lax.fori_loop(0, nbatch, step, 0, unroll=4)


def unpack(packed, nbatch, columns):
    return pl.pallas_call(
        unpack_kernel,
        out_shape=jax.ShapeDtypeStruct((nbatch, columns, columns), BF16),
        in_specs=[VMEM],
        out_specs=VMEM,
        scratch_shapes=[pltpu.VMEM((padded_rows(nbatch), columns), F32)],
        compiler_params=params(),
        cost_estimate=pl.CostEstimate(
            flops=nbatch * columns * columns * 4,
            bytes_accessed=nbatch * columns * columns * 3,
            transcendentals=0,
        ),
    )(packed)


def fetch(copies, semaphores):
    started = [
        pltpu.make_async_copy(source, target, semaphores.at[i])
        for i, (source, target) in enumerate(copies)
    ]
    for copy in started:
        copy.start()
    for copy in started:
        copy.wait()


def row_places(block_ref, b, rows):
    return [
        pl.ds(pl.multiple_of(block_ref[b, j] * rows, rows), rows) for j in range(block_ref.shape[1])
    ]


def apply_kernel(pieces, rows, *refs):
    block_refs, ham_refs = refs[:pieces], refs[pieces : 2 * pieces]
    window_refs = refs[2 * pieces : 2 * pieces + 3]
    out_before, out_own, out_after = refs[2 * pieces + 3 : 2 * pieces + 6]
    hams, window, total, semaphores = refs[2 * pieces + 6 :]
    region = window_refs[0].shape[0]
    copies = [(ref, hams.at[p]) for p, ref in enumerate(ham_refs)]
    for side, ref in enumerate(window_refs):
        copies.append((ref, window.at[pl.ds(side * region, region), :]))
    fetch(copies, semaphores)
    total[...] = jnp.zeros_like(total)

    def step(b, carry):
        places, products = [], []
        for p in range(pieces):
            place = row_places(block_refs[p], b, rows)
            picked = jnp.concatenate([window[at, :] for at in place], axis=0)
            products.append(jnp.dot(hams[p, b], picked, preferred_element_type=F32))
            places.append(place)
        for place, product in zip(places, products):
            for j, at in enumerate(place):
                total[at, :] += product[j * rows : (j + 1) * rows]
        return carry

    lax.fori_loop(0, hams.shape[1], step, 0)
    out_before[...] = total[:region].astype(BF16)
    out_own[...] = total[region : 2 * region]
    out_after[...] = total[2 * region :].astype(BF16)


def apply_window(blocks, hams, before, own, after):
    pieces, per_batch = len(hams), blocks[0].shape[1]
    nbatch, columns = hams[0].shape[:2]
    region, width = own.shape
    return pl.pallas_call(
        functools.partial(apply_kernel, pieces, columns // per_batch),
        out_shape=[
            jax.ShapeDtypeStruct((region, width), BF16),
            jax.ShapeDtypeStruct((region, width), F32),
            jax.ShapeDtypeStruct((region, width), BF16),
        ],
        in_specs=[SMEM] * pieces + [HBM] * (pieces + 3),
        out_specs=[VMEM] * 3,
        scratch_shapes=[
            pltpu.VMEM((pieces, nbatch, columns, columns), BF16),
            pltpu.VMEM((3 * region, width), BF16),
            pltpu.VMEM((3 * region, width), F32),
            pltpu.SemaphoreType.DMA((pieces + 3,)),
        ],
        compiler_params=params(),
        cost_estimate=pl.CostEstimate(
            flops=2 * pieces * nbatch * columns * columns * width,
            bytes_accessed=pieces * nbatch * columns * columns * 2 + 14 * region * width,
            transcendentals=0,
        ),
    )(*blocks, *hams, before, own, after)


def overlap_kernel(pieces, rows, *refs):
    block_refs = refs[:pieces]
    sources = refs[pieces : pieces + 12]
    out_refs = refs[pieces + 12 : 2 * pieces + 12]
    occ, resp, semaphores = refs[2 * pieces + 12 :]
    region, width = sources[0].shape
    copies = []
    for i, source in enumerate(sources):
        target, side, part = (occ, resp)[i // 6], i % 6 // 2, i % 2
        place = (pl.ds(side * region, region), pl.ds(part * width, width))
        copies.append((source, target.at[place]))
    fetch(copies, semaphores)

    def step(b, carry):
        for p in range(pieces):
            place = row_places(block_refs[p], b, rows)
            left = jnp.concatenate([resp[at, :] for at in place], axis=0)
            right = jnp.concatenate([occ[at, :] for at in place], axis=0)
            product = lax.dot_general(left, right, NT, preferred_element_type=F32)
            out_refs[p][b] = product.astype(out_refs[p].dtype)
        return carry

    lax.fori_loop(0, out_refs[0].shape[0], step, 0, unroll=4)


def overlaps(blocks, columns, occ_parts, resp_parts, types):
    pieces = len(blocks)
    nbatch, per_batch = blocks[0].shape
    region, width = occ_parts[0].shape
    return pl.pallas_call(
        functools.partial(overlap_kernel, pieces, columns // per_batch),
        out_shape=[jax.ShapeDtypeStruct((nbatch, columns, columns), kind) for kind in types],
        in_specs=[SMEM] * pieces + [HBM] * 12,
        out_specs=[VMEM] * pieces,
        scratch_shapes=[
            pltpu.VMEM((3 * region, 2 * width), BF16),
            pltpu.VMEM((3 * region, 2 * width), BF16),
            pltpu.SemaphoreType.DMA((12,)),
        ],
        compiler_params=params(),
        cost_estimate=pl.CostEstimate(
            flops=4 * pieces * nbatch * columns * columns * width,
            bytes_accessed=24 * region * width + pieces * nbatch * columns * columns * 3,
            transcendentals=0,
        ),
    )(*blocks, *occ_parts, *resp_parts)


def density_kernel(counts_ref, basis_ref, first_ref, second_ref, scale_ref, out_ref):
    def step(b, carry):
        values = basis_ref[b]
        overlap = first_ref[b] + second_ref[b].astype(F32)
        product = split_dot(overlap, values, NT)
        density = 4.0 * jnp.sum(product * values.astype(F32).T, axis=0, keepdims=True)
        out_ref[pl.ds(b, 1), :] = live_row(scale_ref, counts_ref, b) * density
        return carry

    lax.fori_loop(0, basis_ref.shape[0], step, 0, unroll=4)


def density(basis_values, counts, first, second, scale):
    nbatch, points, columns = basis_values.shape
    return pl.pallas_call(
        density_kernel,
        out_shape=jax.ShapeDtypeStruct((nbatch, points), F32),
        in_specs=[SMEM] + [VMEM] * 4,
        out_specs=VMEM,
        compiler_params=params(),
        cost_estimate=pl.CostEstimate(
            flops=4 * nbatch * points * columns * columns,
            bytes_accessed=basis_values.size * 2 + nbatch * columns * columns * 6,
            transcendentals=0,
        ),
    )(counts, basis_values, first, second, scale)


def flip(array, axis, mask):
    return lax.ppermute(array, axis, [(i, i ^ mask) for i in range(lax.axis_size(axis))])


def neighbours(array):
    size = lax.axis_size("grid")
    before = lax.ppermute(array, "grid", [(i, (i + 1) % size) for i in range(size)])
    after = lax.ppermute(array, "grid", [((i + 1) % size, i) for i in range(size)])
    return before, after


def column_part(array, index, width):
    return lax.dynamic_slice_in_dim(array, index * width, width, 1)


def trade(array, rows, choice):
    keep = lax.dynamic_slice_in_dim(array, choice * rows, rows, 1)
    return keep, lax.dynamic_slice_in_dim(array, (1 - choice) * rows, rows, 1).astype(BF16)


def join(own, other, choice):
    low, high = jnp.where(choice == 0, own, other), jnp.where(choice == 0, other, own)
    return jnp.concatenate([low, high], axis=1)


def partners(masks):
    size, tiles = lax.axis_size("grid"), lax.axis_size("tile")
    return [
        (g * tiles + t, (g ^ masks[t % 2]) * tiles + t) for g in range(size) for t in range(tiles)
    ]


def swap(array, masks):
    return lax.ppermute(array, ("grid", "tile"), partners(masks))


def rotate(parts, levels, energies):
    if lax.axis_size("grid") != 8:
        total = lax.psum(parts, "grid")
        return (total / (levels[None, :, None] - energies[:, None, :])).astype(BF16)
    grid, core = lax.axis_index("grid"), lax.axis_index("tile") % 2
    first, second = (grid >> core) & 1, (grid >> (1 - core)) & 1
    half = parts.shape[1] // 2
    quarter = half // 2
    keep, send = trade(parts, half, first)
    total = keep + swap(send, (1, 2)).astype(F32)
    keep, send = trade(total, quarter, second)
    total = keep + swap(send, (2, 1)).astype(F32)
    total = total + swap(total.astype(BF16), (4, 4)).astype(F32)
    level = lax.dynamic_slice_in_dim(levels, first * half + second * quarter, quarter, 0)
    own = (total / (level[None, :, None] - energies[:, None, :])).astype(BF16)
    own = join(own, swap(own, (2, 1)), second)
    return join(own, swap(own, (1, 2)), first)


def per_device(
    basis_values,
    blocks,
    counts,
    weighted_potential,
    xc_kernel,
    occ_coef,
    virt_coef,
    occ_energy,
    virt_energy,
):
    nbatch, _, columns = basis_values.shape
    region, occ_count = occ_coef.shape
    width = occ_count // lax.axis_size("tile")
    tile = lax.axis_index("tile")
    chip, core = tile // 2, tile % 2
    quarter = 2 * core + chip

    occ_own = column_part(occ_coef, quarter, width)
    occ_before, occ_after = neighbours(occ_own)

    potential, occ_own = lax.optimization_barrier((weighted_potential, occ_own))
    middle = -(-nbatch // 2)
    lists = [blocks, flip(blocks, "tile", 1), flip(blocks, "tile", 2)]
    lists.append(flip(lists[2], "tile", 1))
    fulls, arrived = [], []
    for start, stop in ((0, middle), (middle, nbatch)):
        full, packed = integrate(basis_values, counts, potential, start, stop)
        fulls.append(full)
        arrived.append(flip(packed, "tile", 2))
        potential, lists = lax.optimization_barrier((potential, lists))
    lists, arrived[1], occ_before, occ_after = lax.optimization_barrier(
        (lists, arrived[1], occ_before, occ_after)
    )
    hams, places = [], []
    for i, (start, stop) in enumerate(((0, middle), (middle, nbatch))):
        far = unpack(arrived[i], stop - start, columns)
        hams += [fulls[i], flip(fulls[i], "tile", 1), far, flip(far, "tile", 1)]
        places += [array[start:stop] for array in lists]
    blocks_near = lists[1]
    virt_near = flip(virt_coef, "tile", 1)
    energies = jnp.stack([virt_energy, flip(virt_energy, "tile", 1)])

    to_before, own_sum, to_after = apply_window(
        places,
        hams,
        occ_before,
        occ_own,
        occ_after,
    )
    levels = [
        lax.dynamic_slice_in_dim(occ_energy, place * width, width, 0)
        for place in (quarter, quarter ^ 1)
    ]
    own_sum, energies, levels = lax.optimization_barrier((own_sum, energies, levels))
    size = lax.axis_size("grid")
    from_before = lax.ppermute(to_after, "grid", [(i, (i + 1) % size) for i in range(size)])
    from_after = lax.ppermute(to_before, "grid", [((i + 1) % size, i) for i in range(size)])
    ham_own = (own_sum + from_before.astype(F32) + from_after.astype(F32)).astype(BF16)
    ham_sums = [ham_own, flip(ham_own, "tile", 2)]

    occ_far = column_part(occ_coef, quarter ^ 1, width)
    late_before, late_after, _ = lax.optimization_barrier((occ_before, occ_after, ham_sums[1]))
    before_far, after_far = flip(late_before, "tile", 2), flip(late_after, "tile", 2)

    virtuals = [virt_coef, virt_near]
    parts = []
    for ham_sum in ham_sums:
        ham_sum, parts = lax.optimization_barrier((ham_sum, parts))
        products = [
            lax.dot_general(ham_sum, virt, (((0,), (0,)), ((), ())), preferred_element_type=F32)
            for virt in virtuals
        ]
        parts.append(jnp.stack(products))
    rotated = [rotate(part, level, energies) for part, level in zip(parts, levels)]
    rotated[0], before_far, after_far = lax.optimization_barrier(
        (rotated[0], before_far, after_far)
    )
    coefs = []
    for rotation in rotated:
        terms = [
            lax.dot_general(virt, rotation[i], NT, preferred_element_type=F32)
            for i, virt in enumerate(virtuals)
        ]
        coefs.append(terms[0] + terms[1])
    coef_far = flip(coefs[1].astype(BF16), "tile", 2)
    resp_own = (coefs[0] + coef_far.astype(F32)).astype(BF16)

    resp_before, resp_after = neighbours(resp_own)
    resp_far, resp_before, resp_after = lax.optimization_barrier(
        (flip(resp_own, "tile", 2), resp_before, resp_after)
    )
    resp_before_far, resp_after_far = flip(resp_before, "tile", 2), flip(resp_after, "tile", 2)
    first = chip == 0
    half = jnp.concatenate(
        [jnp.where(first, resp_own, resp_far), jnp.where(first, resp_far, resp_own)], axis=1
    )
    half_near = flip(half, "tile", 1)
    first = core == 0
    response_coef = jnp.concatenate(
        [jnp.where(first, half, half_near), jnp.where(first, half_near, half)], axis=1
    )

    lists, response_coef = lax.optimization_barrier(([blocks, blocks_near], response_coef))
    overlap_own, overlap_near = overlaps(
        lists,
        columns,
        [occ_before, before_far, occ_own, occ_far, occ_after, after_far],
        [resp_before, resp_before_far, resp_own, resp_far, resp_after, resp_after_far],
        [F32, BF16],
    )
    response_potential = density(
        basis_values, counts, overlap_own, flip(overlap_near, "tile", 1), xc_kernel
    )
    return (response_coef, response_potential)


def solution(mesh):
    in_specs = (
        P(("grid", "tile"), None, None),
        P(("grid", "tile"), None),
        P(("grid", "tile")),
        P(("grid", "tile"), None),
        P(("grid", "tile"), None),
        P("grid", None),
        P("grid", "tile"),
        P(),
        P("tile"),
    )
    out_specs = (P("grid", None), P(("grid", "tile"), None))
    return jax.shard_map(
        per_device, mesh=mesh, in_specs=in_specs, out_specs=out_specs, check_vma=False
    )
```

```python
import functools

import jax
import jax.numpy as jnp
from jax import lax
from jax.experimental import pallas as pl
from jax.experimental.pallas import tpu as pltpu
from jax.sharding import PartitionSpec as P

VMEM = pl.BlockSpec(memory_space=pltpu.VMEM)
SMEM = pl.BlockSpec(memory_space=pltpu.SMEM)
HBM = pl.BlockSpec(memory_space=pl.ANY)
MIB = 1024 * 1024
F32 = jnp.float32
BF16 = jnp.bfloat16
NT = (((1,), (1,)), ((), ()))


def params(mib=20):
    return pltpu.CompilerParams(vmem_limit_bytes=mib * MIB)


def split_dot(full, other, dims):
    high = full.astype(BF16)
    low = (full - high.astype(F32)).astype(BF16)
    return lax.dot_general(high, other, dims, preferred_element_type=F32) + lax.dot_general(
        low, other, dims, preferred_element_type=F32
    )


def triangle(size):
    rows = lax.broadcasted_iota(jnp.int32, (size, size), 0)
    return rows, lax.broadcasted_iota(jnp.int32, (size, size), 1)


def live_row(values_ref, counts_ref, b):
    row = values_ref[pl.ds(b, 1), :]
    points = lax.broadcasted_iota(jnp.int32, row.shape, 1)
    return jnp.where(points < counts_ref[b], row, 0.0)


def integrate_kernel(counts_ref, basis_ref, weights_ref, full_ref, *refs):
    packed_refs, diagonal = refs[:-1], refs[-1]
    half = full_ref.shape[2] // 2
    row, column = triangle(half)
    start = 0
    for packed_ref, nbatch in zip(packed_refs, groups(full_ref.shape[0])):
        diagonal[...] = jnp.zeros_like(diagonal)

        def step(b, carry, start=start, packed_ref=packed_ref):
            values = basis_ref[start + b]
            weighted = values.astype(F32).T * live_row(weights_ref, counts_ref, start + b)
            ham = split_dot(weighted, values, (((1,), (0,)), ((), ())))
            full_ref[start + b] = ham.astype(BF16)
            last = ham[half:, half:]
            mixed = jnp.where(row >= column, ham[:half, :half], last)
            packed = jnp.concatenate([ham[:half, half:], mixed], axis=1)
            packed_ref[pl.ds(pl.multiple_of(b * half, half), half), :] = packed.astype(BF16)
            line = jnp.sum(jnp.where(row == column, last, 0.0), axis=0, keepdims=True)
            diagonal[pl.ds(b, 1), :] = jnp.concatenate([line, jnp.zeros_like(line)], axis=1)
            return carry

        lax.fori_loop(0, nbatch, step, 0, unroll=4)
        packed_ref[nbatch * half :, :] = diagonal[: packed_ref.shape[0] - nbatch * half].astype(BF16)
        start += nbatch


def groups(nbatch):
    first = -(-nbatch // 2)
    return [first, nbatch - first] if nbatch > first else [first]


def padded_rows(nbatch):
    return -(-nbatch // 32) * 32


def integrate(basis_values, counts, weights):
    nbatch, points, columns = basis_values.shape
    rows = [count * columns // 2 + padded_rows(count) for count in groups(nbatch)]
    return pl.pallas_call(
        integrate_kernel,
        out_shape=[jax.ShapeDtypeStruct((nbatch, columns, columns), BF16)]
        + [jax.ShapeDtypeStruct((row, columns), BF16) for row in rows],
        in_specs=[SMEM, VMEM, VMEM],
        out_specs=[VMEM] * (1 + len(rows)),
        scratch_shapes=[pltpu.VMEM((padded_rows(groups(nbatch)[0]), columns), F32)],
        compiler_params=params(),
        cost_estimate=pl.CostEstimate(
            flops=4 * nbatch * points * columns * columns,
            bytes_accessed=nbatch * columns * (points * 2 + columns * 3),
            transcendentals=0,
        ),
    )(counts, basis_values, weights)


def unpack_kernel(packed_ref, full_ref, diagonal):
    nbatch = full_ref.shape[0]
    half = full_ref.shape[1] // 2
    row, column = triangle(half)
    diagonal[...] = packed_ref[nbatch * half :, :].astype(F32)

    def step(b, carry):
        packed = packed_ref[pl.ds(pl.multiple_of(b * half, half), half), :].astype(F32)
        turned = packed.T
        mixed, mixed_turned = packed[:, half:], turned[half:]
        first = jnp.where(row >= column, mixed, mixed_turned)
        last = jnp.where(row < column, mixed, mixed_turned)
        last = jnp.where(row == column, diagonal[pl.ds(b, 1), :][:, :half], last)
        upper = jnp.concatenate([first, packed[:, :half]], axis=1)
        lower = jnp.concatenate([turned[:half], last], axis=1)
        full_ref[b] = jnp.concatenate([upper, lower], axis=0).astype(BF16)
        return carry

    lax.fori_loop(0, nbatch, step, 0, unroll=4)


def unpack(packed, nbatch, columns):
    return pl.pallas_call(
        unpack_kernel,
        out_shape=jax.ShapeDtypeStruct((nbatch, columns, columns), BF16),
        in_specs=[VMEM],
        out_specs=VMEM,
        scratch_shapes=[pltpu.VMEM((padded_rows(nbatch), columns), F32)],
        compiler_params=params(),
        cost_estimate=pl.CostEstimate(
            flops=nbatch * columns * columns * 4,
            bytes_accessed=nbatch * columns * columns * 3,
            transcendentals=0,
        ),
    )(packed)


def fetch(copies, semaphores):
    started = [
        pltpu.make_async_copy(source, target, semaphores.at[i])
        for i, (source, target) in enumerate(copies)
    ]
    for copy in started:
        copy.start()
    for copy in started:
        copy.wait()


def row_places(block_ref, b, rows):
    return [
        pl.ds(pl.multiple_of(block_ref[b, j] * rows, rows), rows) for j in range(block_ref.shape[1])
    ]


def apply_kernel(starts, rows, *refs):
    pieces = len(starts)
    block_refs, ham_refs = refs[:pieces], refs[pieces : 2 * pieces]
    window_refs = refs[2 * pieces : 2 * pieces + 3]
    out_before, out_own, out_after = refs[2 * pieces + 3 : 2 * pieces + 6]
    window, total = refs[2 * pieces + 6 :]
    region = window_refs[0].shape[0]
    for side, ref in enumerate(window_refs):
        window[side * region : (side + 1) * region] = ref[...]
    total[...] = jnp.zeros_like(total)

    def steps(members, count):
        def step(b, carry):
            places, products = [], []
            for p in members:
                place = row_places(block_refs[p], starts[p] + b, rows)
                picked = jnp.concatenate([window[at, :] for at in place], axis=0)
                products.append(jnp.dot(ham_refs[p][b], picked, preferred_element_type=F32))
                places.append(place)
            for place, product in zip(places, products):
                for j, at in enumerate(place):
                    total[at, :] += product[j * rows : (j + 1) * rows]
            return carry

        lax.fori_loop(0, count, step, 0, unroll=2)

    counts = [ref.shape[0] for ref in ham_refs]
    for count in sorted(set(counts)):
        steps([p for p in range(pieces) if counts[p] == count], count)
    out_before[...] = total[:region].astype(BF16)
    out_own[...] = total[region : 2 * region]
    out_after[...] = total[2 * region :].astype(BF16)


def apply_window(blocks, hams, starts, before, own, after):
    pieces, per_batch = len(hams), blocks[0].shape[1]
    columns = hams[0].shape[1]
    region, width = own.shape
    work = sum(ham.shape[0] for ham in hams)
    return pl.pallas_call(
        functools.partial(apply_kernel, starts, columns // per_batch),
        out_shape=[
            jax.ShapeDtypeStruct((region, width), BF16),
            jax.ShapeDtypeStruct((region, width), F32),
            jax.ShapeDtypeStruct((region, width), BF16),
        ],
        in_specs=[SMEM] * pieces + [VMEM] * (pieces + 3),
        out_specs=[VMEM] * 3,
        scratch_shapes=[
            pltpu.VMEM((3 * region, width), BF16),
            pltpu.VMEM((3 * region, width), F32),
        ],
        compiler_params=params(),
        cost_estimate=pl.CostEstimate(
            flops=2 * work * columns * columns * width,
            bytes_accessed=work * columns * columns * 2 + 14 * region * width,
            transcendentals=0,
        ),
    )(*blocks, *hams, before, own, after)


def overlap_kernel(pieces, rows, *refs):
    block_refs = refs[:pieces]
    sources = refs[pieces : pieces + 12]
    out_refs = refs[pieces + 12 : 2 * pieces + 12]
    occ, resp, semaphores = refs[2 * pieces + 12 :]
    region, width = sources[0].shape
    copies = []
    for i, source in enumerate(sources):
        target, side, part = (occ, resp)[i // 6], i % 6 // 2, i % 2
        place = (pl.ds(side * region, region), pl.ds(part * width, width))
        copies.append((source, target.at[place]))
    fetch(copies, semaphores)

    def step(b, carry):
        for p in range(pieces):
            place = row_places(block_refs[p], b, rows)
            left = jnp.concatenate([resp[at, :] for at in place], axis=0)
            right = jnp.concatenate([occ[at, :] for at in place], axis=0)
            product = lax.dot_general(left, right, NT, preferred_element_type=F32)
            out_refs[p][b] = product.astype(out_refs[p].dtype)
        return carry

    lax.fori_loop(0, out_refs[0].shape[0], step, 0, unroll=4)


def overlaps(blocks, columns, occ_parts, resp_parts, types):
    pieces = len(blocks)
    nbatch, per_batch = blocks[0].shape
    region, width = occ_parts[0].shape
    return pl.pallas_call(
        functools.partial(overlap_kernel, pieces, columns // per_batch),
        out_shape=[jax.ShapeDtypeStruct((nbatch, columns, columns), kind) for kind in types],
        in_specs=[SMEM] * pieces + [HBM] * 12,
        out_specs=[VMEM] * pieces,
        scratch_shapes=[
            pltpu.VMEM((3 * region, 2 * width), BF16),
            pltpu.VMEM((3 * region, 2 * width), BF16),
            pltpu.SemaphoreType.DMA((12,)),
        ],
        compiler_params=params(),
        cost_estimate=pl.CostEstimate(
            flops=4 * pieces * nbatch * columns * columns * width,
            bytes_accessed=24 * region * width + pieces * nbatch * columns * columns * 3,
            transcendentals=0,
        ),
    )(*blocks, *occ_parts, *resp_parts)


def density_kernel(counts_ref, basis_ref, first_ref, second_ref, scale_ref, out_ref):
    def step(b, carry):
        values = basis_ref[b]
        overlap = first_ref[b] + second_ref[b].astype(F32)
        product = split_dot(overlap, values, NT)
        density = 4.0 * jnp.sum(product * values.astype(F32).T, axis=0, keepdims=True)
        out_ref[pl.ds(b, 1), :] = live_row(scale_ref, counts_ref, b) * density
        return carry

    lax.fori_loop(0, basis_ref.shape[0], step, 0, unroll=4)


def density(basis_values, counts, first, second, scale):
    nbatch, points, columns = basis_values.shape
    return pl.pallas_call(
        density_kernel,
        out_shape=jax.ShapeDtypeStruct((nbatch, points), F32),
        in_specs=[SMEM] + [VMEM] * 4,
        out_specs=VMEM,
        compiler_params=params(),
        cost_estimate=pl.CostEstimate(
            flops=4 * nbatch * points * columns * columns,
            bytes_accessed=basis_values.size * 2 + nbatch * columns * columns * 6,
            transcendentals=0,
        ),
    )(counts, basis_values, first, second, scale)


def flip(array, axis, mask):
    return lax.ppermute(array, axis, [(i, i ^ mask) for i in range(lax.axis_size(axis))])


def neighbours(array):
    size = lax.axis_size("grid")
    before = lax.ppermute(array, "grid", [(i, (i + 1) % size) for i in range(size)])
    after = lax.ppermute(array, "grid", [((i + 1) % size, i) for i in range(size)])
    return before, after


def column_part(array, index, width):
    return lax.dynamic_slice_in_dim(array, index * width, width, 1)


def trade(array, rows, choice):
    keep = lax.dynamic_slice_in_dim(array, choice * rows, rows, 0)
    return keep, lax.dynamic_slice_in_dim(array, (1 - choice) * rows, rows, 0).astype(BF16)


def join(own, other, choice):
    low, high = jnp.where(choice == 0, own, other), jnp.where(choice == 0, other, own)
    return jnp.concatenate([low, high], axis=0)


def halve(part, order):
    half = part.shape[0] // 2
    keep, send = trade(part, half, (lax.axis_index("grid") >> order) & 1)
    return keep, flip(send, "grid", 1 << order)


def rotate(part, level, energy, order, halved):
    if lax.axis_size("grid") != 8:
        total = lax.psum(part, "grid")
        return (total / (level[:, None] - energy[None, :])).astype(BF16)
    grid = lax.axis_index("grid")
    first, second = (grid >> order) & 1, (grid >> (1 - order)) & 1
    half = part.shape[0] // 2
    quarter = half // 2
    keep, coming = halved
    total = keep + coming.astype(F32)
    keep, send = trade(total, quarter, second)
    total = keep + flip(send, "grid", 2 >> order).astype(F32)
    total = total + flip(total.astype(BF16), "grid", 4).astype(F32)
    level = lax.dynamic_slice_in_dim(level, first * half + second * quarter, quarter, 0)
    own = (total / (level[:, None] - energy[None, :])).astype(BF16)
    own = join(own, flip(own, "grid", 2 >> order), second)
    return join(own, flip(own, "grid", 1 << order), first)


def per_device(
    basis_values,
    blocks,
    counts,
    weighted_potential,
    xc_kernel,
    occ_coef,
    virt_coef,
    occ_energy,
    virt_energy,
):
    nbatch, _, columns = basis_values.shape
    region, occ_count = occ_coef.shape
    width = occ_count // lax.axis_size("tile")
    tile = lax.axis_index("tile")
    chip, core = tile // 2, tile % 2
    quarter = 2 * core + chip

    occ_own = column_part(occ_coef, quarter, width)

    lists = [blocks, flip(blocks, "tile", 1), flip(blocks, "tile", 2)]
    ham, *packed = integrate(basis_values, counts, weighted_potential)
    arrived = [flip(array, "tile", 2) for array in packed]
    occ_own, ham, lists = lax.optimization_barrier((occ_own, ham, lists))
    lists.append(flip(lists[2], "tile", 1))
    occ_before, occ_after = neighbours(occ_own)
    hams, places, starts, start = [ham, flip(ham, "tile", 1)], lists[:2], [0, 0], 0
    arrived[-1], occ_before, occ_after = lax.optimization_barrier(
        (arrived[-1], occ_before, occ_after)
    )
    for array, count in zip(arrived, groups(nbatch)):
        far = unpack(array, count, columns)
        hams += [far, flip(far, "tile", 1)]
        places, starts, start = places + lists[2:], starts + [start] * 2, start + count
    blocks_near = lists[1]
    virt_near = flip(virt_coef, "tile", 1)
    energies = [virt_energy, flip(virt_energy, "tile", 1)]

    to_before, own_sum, to_after = apply_window(
        places,
        hams,
        starts,
        occ_before,
        occ_own,
        occ_after,
    )
    levels = [
        lax.dynamic_slice_in_dim(occ_energy, place * width, width, 0)
        for place in (quarter, quarter ^ 1)
    ]
    own_sum, energies, levels = lax.optimization_barrier((own_sum, energies, levels))
    size = lax.axis_size("grid")
    from_before = lax.ppermute(to_after, "grid", [(i, (i + 1) % size) for i in range(size)])
    from_after = lax.ppermute(to_before, "grid", [((i + 1) % size, i) for i in range(size)])
    ham_own = (own_sum + from_before.astype(F32) + from_after.astype(F32)).astype(BF16)
    ham_sums = [ham_own, flip(ham_own, "tile", 2)]

    virtuals = [virt_coef, virt_near]
    parts, halved, (ham_own, ham_far) = [], [], ham_sums
    for side in range(2):
        if side == 1:
            ham_far, parts, halved = lax.optimization_barrier((ham_far, parts, halved))
        for order, virt in enumerate(virtuals):
            ham_sum = (ham_own, ham_far)[side]
            part = lax.dot_general(
                ham_sum, virt, (((0,), (0,)), ((), ())), preferred_element_type=F32
            )
            parts.append(part)
            halved.append(halve(part, order))
    occ_far = column_part(occ_coef, quarter ^ 1, width)
    late_before, late_after, _ = lax.optimization_barrier((occ_before, occ_after, parts[3]))
    before_far, after_far = flip(late_before, "tile", 2), flip(late_after, "tile", 2)

    rotated = [
        rotate(part, levels[i // 2], energies[i % 2], i % 2, halved[i])
        for i, part in enumerate(parts)
    ]
    rotated[0], before_far, after_far = lax.optimization_barrier(
        (rotated[0], before_far, after_far)
    )
    coefs = []
    for i in range(2):
        terms = [
            lax.dot_general(virt, rotation, NT, preferred_element_type=F32)
            for virt, rotation in zip(virtuals, rotated[2 * i : 2 * i + 2])
        ]
        coefs.append(terms[0] + terms[1])
    coef_own, coef_far = lax.optimization_barrier(
        (coefs[0], flip(coefs[1].astype(BF16), "tile", 2))
    )
    resp_own = (coef_own + coef_far.astype(F32)).astype(BF16)

    resp_before, resp_after = neighbours(resp_own)
    resp_before_far, resp_after_far = flip(resp_before, "tile", 2), flip(resp_after, "tile", 2)
    resp_far, *_ = lax.optimization_barrier((flip(resp_own, "tile", 2), resp_before, resp_after))
    first = chip == 0
    half = jnp.concatenate(
        [jnp.where(first, resp_own, resp_far), jnp.where(first, resp_far, resp_own)], axis=1
    )
    half_near = flip(half, "tile", 1)
    first = core == 0
    response_coef = jnp.concatenate(
        [jnp.where(first, half, half_near), jnp.where(first, half_near, half)], axis=1
    )

    lists, response_coef = lax.optimization_barrier(([blocks, blocks_near], response_coef))
    overlap_own, overlap_near = overlaps(
        lists,
        columns,
        [occ_before, before_far, occ_own, occ_far, occ_after, after_far],
        [resp_before, resp_before_far, resp_own, resp_far, resp_after, resp_after_far],
        [F32, BF16],
    )
    response_potential = density(
        basis_values, counts, overlap_own, flip(overlap_near, "tile", 1), xc_kernel
    )
    return (response_coef, response_potential)


def solution(mesh):
    in_specs = (
        P(("grid", "tile"), None, None),
        P(("grid", "tile"), None),
        P(("grid", "tile")),
        P(("grid", "tile"), None),
        P(("grid", "tile"), None),
        P("grid", None),
        P("grid", "tile"),
        P(),
        P("tile"),
    )
    out_specs = (P("grid", None), P(("grid", "tile"), None))
    return jax.shard_map(
        per_device, mesh=mesh, in_specs=in_specs, out_specs=out_specs, check_vma=False
    )
```

```python
import functools

import jax
import jax.numpy as jnp
from jax import lax
from jax.experimental import pallas as pl
from jax.experimental.pallas import tpu as pltpu
from jax.sharding import PartitionSpec as P

VMEM = pl.BlockSpec(memory_space=pltpu.VMEM)
SMEM = pl.BlockSpec(memory_space=pltpu.SMEM)
HBM = pl.BlockSpec(memory_space=pl.ANY)
MIB = 1024 * 1024
F32 = jnp.float32
BF16 = jnp.bfloat16
NT = (((1,), (1,)), ((), ()))


def params(mib=20):
    return pltpu.CompilerParams(vmem_limit_bytes=mib * MIB)


def place_in(array, space):
    return pltpu.with_memory_space_constraint(array, space)


def fetch(copies, semaphores):
    started = [
        pltpu.make_async_copy(source, target, semaphores.at[i])
        for i, (source, target) in enumerate(copies)
    ]
    for copy in started:
        copy.start()
    return started


def load_kernel(source_ref, out_ref, semaphores):
    rows = source_ref.shape[0] // semaphores.shape[0]
    places = [pl.ds(i * rows, rows) for i in range(semaphores.shape[0])]
    for copy in fetch([(source_ref.at[at], out_ref.at[at]) for at in places], semaphores):
        copy.wait()


def load(array):
    parts = 4 if array.shape[0] % 64 == 0 else 1
    return pl.pallas_call(
        load_kernel,
        out_shape=pltpu.VMEM(array.shape, array.dtype),
        in_specs=[HBM],
        out_specs=VMEM,
        scratch_shapes=[pltpu.SemaphoreType.DMA((parts,))],
        compiler_params=params(),
        cost_estimate=pl.CostEstimate(
            flops=0, bytes_accessed=2 * array.size * array.dtype.itemsize, transcendentals=0
        ),
    )(place_in(array, pltpu.HBM))


def split_dot(full, other, dims):
    high = full.astype(BF16)
    low = (full - high.astype(F32)).astype(BF16)
    return lax.dot_general(high, other, dims, preferred_element_type=F32) + lax.dot_general(
        low, other, dims, preferred_element_type=F32
    )


def triangle(size):
    rows = lax.broadcasted_iota(jnp.int32, (size, size), 0)
    return rows, lax.broadcasted_iota(jnp.int32, (size, size), 1)


def live_row(values_ref, counts_ref, b):
    row = values_ref[pl.ds(b, 1), :]
    points = lax.broadcasted_iota(jnp.int32, row.shape, 1)
    return jnp.where(points < counts_ref[b], row, 0.0)


def integrate_kernel(counts_ref, basis_hbm, weights_hbm, full_ref, *refs):
    packed_refs, (diagonal, basis_ref, weights_ref, semaphores) = refs[:-4], refs[-4:]
    half = full_ref.shape[2] // 2
    row, column = triangle(half)
    sizes = groups(full_ref.shape[0])
    starts = [sum(sizes[:i]) for i in range(len(sizes))]
    copies = [(weights_hbm, weights_ref)]
    for start, size in zip(starts, sizes):
        copies.append((basis_hbm.at[pl.ds(start, size)], basis_ref.at[pl.ds(start, size)]))
    weights_copy, *basis_copies = fetch(copies, semaphores)
    weights_copy.wait()
    for copy, packed_ref, start, size in zip(basis_copies, packed_refs, starts, sizes):
        copy.wait()
        diagonal[...] = jnp.zeros_like(diagonal)

        def step(b, carry, start=start, packed_ref=packed_ref):
            values = basis_ref[start + b]
            weighted = values.astype(F32).T * live_row(weights_ref, counts_ref, start + b)
            ham = split_dot(weighted, values, (((1,), (0,)), ((), ())))
            full_ref[start + b] = ham.astype(BF16)
            last = ham[half:, half:]
            mixed = jnp.where(row >= column, ham[:half, :half], last)
            packed = jnp.concatenate([ham[:half, half:], mixed], axis=1)
            packed_ref[pl.ds(pl.multiple_of(b * half, half), half), :] = packed.astype(BF16)
            line = jnp.sum(jnp.where(row == column, last, 0.0), axis=0, keepdims=True)
            diagonal[pl.ds(b, 1), :] = jnp.concatenate([line, jnp.zeros_like(line)], axis=1)
            return carry

        lax.fori_loop(0, size, step, 0, unroll=4)
        tail = packed_ref.shape[0] - size * half
        packed_ref[size * half :, :] = diagonal[:tail].astype(BF16)


def groups(nbatch):
    first = -(-nbatch // 2)
    return [first, nbatch - first] if nbatch > first else [first]


def padded_rows(nbatch):
    return -(-nbatch // 32) * 32


def integrate(basis_values, counts, weights):
    nbatch, points, columns = basis_values.shape
    sizes = groups(nbatch)
    rows = [size * columns // 2 + padded_rows(size) for size in sizes]
    return pl.pallas_call(
        integrate_kernel,
        out_shape=[pltpu.VMEM((nbatch, columns, columns), BF16)]
        + [jax.ShapeDtypeStruct((row, columns), BF16) for row in rows],
        in_specs=[SMEM, HBM, HBM],
        out_specs=[VMEM] * (1 + len(rows)),
        scratch_shapes=[
            pltpu.VMEM((padded_rows(sizes[0]), columns), F32),
            pltpu.VMEM(basis_values.shape, BF16),
            pltpu.VMEM(weights.shape, F32),
            pltpu.SemaphoreType.DMA((1 + len(sizes),)),
        ],
        compiler_params=params(),
        cost_estimate=pl.CostEstimate(
            flops=4 * nbatch * points * columns * columns,
            bytes_accessed=nbatch * columns * (points * 2 + columns * 3),
            transcendentals=0,
        ),
    )(counts, place_in(basis_values, pltpu.HBM), place_in(weights, pltpu.HBM))


def unpack_kernel(packed_ref, full_ref, diagonal):
    nbatch = full_ref.shape[0]
    half = full_ref.shape[1] // 2
    row, column = triangle(half)
    diagonal[...] = packed_ref[nbatch * half :, :].astype(F32)

    def step(b, carry):
        packed = packed_ref[pl.ds(pl.multiple_of(b * half, half), half), :].astype(F32)
        turned = packed.T
        mixed, mixed_turned = packed[:, half:], turned[half:]
        first = jnp.where(row >= column, mixed, mixed_turned)
        last = jnp.where(row < column, mixed, mixed_turned)
        last = jnp.where(row == column, diagonal[pl.ds(b, 1), :][:, :half], last)
        upper = jnp.concatenate([first, packed[:, :half]], axis=1)
        lower = jnp.concatenate([turned[:half], last], axis=1)
        full_ref[b] = jnp.concatenate([upper, lower], axis=0).astype(BF16)
        return carry

    lax.fori_loop(0, nbatch, step, 0, unroll=4)


def unpack(packed, nbatch, columns):
    return pl.pallas_call(
        unpack_kernel,
        out_shape=jax.ShapeDtypeStruct((nbatch, columns, columns), BF16),
        in_specs=[VMEM],
        out_specs=VMEM,
        scratch_shapes=[pltpu.VMEM((padded_rows(nbatch), columns), F32)],
        compiler_params=params(),
        cost_estimate=pl.CostEstimate(
            flops=nbatch * columns * columns * 4,
            bytes_accessed=nbatch * columns * columns * 3,
            transcendentals=0,
        ),
    )(packed)


def row_places(block_ref, b, rows):
    return [
        pl.ds(pl.multiple_of(block_ref[b, j] * rows, rows), rows) for j in range(block_ref.shape[1])
    ]


def apply_kernel(starts, rows, *refs):
    pieces = len(starts)
    block_refs, ham_refs = refs[:pieces], refs[pieces : 2 * pieces]
    window_refs = refs[2 * pieces : 2 * pieces + 3]
    out_before, out_own, out_after = refs[2 * pieces + 3 : 2 * pieces + 6]
    window, total = refs[2 * pieces + 6 :]
    region = window_refs[0].shape[0]
    for side, ref in enumerate(window_refs):
        window[side * region : (side + 1) * region] = ref[...]
    total[...] = jnp.zeros_like(total)

    def steps(members, count):
        def step(b, carry):
            places, products = [], []
            for p, first in members:
                place = row_places(block_refs[p], starts[p] + first + b, rows)
                picked = jnp.concatenate([window[at, :] for at in place], axis=0)
                products.append(jnp.dot(ham_refs[p][first + b], picked, preferred_element_type=F32))
                places.append(place)
            for place, product in zip(places, products):
                for j, at in enumerate(place):
                    total[at, :] += product[j * rows : (j + 1) * rows]
            return carry

        lax.fori_loop(0, count, step, 0, unroll=2)

    shares = {}
    smallest = min(ref.shape[0] for ref in ham_refs)
    for p, ref in enumerate(ham_refs):
        for first in range(0, ref.shape[0], smallest):
            count = min(smallest, ref.shape[0] - first)
            shares.setdefault(count, []).append((p, first))
    for count, members in shares.items():
        steps(members, count)
    out_before[...] = total[:region].astype(BF16)
    out_own[...] = total[region : 2 * region]
    out_after[...] = total[2 * region :].astype(BF16)


def apply_window(blocks, hams, starts, before, own, after):
    pieces, per_batch = len(hams), blocks[0].shape[1]
    columns = hams[0].shape[1]
    region, width = own.shape
    work = sum(ham.shape[0] for ham in hams)
    return pl.pallas_call(
        functools.partial(apply_kernel, starts, columns // per_batch),
        out_shape=[
            jax.ShapeDtypeStruct((region, width), BF16),
            jax.ShapeDtypeStruct((region, width), F32),
            jax.ShapeDtypeStruct((region, width), BF16),
        ],
        in_specs=[SMEM] * pieces + [VMEM] * (pieces + 3),
        out_specs=[VMEM] * 3,
        scratch_shapes=[
            pltpu.VMEM((3 * region, width), BF16),
            pltpu.VMEM((3 * region, width), F32),
        ],
        compiler_params=params(),
        cost_estimate=pl.CostEstimate(
            flops=2 * work * columns * columns * width,
            bytes_accessed=work * columns * columns * 2 + 14 * region * width,
            transcendentals=0,
        ),
    )(*blocks, *[place_in(array, pltpu.VMEM) for array in (*hams, before, own, after)])


def overlap_kernel(pieces, rows, *refs):
    block_refs = refs[:pieces]
    sources = refs[pieces : pieces + 12]
    out_refs = refs[pieces + 12 : 2 * pieces + 12]
    occ, resp = refs[2 * pieces + 12 :]
    region, width = sources[0].shape
    for i, source in enumerate(sources):
        target, side, part = (occ, resp)[i // 6], i % 6 // 2, i % 2
        target[side * region : (side + 1) * region, part * width : (part + 1) * width] = source[...]

    def step(b, carry):
        for p in range(pieces):
            place = row_places(block_refs[p], b, rows)
            left = jnp.concatenate([resp[at, :] for at in place], axis=0)
            right = jnp.concatenate([occ[at, :] for at in place], axis=0)
            product = lax.dot_general(left, right, NT, preferred_element_type=F32)
            out_refs[p][b] = product.astype(out_refs[p].dtype)
        return carry

    lax.fori_loop(0, out_refs[0].shape[0], step, 0, unroll=4)


def overlaps(blocks, columns, occ_parts, resp_parts, types):
    pieces = len(blocks)
    nbatch, per_batch = blocks[0].shape
    region, width = occ_parts[0].shape
    return pl.pallas_call(
        functools.partial(overlap_kernel, pieces, columns // per_batch),
        out_shape=[pltpu.VMEM((nbatch, columns, columns), kind) for kind in types],
        in_specs=[SMEM] * pieces + [VMEM] * 12,
        out_specs=[VMEM] * pieces,
        scratch_shapes=[pltpu.VMEM((3 * region, 2 * width), BF16)] * 2,
        compiler_params=params(),
        cost_estimate=pl.CostEstimate(
            flops=4 * pieces * nbatch * columns * columns * width,
            bytes_accessed=24 * region * width + pieces * nbatch * columns * columns * 3,
            transcendentals=0,
        ),
    )(*blocks, *[place_in(array, pltpu.VMEM) for array in (*occ_parts, *resp_parts)])


def density_kernel(counts_ref, basis_ref, first_ref, second_ref, scale_ref, out_ref):
    def step(b, carry):
        values = basis_ref[b]
        overlap = first_ref[b] + second_ref[b].astype(F32)
        product = split_dot(overlap, values, NT)
        density = 4.0 * jnp.sum(product * values.astype(F32).T, axis=0, keepdims=True)
        out_ref[pl.ds(b, 1), :] = live_row(scale_ref, counts_ref, b) * density
        return carry

    lax.fori_loop(0, basis_ref.shape[0], step, 0, unroll=4)


def density(basis_values, counts, first, second, scale):
    nbatch, points, columns = basis_values.shape
    return pl.pallas_call(
        density_kernel,
        out_shape=jax.ShapeDtypeStruct((nbatch, points), F32),
        in_specs=[SMEM] + [VMEM] * 4,
        out_specs=VMEM,
        compiler_params=params(),
        cost_estimate=pl.CostEstimate(
            flops=4 * nbatch * points * columns * columns,
            bytes_accessed=basis_values.size * 2 + nbatch * columns * columns * 6,
            transcendentals=0,
        ),
    )(counts, basis_values, first, second, scale)


def flip(array, axis, mask):
    return lax.ppermute(array, axis, [(i, i ^ mask) for i in range(lax.axis_size(axis))])


def neighbours(array):
    size = lax.axis_size("grid")
    before = lax.ppermute(array, "grid", [(i, (i + 1) % size) for i in range(size)])
    after = lax.ppermute(array, "grid", [((i + 1) % size, i) for i in range(size)])
    return before, after


def column_part(array, index, width):
    return lax.dynamic_slice_in_dim(array, index * width, width, 1)


def trade(array, rows, choice):
    keep = lax.dynamic_slice_in_dim(array, choice * rows, rows, 1)
    return keep, lax.dynamic_slice_in_dim(array, (1 - choice) * rows, rows, 1).astype(BF16)


def join(own, other, choice):
    low, high = jnp.where(choice == 0, own, other), jnp.where(choice == 0, other, own)
    return jnp.concatenate([low, high], axis=1)


def halve(part, order):
    half = part.shape[1] // 2
    keep, send = trade(part, half, (lax.axis_index("grid") >> order) & 1)
    return keep, flip(send, "grid", 1 << order)


def rotate(part, level, energy, order, halved):
    if lax.axis_size("grid") != 8:
        total = lax.psum(part, "grid")
        return (total / (level[None, :, None] - energy[:, None, :])).astype(BF16)
    grid = lax.axis_index("grid")
    first, second = (grid >> order) & 1, (grid >> (1 - order)) & 1
    half = part.shape[1] // 2
    quarter = half // 2
    keep, coming = halved
    total = keep + coming.astype(F32)
    keep, send = trade(total, quarter, second)
    total = keep + flip(send, "grid", 2 >> order).astype(F32)
    total = total + flip(total.astype(BF16), "grid", 4).astype(F32)
    level = lax.dynamic_slice_in_dim(level, first * half + second * quarter, quarter, 0)
    own = (total / (level[None, :, None] - energy[:, None, :])).astype(BF16)
    own = join(own, flip(own, "grid", 2 >> order), second)
    return join(own, flip(own, "grid", 1 << order), first)


def per_device(
    basis_values,
    blocks,
    counts,
    weighted_potential,
    xc_kernel,
    occ_coef,
    virt_coef,
    occ_energy,
    virt_energy,
):
    nbatch, _, columns = basis_values.shape
    region, occ_count = occ_coef.shape
    width = occ_count // lax.axis_size("tile")
    tile = lax.axis_index("tile")
    chip, core = tile // 2, tile % 2
    quarter = 2 * core + chip

    occ_own = column_part(occ_coef, quarter, width)

    lists = [blocks, flip(blocks, "tile", 1), flip(blocks, "tile", 2)]
    ham, *packed = integrate(basis_values, counts, weighted_potential)
    arrived = [flip(array, "tile", 2) for array in packed]
    occ_own, ham, lists = lax.optimization_barrier((occ_own, ham, lists))
    lists.append(flip(lists[2], "tile", 1))
    occ_before, occ_after = neighbours(occ_own)
    hams, places, starts, start = [ham, flip(ham, "tile", 1)], lists[:2], [0, 0], 0
    arrived[-1], occ_before, occ_after = lax.optimization_barrier(
        (arrived[-1], occ_before, occ_after)
    )
    for array, count in zip(arrived, groups(nbatch)):
        far = unpack(array, count, columns)
        hams += [far, flip(far, "tile", 1)]
        places, starts, start = places + lists[2:], starts + [start] * 2, start + count
    blocks_near = lists[1]
    virtuals = [load(virt_coef), load(flip(virt_coef, "tile", 1))]
    energies = jnp.stack([virt_energy, flip(virt_energy, "tile", 1)])

    to_before, own_sum, to_after = apply_window(
        places,
        hams,
        starts,
        occ_before,
        occ_own,
        occ_after,
    )
    levels = [
        lax.dynamic_slice_in_dim(occ_energy, place * width, width, 0)
        for place in (quarter, quarter ^ 1)
    ]
    own_sum, energies, levels, virtuals = lax.optimization_barrier(
        (own_sum, energies, levels, virtuals)
    )
    size = lax.axis_size("grid")
    from_before = lax.ppermute(to_after, "grid", [(i, (i + 1) % size) for i in range(size)])
    from_after = lax.ppermute(to_before, "grid", [((i + 1) % size, i) for i in range(size)])
    ham_own = (own_sum + from_before.astype(F32) + from_after.astype(F32)).astype(BF16)

    parts, halved = [], []
    for order, ham_sum in enumerate((ham_own, ham_own)):
        if order == 1:
            ham_sum, parts = lax.optimization_barrier((ham_sum, parts))
            ham_sum = flip(ham_sum, "tile", 2)
        products = [
            lax.dot_general(ham_sum, virt, (((0,), (0,)), ((), ())), preferred_element_type=F32)
            for virt in virtuals
        ]
        parts.append(jnp.stack(products))
        halved.append(halve(parts[order], order))

    occ_far = column_part(occ_coef, quarter ^ 1, width)
    late_before, late_after, _ = lax.optimization_barrier((occ_before, occ_after, parts[1]))
    before_far, after_far = flip(late_before, "tile", 2), flip(late_after, "tile", 2)

    rotated = [
        rotate(part, levels[order], energies, order, halved[order])
        for order, part in enumerate(parts)
    ]
    rotated[0], before_far, after_far = lax.optimization_barrier(
        (rotated[0], before_far, after_far)
    )
    coefs = []
    for rotation in rotated:
        terms = [
            lax.dot_general(virt, rotation[i], NT, preferred_element_type=F32)
            for i, virt in enumerate(virtuals)
        ]
        coefs.append(terms[0] + terms[1])
    coef_own, coef_far = lax.optimization_barrier(
        (coefs[0], flip(coefs[1].astype(BF16), "tile", 2))
    )
    resp_own = (coef_own + coef_far.astype(F32)).astype(BF16)

    resp_before, resp_after = neighbours(resp_own)
    resp_before_far, resp_after_far = flip(resp_before, "tile", 2), flip(resp_after, "tile", 2)
    resp_far, *_ = lax.optimization_barrier((flip(resp_own, "tile", 2), resp_before, resp_after))
    first = chip == 0
    half = jnp.concatenate(
        [jnp.where(first, resp_own, resp_far), jnp.where(first, resp_far, resp_own)], axis=1
    )
    half_near = flip(half, "tile", 1)
    first = core == 0
    response_coef = jnp.concatenate(
        [jnp.where(first, half, half_near), jnp.where(first, half_near, half)], axis=1
    )

    lists, response_coef = lax.optimization_barrier(([blocks, blocks_near], response_coef))
    overlap_own, overlap_near = overlaps(
        lists,
        columns,
        [occ_before, before_far, occ_own, occ_far, occ_after, after_far],
        [resp_before, resp_before_far, resp_own, resp_far, resp_after, resp_after_far],
        [F32, BF16],
    )
    response_potential = density(
        basis_values, counts, overlap_own, flip(overlap_near, "tile", 1), xc_kernel
    )
    return (response_coef, response_potential)


def solution(mesh):
    in_specs = (
        P(("grid", "tile"), None, None),
        P(("grid", "tile"), None),
        P(("grid", "tile")),
        P(("grid", "tile"), None),
        P(("grid", "tile"), None),
        P("grid", None),
        P("grid", "tile"),
        P(),
        P("tile"),
    )
    out_specs = (P("grid", None), P(("grid", "tile"), None))
    return jax.shard_map(
        per_device, mesh=mesh, in_specs=in_specs, out_specs=out_specs, check_vma=False
    )
```

```python
import functools

import jax
import jax.numpy as jnp
from jax import lax
from jax.experimental import pallas as pl
from jax.experimental.pallas import tpu as pltpu
from jax.sharding import PartitionSpec as P

VMEM = pl.BlockSpec(memory_space=pltpu.VMEM)
SMEM = pl.BlockSpec(memory_space=pltpu.SMEM)
HBM = pl.BlockSpec(memory_space=pl.ANY)
MIB = 1024 * 1024
F32 = jnp.float32
BF16 = jnp.bfloat16
NT = (((1,), (1,)), ((), ()))


def params(mib=4):
    return pltpu.CompilerParams(vmem_limit_bytes=mib * MIB)


def place_in(array, space):
    return pltpu.with_memory_space_constraint(array, space)


def fetch(copies, semaphores):
    started = [
        pltpu.make_async_copy(source, target, semaphores.at[i])
        for i, (source, target) in enumerate(copies)
    ]
    for copy in started:
        copy.start()
    return started


def load_kernel(source_ref, out_ref, semaphores):
    rows = source_ref.shape[0] // semaphores.shape[0]
    places = [pl.ds(i * rows, rows) for i in range(semaphores.shape[0])]
    for copy in fetch([(source_ref.at[at], out_ref.at[at]) for at in places], semaphores):
        copy.wait()


def load(array):
    parts = 4 if array.shape[0] % 64 == 0 else 1
    return pl.pallas_call(
        load_kernel,
        out_shape=pltpu.VMEM(array.shape, array.dtype),
        in_specs=[HBM],
        out_specs=VMEM,
        scratch_shapes=[pltpu.SemaphoreType.DMA((parts,))],
        compiler_params=params(),
        cost_estimate=pl.CostEstimate(
            flops=0, bytes_accessed=2 * array.size * array.dtype.itemsize, transcendentals=0
        ),
    )(place_in(array, pltpu.HBM))


def split_dot(full, other, dims):
    high = full.astype(BF16)
    low = (full - high.astype(F32)).astype(BF16)
    return lax.dot_general(high, other, dims, preferred_element_type=F32) + lax.dot_general(
        low, other, dims, preferred_element_type=F32
    )


def triangle(size):
    rows = lax.broadcasted_iota(jnp.int32, (size, size), 0)
    return rows, lax.broadcasted_iota(jnp.int32, (size, size), 1)


def live_row(values_ref, counts_ref, b):
    row = values_ref[b : b + 1, :]
    points = lax.broadcasted_iota(jnp.int32, row.shape, 1)
    return jnp.where(points < counts_ref[b], row, 0.0)


def integrate_kernel(start, counts_hbm, basis_hbm, weights_hbm, full_ref, packed_ref, *scratch):
    diagonal, basis_ref, weights_ref, counts_ref, semaphores = scratch
    size = full_ref.shape[0]
    half = full_ref.shape[2] // 2
    row, column = triangle(half)
    cut = -(-size // 2)
    copies = [(counts_hbm, counts_ref), (weights_hbm, weights_ref)]
    for place in (pl.ds(0, cut), pl.ds(cut, size - cut)):
        copies.append((basis_hbm.at[pl.ds(start + place.start, place.size)], basis_ref.at[place]))
    waits = fetch(copies if cut < size else copies[:3], semaphores)
    diagonal[...] = jnp.zeros_like(diagonal)
    for b in range(size):
        if b == 0:
            for copy in waits[:3]:
                copy.wait()
        elif b == cut:
            waits[3].wait()
        values = basis_ref[b]
        weighted = values.astype(F32).T * live_row(weights_ref, counts_ref, start + b)
        ham = split_dot(weighted, values, (((1,), (0,)), ((), ())))
        full_ref[b] = ham.astype(BF16)
        last = ham[half:, half:]
        mixed = jnp.where(row >= column, ham[:half, :half], last)
        packed = jnp.concatenate([ham[:half, half:], mixed], axis=1)
        packed_ref[b * half : (b + 1) * half, :] = packed.astype(BF16)
        line = jnp.sum(jnp.where(row == column, last, 0.0), axis=0, keepdims=True)
        diagonal[b : b + 1, :] = jnp.concatenate([line, jnp.zeros_like(line)], axis=1)
    packed_ref[size * half :, :] = diagonal[...].astype(BF16)


def groups(nbatch):
    first = -(-nbatch // 2)
    return [first, nbatch - first] if nbatch > first else [first]


def padded_rows(nbatch):
    return -(-nbatch // 32) * 32


def integrate(basis_values, counts, weights, start, size):
    _, points, columns = basis_values.shape
    extra = padded_rows(size)
    return pl.pallas_call(
        functools.partial(integrate_kernel, start),
        out_shape=[
            pltpu.VMEM((size, columns, columns), BF16),
            jax.ShapeDtypeStruct((size * columns // 2 + extra, columns), BF16),
        ],
        in_specs=[HBM, HBM, HBM],
        out_specs=[VMEM, VMEM],
        scratch_shapes=[
            pltpu.VMEM((extra, columns), F32),
            pltpu.VMEM((size, points, columns), BF16),
            pltpu.VMEM(weights.shape, F32),
            pltpu.SMEM(counts.shape, jnp.int32),
            pltpu.SemaphoreType.DMA((4,)),
        ],
        compiler_params=params(6),
        cost_estimate=pl.CostEstimate(
            flops=4 * size * points * columns * columns,
            bytes_accessed=size * columns * (points * 2 + columns * 3),
            transcendentals=0,
        ),
    )(*[place_in(array, pltpu.HBM) for array in (counts, basis_values, weights)])


def unpack_kernel(packed_ref, full_ref, diagonal):
    nbatch = full_ref.shape[0]
    half = full_ref.shape[1] // 2
    row, column = triangle(half)
    diagonal[...] = packed_ref[nbatch * half :, :].astype(F32)

    def step(b, carry):
        packed = packed_ref[pl.ds(pl.multiple_of(b * half, half), half), :].astype(F32)
        turned = packed.T
        mixed, mixed_turned = packed[:, half:], turned[half:]
        first = jnp.where(row >= column, mixed, mixed_turned)
        last = jnp.where(row < column, mixed, mixed_turned)
        last = jnp.where(row == column, diagonal[pl.ds(b, 1), :][:, :half], last)
        upper = jnp.concatenate([first, packed[:, :half]], axis=1)
        lower = jnp.concatenate([turned[:half], last], axis=1)
        full_ref[b] = jnp.concatenate([upper, lower], axis=0).astype(BF16)
        return carry

    lax.fori_loop(0, nbatch, step, 0, unroll=4)


def unpack(packed, nbatch, columns):
    return pl.pallas_call(
        unpack_kernel,
        out_shape=jax.ShapeDtypeStruct((nbatch, columns, columns), BF16),
        in_specs=[VMEM],
        out_specs=VMEM,
        scratch_shapes=[pltpu.VMEM((padded_rows(nbatch), columns), F32)],
        compiler_params=params(),
        cost_estimate=pl.CostEstimate(
            flops=nbatch * columns * columns * 4,
            bytes_accessed=nbatch * columns * columns * 3,
            transcendentals=0,
        ),
    )(packed)


def row_places(block_ref, b, rows):
    return [
        pl.ds(pl.multiple_of(block_ref[b, j] * rows, rows), rows) for j in range(block_ref.shape[1])
    ]


def apply_kernel(starts, rows, *refs):
    pieces = len(starts)
    block_refs, ham_refs = refs[:pieces], refs[pieces : 2 * pieces]
    window_refs = refs[2 * pieces : 2 * pieces + 3]
    out_before, out_own, out_after = refs[2 * pieces + 3 : 2 * pieces + 6]
    window, total = refs[2 * pieces + 6 :]
    region = window_refs[0].shape[0]
    for side, ref in enumerate(window_refs):
        window[side * region : (side + 1) * region] = ref[...]
    total[...] = jnp.zeros_like(total)

    def steps(members, count):
        def step(b, carry):
            places, products = [], []
            for p, first in members:
                place = row_places(block_refs[p], starts[p] + first + b, rows)
                picked = jnp.concatenate([window[at, :] for at in place], axis=0)
                products.append(jnp.dot(ham_refs[p][first + b], picked, preferred_element_type=F32))
                places.append(place)
            for place, product in zip(places, products):
                for j, at in enumerate(place):
                    total[at, :] += product[j * rows : (j + 1) * rows]
            return carry

        lax.fori_loop(0, count, step, 0, unroll=2)

    shares = {}
    smallest = min(ref.shape[0] for ref in ham_refs)
    for p, ref in enumerate(ham_refs):
        for first in range(0, ref.shape[0], smallest):
            count = min(smallest, ref.shape[0] - first)
            shares.setdefault(count, []).append((p, first))
    for count, members in shares.items():
        steps(members, count)
    out_before[...] = total[:region].astype(BF16)
    out_own[...] = total[region : 2 * region]
    out_after[...] = total[2 * region :].astype(BF16)


def apply_window(blocks, hams, starts, before, own, after):
    pieces, per_batch = len(hams), blocks[0].shape[1]
    columns = hams[0].shape[1]
    region, width = own.shape
    work = sum(ham.shape[0] for ham in hams)
    return pl.pallas_call(
        functools.partial(apply_kernel, starts, columns // per_batch),
        out_shape=[
            jax.ShapeDtypeStruct((region, width), BF16),
            jax.ShapeDtypeStruct((region, width), F32),
            jax.ShapeDtypeStruct((region, width), BF16),
        ],
        in_specs=[SMEM] * pieces + [VMEM] * (pieces + 3),
        out_specs=[VMEM] * 3,
        scratch_shapes=[
            pltpu.VMEM((3 * region, width), BF16),
            pltpu.VMEM((3 * region, width), F32),
        ],
        compiler_params=params(6),
        cost_estimate=pl.CostEstimate(
            flops=2 * work * columns * columns * width,
            bytes_accessed=work * columns * columns * 2 + 14 * region * width,
            transcendentals=0,
        ),
    )(*blocks, *[place_in(array, pltpu.VMEM) for array in (*hams, before, own, after)])


def overlap_kernel(pieces, rows, *refs):
    block_refs = refs[:pieces]
    sources = refs[pieces : pieces + 12]
    out_refs = refs[pieces + 12 : 2 * pieces + 12]
    occ, resp = refs[2 * pieces + 12 :]
    region, width = sources[0].shape
    for i, source in enumerate(sources):
        target, side, part = (occ, resp)[i // 6], i % 6 // 2, i % 2
        target[side * region : (side + 1) * region, part * width : (part + 1) * width] = source[...]

    def step(b, carry):
        for p in range(pieces):
            place = row_places(block_refs[p], b, rows)
            left = jnp.concatenate([resp[at, :] for at in place], axis=0)
            right = jnp.concatenate([occ[at, :] for at in place], axis=0)
            product = lax.dot_general(left, right, NT, preferred_element_type=F32)
            out_refs[p][b] = product.astype(out_refs[p].dtype)
        return carry

    lax.fori_loop(0, out_refs[0].shape[0], step, 0, unroll=4)


def overlaps(blocks, columns, occ_parts, resp_parts, types):
    pieces = len(blocks)
    nbatch, per_batch = blocks[0].shape
    region, width = occ_parts[0].shape
    return pl.pallas_call(
        functools.partial(overlap_kernel, pieces, columns // per_batch),
        out_shape=[pltpu.VMEM((nbatch, columns, columns), kind) for kind in types],
        in_specs=[SMEM] * pieces + [VMEM] * 12,
        out_specs=[VMEM] * pieces,
        scratch_shapes=[pltpu.VMEM((3 * region, 2 * width), BF16)] * 2,
        compiler_params=params(8),
        cost_estimate=pl.CostEstimate(
            flops=4 * pieces * nbatch * columns * columns * width,
            bytes_accessed=24 * region * width + pieces * nbatch * columns * columns * 3,
            transcendentals=0,
        ),
    )(*blocks, *[place_in(array, pltpu.VMEM) for array in (*occ_parts, *resp_parts)])


def density_kernel(counts_ref, basis_ref, first_ref, second_ref, scale_ref, out_ref):
    for b in range(basis_ref.shape[0]):
        values = basis_ref[b]
        overlap = first_ref[b] + second_ref[b].astype(F32)
        product = split_dot(overlap, values, NT)
        density = 4.0 * jnp.sum(product * values.astype(F32).T, axis=0, keepdims=True)
        out_ref[b : b + 1, :] = live_row(scale_ref, counts_ref, b) * density


def density(basis_values, counts, first, second, scale):
    nbatch, points, columns = basis_values.shape
    return pl.pallas_call(
        density_kernel,
        out_shape=jax.ShapeDtypeStruct((nbatch, points), F32),
        in_specs=[SMEM] + [VMEM] * 4,
        out_specs=VMEM,
        compiler_params=params(),
        cost_estimate=pl.CostEstimate(
            flops=4 * nbatch * points * columns * columns,
            bytes_accessed=basis_values.size * 2 + nbatch * columns * columns * 6,
            transcendentals=0,
        ),
    )(counts, basis_values, first, second, scale)


def flip(array, axis, mask):
    return lax.ppermute(array, axis, [(i, i ^ mask) for i in range(lax.axis_size(axis))])


def neighbours(array):
    size = lax.axis_size("grid")
    before = lax.ppermute(array, "grid", [(i, (i + 1) % size) for i in range(size)])
    after = lax.ppermute(array, "grid", [((i + 1) % size, i) for i in range(size)])
    return before, after


def column_part(array, index, width):
    return lax.dynamic_slice_in_dim(array, index * width, width, 1)


def trade(array, rows, choice):
    keep = lax.dynamic_slice_in_dim(array, choice * rows, rows, 1)
    return keep, lax.dynamic_slice_in_dim(array, (1 - choice) * rows, rows, 1).astype(BF16)


def join(own, other, choice):
    low, high = jnp.where(choice == 0, own, other), jnp.where(choice == 0, other, own)
    return jnp.concatenate([low, high], axis=1)


def swap(array, masks):
    size, tiles = lax.axis_size("grid"), lax.axis_size("tile")
    pairs = [
        (g * tiles + t, (g ^ masks[t % 2]) * tiles + t) for g in range(size) for t in range(tiles)
    ]
    return lax.ppermute(array, ("grid", "tile"), pairs)


def together(*arrays):
    return lax.optimization_barrier(arrays)


class Reduction:
    def __init__(self, part, level, energy):
        grid, core = lax.axis_index("grid"), lax.axis_index("tile") % 2
        self.masks = (1, 2), (2, 1)
        self.first, self.second = (grid >> core) & 1, (grid >> (1 - core)) & 1
        self.level, self.energy = level, energy
        self.half = part.shape[1] // 2
        self.keep, send = trade(part, self.half, self.first)
        self.coming = swap(send, self.masks[0])

    def narrow(self):
        total = self.keep + self.coming.astype(F32)
        self.keep, send = trade(total, self.half // 2, self.second)
        self.total = self.keep + swap(send, self.masks[1]).astype(F32)
        self.across = self.total.astype(BF16)

    def cross(self):
        self.coming = flip(self.across, "grid", 4)

    def divide(self):
        quarter = self.half // 2
        place = self.first * self.half + self.second * quarter
        level = lax.dynamic_slice_in_dim(self.level, place, quarter, 0)
        total = self.total + self.coming.astype(F32)
        own = (total / (level[None, :, None] - self.energy[:, None, :])).astype(BF16)
        self.part = join(own, swap(own, self.masks[1]), self.second)
        self.coming = swap(self.part, self.masks[0])

    def result(self):
        return join(self.part, self.coming, self.first)


def per_device(
    basis_values,
    blocks,
    counts,
    weighted_potential,
    xc_kernel,
    occ_coef,
    virt_coef,
    occ_energy,
    virt_energy,
):
    nbatch, _, columns = basis_values.shape
    region, occ_count = occ_coef.shape
    width = occ_count // lax.axis_size("tile")
    tile = lax.axis_index("tile")
    chip, core = tile // 2, tile % 2
    quarter = 2 * core + chip

    occ_own = column_part(occ_coef, quarter, width)

    lists = [blocks, flip(blocks, "tile", 1), flip(blocks, "tile", 2)]
    fulls, arrived, weights = [], [], weighted_potential
    for i, size in enumerate(groups(nbatch)):
        full, packed = integrate(basis_values, counts, weights, sum(groups(nbatch)[:i]), size)
        arrived.append(flip(packed, "tile", 2))
        if i == 0:
            occ_own, full = together(occ_own, full)
            occ_before, occ_after = neighbours(occ_own)
            weights, lists = together(weights, lists)
        fulls.append(full)
    lists.append(flip(lists[2], "tile", 1))
    hams, places, starts = [], [], []
    for i, size in enumerate(groups(nbatch)):
        far = unpack(arrived[i], size, columns)
        hams += [fulls[i], flip(fulls[i], "tile", 1), far, flip(far, "tile", 1)]
        places, starts = places + lists, starts + [sum(groups(nbatch)[:i])] * 4
    blocks_near = lists[1]
    virtuals = [load(virt_coef), load(flip(virt_coef, "tile", 1))]
    energies = jnp.stack([virt_energy, flip(virt_energy, "tile", 1)])

    to_before, own_sum, to_after = apply_window(
        places,
        hams,
        starts,
        occ_before,
        occ_own,
        occ_after,
    )
    levels = [
        lax.dynamic_slice_in_dim(occ_energy, place * width, width, 0)
        for place in (quarter, quarter ^ 1)
    ]
    own_sum, energies, levels, virtuals = lax.optimization_barrier(
        (own_sum, energies, levels, virtuals)
    )
    size = lax.axis_size("grid")
    from_before = lax.ppermute(to_after, "grid", [(i, (i + 1) % size) for i in range(size)])
    from_after = lax.ppermute(to_before, "grid", [((i + 1) % size, i) for i in range(size)])
    ham_own = (own_sum + from_before.astype(F32) + from_after.astype(F32)).astype(BF16)

    occ_far = column_part(occ_coef, quarter ^ 1, width)

    def products(ham_sum):
        dots = [
            lax.dot_general(ham_sum, virt, (((0,), (0,)), ((), ())), preferred_element_type=F32)
            for virt in virtuals
        ]
        return jnp.stack(dots)

    own_part = products(ham_own)
    ham_late, _ = together(ham_own, own_part)
    ham_far = flip(ham_late, "tile", 2)
    far_part = products(ham_far)
    if lax.axis_size("grid") == 8:
        own = Reduction(own_part, levels[0], energies)
        far = Reduction(far_part, levels[1], energies)
        own.narrow()
        far.narrow()
        far.cross()
        own.across, occ_before, occ_after = together(own.across, occ_before, occ_after)
        own.cross()
        before_far, after_far = flip(occ_before, "tile", 2), flip(occ_after, "tile", 2)
        own.coming, before_far, after_far = together(own.coming, before_far, after_far)
        own.divide()
        far.divide()
        rotated = [own.result(), far.result()]
    else:
        rotated = [
            (
                lax.psum(part, "grid") / (level[None, :, None] - energies[:, None, :])
            ).astype(BF16)
            for part, level in zip((own_part, far_part), levels)
        ]
        before_far, after_far = flip(occ_before, "tile", 2), flip(occ_after, "tile", 2)

    coefs = []
    for rotation in rotated:
        terms = [
            lax.dot_general(virt, rotation[i], NT, preferred_element_type=F32)
            for i, virt in enumerate(virtuals)
        ]
        coefs.append(terms[0] + terms[1])
    coef_own, coef_far = lax.optimization_barrier(
        (coefs[0], flip(coefs[1].astype(BF16), "tile", 2))
    )
    resp_own = (coef_own + coef_far.astype(F32)).astype(BF16)

    resp_before, resp_after = neighbours(resp_own)
    resp_before_far = flip(resp_before, "tile", 2)
    resp_after, resp_far = together(resp_after, flip(resp_own, "tile", 2))
    resp_after_far = flip(resp_after, "tile", 2)
    first = chip == 0
    half = jnp.concatenate(
        [jnp.where(first, resp_own, resp_far), jnp.where(first, resp_far, resp_own)], axis=1
    )
    overlap_own, overlap_near = overlaps(
        [blocks, blocks_near],
        columns,
        [occ_before, before_far, occ_own, occ_far, occ_after, after_far],
        [resp_before, resp_before_far, resp_own, resp_far, resp_after, resp_after_far],
        [F32, BF16],
    )
    half_near, overlap_own = together(flip(half, "tile", 1), overlap_own)
    first = core == 0
    response_coef = jnp.concatenate(
        [jnp.where(first, half, half_near), jnp.where(first, half_near, half)], axis=1
    )
    response_potential = density(
        basis_values, counts, overlap_own, flip(overlap_near, "tile", 1), xc_kernel
    )
    return (response_coef, response_potential)


def solution(mesh):
    in_specs = (
        P(("grid", "tile"), None, None),
        P(("grid", "tile"), None),
        P(("grid", "tile")),
        P(("grid", "tile"), None),
        P(("grid", "tile"), None),
        P("grid", None),
        P("grid", "tile"),
        P(),
        P("tile"),
    )
    out_specs = (P("grid", None), P(("grid", "tile"), None))
    return jax.shard_map(
        per_device, mesh=mesh, in_specs=in_specs, out_specs=out_specs, check_vma=False
    )
```

```python
import functools

import jax
import jax.numpy as jnp
from jax import lax
from jax.experimental import pallas as pl
from jax.experimental.pallas import tpu as pltpu
from jax.sharding import PartitionSpec as P

VMEM = pl.BlockSpec(memory_space=pltpu.VMEM)
SMEM = pl.BlockSpec(memory_space=pltpu.SMEM)
HBM = pl.BlockSpec(memory_space=pl.ANY)
MIB = 1024 * 1024
F32 = jnp.float32
BF16 = jnp.bfloat16
LANES = 128
NT = (((1,), (1,)), ((), ()))


def params(mib=4):
    return pltpu.CompilerParams(vmem_limit_bytes=mib * MIB)


def place_in(array, space):
    return pltpu.with_memory_space_constraint(array, space)


def fetch(copies, semaphores):
    started = [
        pltpu.make_async_copy(source, target, semaphores.at[i])
        for i, (source, target) in enumerate(copies)
    ]
    for copy in started:
        copy.start()
    return started


def split_dot(full, other, dims):
    high = full.astype(BF16)
    low = (full - high.astype(F32)).astype(BF16)
    return lax.dot_general(high, other, dims, preferred_element_type=F32) + lax.dot_general(
        low, other, dims, preferred_element_type=F32
    )


def triangle(size):
    rows = lax.broadcasted_iota(jnp.int32, (size, size), 0)
    return rows, lax.broadcasted_iota(jnp.int32, (size, size), 1)


def live_row(values_ref, counts_ref, b):
    row = values_ref[b : b + 1, :]
    points = lax.broadcasted_iota(jnp.int32, row.shape, 1)
    return jnp.where(points < counts_ref[b], row, 0.0)


def integrate_kernel(start, counts_hbm, basis_hbm, weights_hbm, full_ref, packed_ref, *scratch):
    diagonal, basis_ref, weights_ref, counts_ref, semaphores = scratch
    size = full_ref.shape[0]
    half = full_ref.shape[2] // 2
    row, column = triangle(half)
    cut = -(-size // 2)
    copies = [(counts_hbm, counts_ref), (weights_hbm, weights_ref)]
    for place in (pl.ds(0, cut), pl.ds(cut, size - cut)):
        copies.append((basis_hbm.at[pl.ds(start + place.start, place.size)], basis_ref.at[place]))
    waits = fetch(copies if cut < size else copies[:3], semaphores)
    diagonal[...] = jnp.zeros_like(diagonal)
    for b in range(size):
        if b == 0:
            for copy in waits[:3]:
                copy.wait()
        elif b == cut:
            waits[3].wait()
        values = basis_ref[b]
        weighted = values.astype(F32).T * live_row(weights_ref, counts_ref, start + b)
        ham = split_dot(weighted, values, (((1,), (0,)), ((), ())))
        full_ref[b] = ham.astype(BF16)
        last = ham[half:, half:]
        mixed = jnp.where(row >= column, ham[:half, :half], last)
        packed = jnp.concatenate([ham[:half, half:], mixed], axis=1)
        packed_ref[b * half : (b + 1) * half, :] = packed.astype(BF16)
        line = jnp.sum(jnp.where(row == column, last, 0.0), axis=0, keepdims=True)
        diagonal[b : b + 1, :] = jnp.concatenate([line, jnp.zeros_like(line)], axis=1)
    packed_ref[size * half :, :] = diagonal[...].astype(BF16)


def groups(nbatch):
    first = -(-nbatch // 2)
    return [first, nbatch - first] if nbatch > first else [first]


def padded_rows(nbatch):
    return -(-nbatch // 32) * 32


def integrate(basis_values, counts, weights, start, size):
    _, points, columns = basis_values.shape
    extra = padded_rows(size)
    return pl.pallas_call(
        functools.partial(integrate_kernel, start),
        out_shape=[
            pltpu.VMEM((size, columns, columns), BF16),
            jax.ShapeDtypeStruct((size * columns // 2 + extra, columns), BF16),
        ],
        in_specs=[HBM, HBM, HBM],
        out_specs=[VMEM, VMEM],
        scratch_shapes=[
            pltpu.VMEM((extra, columns), F32),
            pltpu.VMEM((size, points, columns), BF16),
            pltpu.VMEM(weights.shape, F32),
            pltpu.SMEM(counts.shape, jnp.int32),
            pltpu.SemaphoreType.DMA((4,)),
        ],
        compiler_params=params(6),
        cost_estimate=pl.CostEstimate(
            flops=4 * size * points * columns * columns,
            bytes_accessed=size * columns * (points * 2 + columns * 3),
            transcendentals=0,
        ),
    )(*[place_in(array, pltpu.HBM) for array in (counts, basis_values, weights)])


def unpack_kernel(packed_ref, full_ref, diagonal):
    nbatch = full_ref.shape[0]
    half = full_ref.shape[1] // 2
    row, column = triangle(half)
    diagonal[...] = packed_ref[nbatch * half :, :].astype(F32)

    def step(b, carry):
        packed = packed_ref[pl.ds(pl.multiple_of(b * half, half), half), :].astype(F32)
        turned = packed.T
        mixed, mixed_turned = packed[:, half:], turned[half:]
        first = jnp.where(row >= column, mixed, mixed_turned)
        last = jnp.where(row < column, mixed, mixed_turned)
        last = jnp.where(row == column, diagonal[pl.ds(b, 1), :][:, :half], last)
        upper = jnp.concatenate([first, packed[:, :half]], axis=1)
        lower = jnp.concatenate([turned[:half], last], axis=1)
        full_ref[b] = jnp.concatenate([upper, lower], axis=0).astype(BF16)
        return carry

    lax.fori_loop(0, nbatch, step, 0, unroll=4)


def unpack(packed, nbatch, columns):
    return pl.pallas_call(
        unpack_kernel,
        out_shape=jax.ShapeDtypeStruct((nbatch, columns, columns), BF16),
        in_specs=[VMEM],
        out_specs=VMEM,
        scratch_shapes=[pltpu.VMEM((padded_rows(nbatch), columns), F32)],
        compiler_params=params(),
        cost_estimate=pl.CostEstimate(
            flops=nbatch * columns * columns * 4,
            bytes_accessed=nbatch * columns * columns * 3,
            transcendentals=0,
        ),
    )(packed)


def row_places(block_ref, b, rows):
    return [
        pl.ds(pl.multiple_of(block_ref[b, j] * rows, rows), rows) for j in range(block_ref.shape[1])
    ]


def apply_kernel(starts, far, rows, *refs):
    pieces = len(starts)
    block_refs, ham_refs = refs[:pieces], list(refs[pieces : 2 * pieces])
    window_refs = refs[2 * pieces : 2 * pieces + 3]
    out_before, out_own, out_after = refs[2 * pieces + 3 : 2 * pieces + 6]
    window, total, semaphores, *held = refs[2 * pieces + 6 :]
    waits = fetch([(ham_refs[p], target) for p, target in zip(far, held)], semaphores)
    for p, target in zip(far, held):
        ham_refs[p] = target
    region = window_refs[0].shape[0]
    for side, ref in enumerate(window_refs):
        window[side * region : (side + 1) * region] = ref[...]
    total[...] = jnp.zeros_like(total)
    for copy in waits:
        copy.wait()

    def steps(members, count):
        def step(b, carry):
            places, products = [], []
            for p, first in members:
                place = row_places(block_refs[p], starts[p] + first + b, rows)
                picked = jnp.concatenate([window[at, :] for at in place], axis=0)
                products.append(jnp.dot(ham_refs[p][first + b], picked, preferred_element_type=F32))
                places.append(place)
            for place, product in zip(places, products):
                for j, at in enumerate(place):
                    total[at, :] += product[j * rows : (j + 1) * rows]
            return carry

        lax.fori_loop(0, count, step, 0, unroll=2)

    shares = {}
    smallest = min(ref.shape[0] for ref in ham_refs)
    for p, ref in enumerate(ham_refs):
        for first in range(0, ref.shape[0], smallest):
            count = min(smallest, ref.shape[0] - first)
            shares.setdefault(count, []).append((p, first))
    for count, members in shares.items():
        steps(members, count)
    out_before[...] = total[:region].astype(BF16)
    out_own[...] = total[region : 2 * region]
    out_after[...] = total[2 * region :].astype(BF16)


def apply_window(blocks, hams, starts, far, before, own, after):
    pieces, per_batch = len(hams), blocks[0].shape[1]
    columns = hams[0].shape[1]
    region, width = own.shape
    work = sum(ham.shape[0] for ham in hams)
    return pl.pallas_call(
        functools.partial(apply_kernel, starts, far, columns // per_batch),
        out_shape=[
            jax.ShapeDtypeStruct((region, width), BF16),
            jax.ShapeDtypeStruct((region, width), F32),
            jax.ShapeDtypeStruct((region, width), BF16),
        ],
        in_specs=[SMEM] * pieces
        + [HBM if p in far else VMEM for p in range(pieces)]
        + [VMEM] * 3,
        out_specs=[VMEM] * 3,
        scratch_shapes=[
            pltpu.VMEM((3 * region, width), BF16),
            pltpu.VMEM((3 * region, width), F32),
            pltpu.SemaphoreType.DMA((len(far),)),
        ]
        + [pltpu.VMEM(hams[p].shape, BF16) for p in far],
        compiler_params=params(8),
        cost_estimate=pl.CostEstimate(
            flops=2 * work * columns * columns * width,
            bytes_accessed=work * columns * columns * 2 + 14 * region * width,
            transcendentals=0,
        ),
    )(
        *blocks,
        *[ham if p in far else place_in(ham, pltpu.VMEM) for p, ham in enumerate(hams)],
        *[place_in(array, pltpu.VMEM) for array in (before, own, after)],
    )


def project_kernel(first_ref, ham_ref, *refs):
    sources, (keep_ref, send_ref, held, semaphores) = refs[:2], refs[2:]
    blocks = semaphores.shape[0] // 2
    width = held.shape[2] // blocks
    copies = []
    for i in range(blocks):
        place = (slice(None), pl.ds(i * width, width))
        for share, source in enumerate(sources):
            copies.append((source.at[place], held.at[(share, *place)]))
    waits = fetch(copies, semaphores)
    turned = ham_ref[...].astype(F32).T.astype(BF16)
    half = turned.shape[0] // 2
    low = first_ref[0] == 0
    for i in range(blocks):
        at = slice(i * width, (i + 1) * width)
        for share in range(2):
            waits[2 * i + share].wait()
            product = jnp.dot(turned, held[share, :, at], preferred_element_type=F32)
            keep_ref[share, :, at] = jnp.where(low, product[:half], product[half:])
            send_ref[share, :, at] = jnp.where(low, product[half:], product[:half]).astype(BF16)


def lane_block(size, most):
    tiles = size // LANES
    return LANES * max(k for k in range(1, tiles + 1) if tiles % k == 0 and k * LANES <= most)


def project(first, ham, virtuals):
    region, width = ham.shape
    virt = virtuals[0].shape[1]
    blocks = virt // lane_block(virt, 512)
    return pl.pallas_call(
        project_kernel,
        out_shape=[
            jax.ShapeDtypeStruct((2, width // 2, virt), F32),
            jax.ShapeDtypeStruct((2, width // 2, virt), BF16),
        ],
        in_specs=[SMEM, VMEM, HBM, HBM],
        out_specs=[VMEM, VMEM],
        scratch_shapes=[
            pltpu.VMEM((2, region, virt), BF16),
            pltpu.SemaphoreType.DMA((2 * blocks,)),
        ],
        compiler_params=params(14),
        cost_estimate=pl.CostEstimate(
            flops=4 * region * width * virt,
            bytes_accessed=4 * region * virt + 6 * width * virt,
            transcendentals=0,
        ),
    )(first.reshape(1), ham, place_in(virtuals[0], pltpu.HBM), virtuals[1])


def expand_kernel(first_ref, part_ref, coming_ref, *refs):
    sources, (out_ref, held, semaphores) = refs[:2], refs[-3:]
    blocks = semaphores.shape[0] // 2
    rows = held.shape[1] // blocks
    copies = []
    for i in range(blocks):
        place = pl.ds(i * rows, rows)
        for share, source in enumerate(sources):
            copies.append((source.at[place], held.at[share, place]))
    waits = fetch(copies, semaphores)
    low = first_ref[0] == 0
    rotations = []
    for share in range(2):
        part, coming = part_ref[share], coming_ref[share]
        halves = [jnp.where(low, part, coming), jnp.where(low, coming, part)]
        rotations.append(jnp.concatenate(halves, axis=0))
    for i in range(blocks):
        at = slice(i * rows, (i + 1) * rows)
        total = None
        for share in range(2):
            waits[2 * i + share].wait()
            product = lax.dot_general(
                held[share, at], rotations[share], NT, preferred_element_type=F32
            )
            total = product if total is None else total + product
        out_ref[at] = total.astype(out_ref.dtype)


def expand(first, part, coming, virtuals, kind, ahead):
    region, virt = virtuals[0].shape
    width = 2 * part.shape[1]
    blocks = 4 if region % 64 == 0 and region > 64 else 1
    return pl.pallas_call(
        expand_kernel,
        out_shape=jax.ShapeDtypeStruct((region, width), kind),
        in_specs=[SMEM, VMEM, VMEM, HBM, HBM] + [HBM] * len(ahead),
        out_specs=VMEM,
        scratch_shapes=[
            pltpu.VMEM((2, region, virt), BF16),
            pltpu.SemaphoreType.DMA((2 * blocks,)),
        ],
        compiler_params=params(14),
        cost_estimate=pl.CostEstimate(
            flops=4 * region * width * virt if kind == BF16 else 0,
            bytes_accessed=4 * region * virt if kind == BF16 else 0,
            transcendentals=0,
        ),
    )(first.reshape(1), part, coming, place_in(virtuals[0], pltpu.HBM), virtuals[1], *ahead)


def overlap_steps(block_ref, occ_ref, resp_ref, out_ref, rows):
    def step(b, carry):
        place = row_places(block_ref, b, rows)
        left = jnp.concatenate([resp_ref[at, :] for at in place], axis=0)
        right = jnp.concatenate([occ_ref[at, :] for at in place], axis=0)
        product = lax.dot_general(left, right, NT, preferred_element_type=F32)
        out_ref[b] = product.astype(out_ref.dtype)
        return carry

    lax.fori_loop(0, out_ref.shape[0], step, 0, unroll=8)


def gather_kernel(rows, block_ref, *refs):
    sources, (out_ref, occ_ref, resp_ref, semaphores) = refs[:12], refs[12:]
    region, width = sources[0].shape
    copies = []
    for i, source in enumerate(sources):
        target, side, part = (occ_ref, resp_ref)[i // 6], i % 6 // 2, i % 2
        place = (pl.ds(side * region, region), pl.ds(part * width, width))
        copies.append((source, target.at[place]))
    for copy in fetch(copies, semaphores):
        copy.wait()
    overlap_steps(block_ref, occ_ref, resp_ref, out_ref, rows)


def gather_overlaps(blocks, columns, occ_parts, resp_parts):
    nbatch, per_batch = blocks.shape
    region, width = occ_parts[0].shape
    return pl.pallas_call(
        functools.partial(gather_kernel, columns // per_batch),
        out_shape=[jax.ShapeDtypeStruct((nbatch, columns, columns), BF16)]
        + [pltpu.VMEM((3 * region, 2 * width), BF16)] * 2,
        in_specs=[SMEM] + [HBM] * 12,
        out_specs=[VMEM] * 3,
        scratch_shapes=[pltpu.SemaphoreType.DMA((12,))],
        compiler_params=params(),
        cost_estimate=pl.CostEstimate(
            flops=4 * nbatch * columns * columns * width,
            bytes_accessed=24 * region * width + nbatch * columns * columns * 2,
            transcendentals=0,
        ),
    )(blocks, *occ_parts, *resp_parts)


def overlap_kernel(rows, block_ref, occ_ref, resp_ref, out_ref):
    overlap_steps(block_ref, occ_ref, resp_ref, out_ref, rows)


def overlaps(blocks, columns, occ_window, resp_window):
    nbatch, per_batch = blocks.shape
    return pl.pallas_call(
        functools.partial(overlap_kernel, columns // per_batch),
        out_shape=pltpu.VMEM((nbatch, columns, columns), F32),
        in_specs=[SMEM, VMEM, VMEM],
        out_specs=VMEM,
        compiler_params=params(),
        cost_estimate=pl.CostEstimate(
            flops=2 * nbatch * columns * columns * occ_window.shape[1],
            bytes_accessed=nbatch * columns * columns * 4,
            transcendentals=0,
        ),
    )(blocks, place_in(occ_window, pltpu.VMEM), place_in(resp_window, pltpu.VMEM))


def density_kernel(
    core_ref, counts_ref, basis_ref, first_ref, second_ref, scale_ref, half_ref, near_ref,
    out_ref, coef_ref, semaphores,
):
    width = half_ref.shape[1]
    copies = []
    for source, place in ((half_ref, core_ref[0]), (near_ref, 1 - core_ref[0])):
        columns = pl.ds(pl.multiple_of(place * width, width), width)
        copies.append((source, coef_ref.at[:, columns]))
    waits = fetch(copies, semaphores)
    for b in range(basis_ref.shape[0]):
        values = basis_ref[b]
        overlap = first_ref[b] + second_ref[b].astype(F32)
        product = split_dot(overlap, values, NT)
        density = 4.0 * jnp.sum(product * values.astype(F32).T, axis=0, keepdims=True)
        out_ref[b : b + 1, :] = live_row(scale_ref, counts_ref, b) * density
    for copy in waits:
        copy.wait()


def density(core, basis_values, counts, first, second, scale, half, half_near):
    nbatch, points, columns = basis_values.shape
    region, width = half.shape
    return pl.pallas_call(
        density_kernel,
        out_shape=[
            jax.ShapeDtypeStruct((nbatch, points), F32),
            jax.ShapeDtypeStruct((region, 2 * width), BF16),
        ],
        in_specs=[SMEM] * 2 + [VMEM] * 4 + [HBM] * 2,
        out_specs=[VMEM, HBM],
        scratch_shapes=[pltpu.SemaphoreType.DMA((2,))],
        compiler_params=params(),
        cost_estimate=pl.CostEstimate(
            flops=4 * nbatch * points * columns * columns,
            bytes_accessed=basis_values.size * 2 + nbatch * columns * columns * 6,
            transcendentals=0,
        ),
    )(core.reshape(1), counts, basis_values, place_in(first, pltpu.VMEM), second, scale, half, half_near)


def flip(array, axis, mask):
    return lax.ppermute(array, axis, [(i, i ^ mask) for i in range(lax.axis_size(axis))])


def neighbours(array):
    size = lax.axis_size("grid")
    before = lax.ppermute(array, "grid", [(i, (i + 1) % size) for i in range(size)])
    after = lax.ppermute(array, "grid", [((i + 1) % size, i) for i in range(size)])
    return before, after


def column_part(array, index, width):
    return lax.dynamic_slice_in_dim(array, index * width, width, 1)


def trade(array, rows, choice):
    keep = lax.dynamic_slice_in_dim(array, choice * rows, rows, 1)
    return keep, lax.dynamic_slice_in_dim(array, (1 - choice) * rows, rows, 1).astype(BF16)


def join(own, other, choice):
    low, high = jnp.where(choice == 0, own, other), jnp.where(choice == 0, other, own)
    return jnp.concatenate([low, high], axis=1)


def swap(array, masks):
    size, tiles = lax.axis_size("grid"), lax.axis_size("tile")
    pairs = [
        (g * tiles + t, (g ^ masks[t % 2]) * tiles + t) for g in range(size) for t in range(tiles)
    ]
    return lax.ppermute(array, ("grid", "tile"), pairs)


def together(*arrays):
    return lax.optimization_barrier(arrays)


class Reduction:
    def __init__(self, ham, virtuals, level, energy):
        grid, core = lax.axis_index("grid"), lax.axis_index("tile") % 2
        self.masks = (1, 2), (2, 1)
        self.first, self.second = (grid >> core) & 1, (grid >> (1 - core)) & 1
        self.level, self.energy = level, energy
        self.half, self.virtuals = ham.shape[1] // 2, virtuals
        self.keep, self.send = project(self.first, ham, virtuals)
        self.coming = swap(self.send, self.masks[0])

    def narrow(self):
        total = self.keep + self.coming.astype(F32)
        self.keep, send = trade(total, self.half // 2, self.second)
        self.total = self.keep + swap(send, self.masks[1]).astype(F32)
        self.across = self.total.astype(BF16)

    def cross(self):
        self.coming = flip(self.across, "grid", 4)

    def divide(self):
        quarter = self.half // 2
        place = self.first * self.half + self.second * quarter
        level = lax.dynamic_slice_in_dim(self.level, place, quarter, 0)
        total = self.total + self.coming.astype(F32)
        own = (total / (level[None, :, None] - self.energy[:, None, :])).astype(BF16)
        self.part = join(own, swap(own, self.masks[1]), self.second)
        self.coming = swap(self.part, self.masks[0])

    def result(self, kind, *ahead):
        return expand(self.first, self.part, self.coming, self.virtuals, kind, ahead)


def per_device(
    basis_values,
    blocks,
    counts,
    weighted_potential,
    xc_kernel,
    occ_coef,
    virt_coef,
    occ_energy,
    virt_energy,
):
    nbatch, _, columns = basis_values.shape
    region, occ_count = occ_coef.shape
    width = occ_count // lax.axis_size("tile")
    tile = lax.axis_index("tile")
    chip, core = tile // 2, tile % 2
    quarter = 2 * core + chip

    occ_own = column_part(occ_coef, quarter, width)

    lists = [blocks, flip(blocks, "tile", 1), flip(blocks, "tile", 2)]
    occ_before, occ_after = neighbours(occ_own)
    sizes, fulls, arrived = groups(nbatch), [], []
    for i, size in enumerate(sizes):
        full, packed = integrate(basis_values, counts, weighted_potential, sum(sizes[:i]), size)
        fulls.append(full)
        arrived.append(flip(packed, "tile", 2))
    arrived[0], occ_before, occ_after = together(arrived[0], occ_before, occ_after)
    arrived[-1], lists[2] = together(arrived[-1], lists[2])
    lists.append(flip(lists[2], "tile", 1))
    hams, places, starts = [], [], []
    for i, size in enumerate(sizes):
        far = unpack(arrived[i], size, columns)
        hams += [fulls[i], flip(fulls[i], "tile", 1), far, flip(far, "tile", 1)]
        places, starts = places + lists, starts + [sum(sizes[:i])] * 4
    blocks_near = lists[1]
    virtuals = [virt_coef, flip(virt_coef, "tile", 1)]
    energies = jnp.stack([virt_energy, flip(virt_energy, "tile", 1)])

    to_before, own_sum, to_after = apply_window(
        places,
        hams,
        starts,
        [p for p in range(len(hams)) if p % 2 == 1],
        occ_before,
        occ_own,
        occ_after,
    )
    levels = [
        lax.dynamic_slice_in_dim(occ_energy, place * width, width, 0)
        for place in (quarter, quarter ^ 1)
    ]
    own_sum, energies, levels = together(own_sum, energies, levels)
    size = lax.axis_size("grid")
    from_before = lax.ppermute(to_after, "grid", [(i, (i + 1) % size) for i in range(size)])
    from_after = lax.ppermute(to_before, "grid", [((i + 1) % size, i) for i in range(size)])
    ham_own = (own_sum + from_before.astype(F32) + from_after.astype(F32)).astype(BF16)

    ham_far = flip(ham_own, "tile", 2)
    occ_far = column_part(occ_coef, quarter ^ 1, width)
    if lax.axis_size("grid") == 8:
        own = Reduction(ham_own, virtuals, levels[0], energies)
        far = Reduction(ham_far, virtuals, levels[1], energies)
        own.narrow()
        far.narrow()
        far.cross()
        own.across, occ_before, occ_after = together(own.across, occ_before, occ_after)
        own.cross()
        before_far, after_far = flip(occ_before, "tile", 2), flip(occ_after, "tile", 2)
        own.coming, before_far, after_far = together(own.coming, before_far, after_far)
        own.divide()
        far.divide()
        coef_far = far.result(BF16)
        coef_own = own.result(F32, coef_far)
    else:
        before_far, after_far = flip(occ_before, "tile", 2), flip(occ_after, "tile", 2)
        coefs = []
        for ham_sum, level in ((ham_own, levels[0]), (ham_far, levels[1])):
            products = [
                lax.dot_general(ham_sum, virt, (((0,), (0,)), ((), ())), preferred_element_type=F32)
                for virt in virtuals
            ]
            total = lax.psum(jnp.stack(products), "grid")
            rotation = (total / (level[None, :, None] - energies[:, None, :])).astype(BF16)
            terms = [
                lax.dot_general(virt, rotation[i], NT, preferred_element_type=F32)
                for i, virt in enumerate(virtuals)
            ]
            coefs.append(terms[0] + terms[1])
        coef_own, coef_far = coefs[0], coefs[1].astype(BF16)
    coef_own, coef_far = together(coef_own, flip(coef_far, "tile", 2))
    resp_own = (coef_own + coef_far.astype(F32)).astype(BF16)

    resp_before, resp_after = neighbours(resp_own)
    resp_before_far = flip(resp_before, "tile", 2)
    resp_after, resp_far = together(resp_after, flip(resp_own, "tile", 2))
    resp_after_far = flip(resp_after, "tile", 2)
    first = chip == 0
    half = jnp.concatenate(
        [jnp.where(first, resp_own, resp_far), jnp.where(first, resp_far, resp_own)], axis=1
    )
    overlap_near, occ_window, resp_window = gather_overlaps(
        blocks_near,
        columns,
        [occ_before, before_far, occ_own, occ_far, occ_after, after_far],
        [resp_before, resp_before_far, resp_own, resp_far, resp_after, resp_after_far],
    )
    response_potential, response_coef = density(
        core,
        basis_values,
        counts,
        overlaps(blocks, columns, occ_window, resp_window),
        flip(overlap_near, "tile", 1),
        xc_kernel,
        half,
        flip(half, "tile", 1),
    )
    return (response_coef, response_potential)


def solution(mesh):
    in_specs = (
        P(("grid", "tile"), None, None),
        P(("grid", "tile"), None),
        P(("grid", "tile")),
        P(("grid", "tile"), None),
        P(("grid", "tile"), None),
        P("grid", None),
        P("grid", "tile"),
        P(),
        P("tile"),
    )
    out_specs = (P("grid", None), P(("grid", "tile"), None))
    return jax.shard_map(
        per_device, mesh=mesh, in_specs=in_specs, out_specs=out_specs, check_vma=False
    )
```

```python
import functools
import math

import jax
import jax.numpy as jnp
from jax import lax
from jax.experimental import pallas as pl
from jax.experimental.pallas import tpu as pltpu
from jax.sharding import PartitionSpec as P

VMEM = pl.BlockSpec(memory_space=pltpu.VMEM)
SMEM = pl.BlockSpec(memory_space=pltpu.SMEM)
HBM = pl.BlockSpec(memory_space=pl.ANY)
MIB = 1024 * 1024
F32 = jnp.float32
BF16 = jnp.bfloat16
NT = (((1,), (1,)), ((), ()))


def params(mib=4):
    return pltpu.CompilerParams(vmem_limit_bytes=mib * MIB)


def place_in(array, space):
    return pltpu.with_memory_space_constraint(array, space)


def fetch(copies, semaphores):
    started = [
        pltpu.make_async_copy(source, target, semaphores.at[i])
        for i, (source, target) in enumerate(copies)
    ]
    for copy in started:
        copy.start()
    return started


def load_kernel(source_ref, out_ref, semaphores):
    rows = source_ref.shape[0] // semaphores.shape[0]
    places = [pl.ds(i * rows, rows) for i in range(semaphores.shape[0])]
    for copy in fetch([(source_ref.at[at], out_ref.at[at]) for at in places], semaphores):
        copy.wait()


def load(array):
    parts = 4 if array.shape[0] % 64 == 0 else 1
    return pl.pallas_call(
        load_kernel,
        out_shape=pltpu.VMEM(array.shape, array.dtype),
        in_specs=[HBM],
        out_specs=VMEM,
        scratch_shapes=[pltpu.SemaphoreType.DMA((parts,))],
        compiler_params=params(),
        cost_estimate=pl.CostEstimate(
            flops=0, bytes_accessed=2 * array.size * array.dtype.itemsize, transcendentals=0
        ),
    )(place_in(array, pltpu.HBM))


def split_dot(full, other, dims):
    high = full.astype(BF16)
    low = (full - high.astype(F32)).astype(BF16)
    return lax.dot_general(high, other, dims, preferred_element_type=F32) + lax.dot_general(
        low, other, dims, preferred_element_type=F32
    )


def triangle(size):
    rows = lax.broadcasted_iota(jnp.int32, (size, size), 0)
    return rows, lax.broadcasted_iota(jnp.int32, (size, size), 1)


def live_row(values_ref, counts_ref, b):
    row = values_ref[b : b + 1, :]
    points = lax.broadcasted_iota(jnp.int32, row.shape, 1)
    return jnp.where(points < counts_ref[b], row, 0.0)


def integrate_kernel(start, counts_hbm, basis_hbm, weights_hbm, full_ref, packed_ref, *scratch):
    diagonal, basis_ref, weights_ref, counts_ref, semaphores = scratch
    size = full_ref.shape[0]
    half = full_ref.shape[2] // 2
    row, column = triangle(half)
    cut = -(-size // 2)
    copies = [(counts_hbm, counts_ref), (weights_hbm, weights_ref)]
    for place in (pl.ds(0, cut), pl.ds(cut, size - cut)):
        copies.append((basis_hbm.at[pl.ds(start + place.start, place.size)], basis_ref.at[place]))
    waits = fetch(copies if cut < size else copies[:3], semaphores)
    diagonal[...] = jnp.zeros_like(diagonal)
    for b in range(size):
        if b == 0:
            for copy in waits[:3]:
                copy.wait()
        elif b == cut:
            waits[3].wait()
        values = basis_ref[b]
        weighted = values.astype(F32).T * live_row(weights_ref, counts_ref, start + b)
        ham = split_dot(weighted, values, (((1,), (0,)), ((), ())))
        full_ref[b] = ham.astype(BF16)
        last = ham[half:, half:]
        mixed = jnp.where(row >= column, ham[:half, :half], last)
        packed = jnp.concatenate([ham[:half, half:], mixed], axis=1)
        packed_ref[b * half : (b + 1) * half, :] = packed.astype(BF16)
        line = jnp.sum(jnp.where(row == column, last, 0.0), axis=0, keepdims=True)
        diagonal[b : b + 1, :] = jnp.concatenate([line, jnp.zeros_like(line)], axis=1)
    packed_ref[size * half :, :] = diagonal[...].astype(BF16)


def groups(nbatch):
    first = -(-nbatch // 2)
    return [first, nbatch - first] if nbatch > first else [first]


def padded_rows(nbatch):
    return -(-nbatch // 32) * 32


def integrate(basis_values, counts, weights, start, size):
    _, points, columns = basis_values.shape
    extra = padded_rows(size)
    return pl.pallas_call(
        functools.partial(integrate_kernel, start),
        out_shape=[
            pltpu.VMEM((size, columns, columns), BF16),
            jax.ShapeDtypeStruct((size * columns // 2 + extra, columns), BF16),
        ],
        in_specs=[HBM, HBM, HBM],
        out_specs=[VMEM, VMEM],
        scratch_shapes=[
            pltpu.VMEM((extra, columns), F32),
            pltpu.VMEM((size, points, columns), BF16),
            pltpu.VMEM(weights.shape, F32),
            pltpu.SMEM(counts.shape, jnp.int32),
            pltpu.SemaphoreType.DMA((4,)),
        ],
        compiler_params=params(6),
        cost_estimate=pl.CostEstimate(
            flops=4 * size * points * columns * columns,
            bytes_accessed=size * columns * (points * 2 + columns * 3),
            transcendentals=0,
        ),
    )(*[place_in(array, pltpu.HBM) for array in (counts, basis_values, weights)])


def unpack_kernel(packed_ref, full_ref, diagonal):
    nbatch = full_ref.shape[0]
    half = full_ref.shape[1] // 2
    row, column = triangle(half)
    diagonal[...] = packed_ref[nbatch * half :, :].astype(F32)

    def step(b, carry):
        packed = packed_ref[pl.ds(pl.multiple_of(b * half, half), half), :].astype(F32)
        turned = packed.T
        mixed, mixed_turned = packed[:, half:], turned[half:]
        first = jnp.where(row >= column, mixed, mixed_turned)
        last = jnp.where(row < column, mixed, mixed_turned)
        last = jnp.where(row == column, diagonal[pl.ds(b, 1), :][:, :half], last)
        upper = jnp.concatenate([first, packed[:, :half]], axis=1)
        lower = jnp.concatenate([turned[:half], last], axis=1)
        full_ref[b] = jnp.concatenate([upper, lower], axis=0).astype(BF16)
        return carry

    lax.fori_loop(0, nbatch, step, 0, unroll=4)


def unpack(packed, nbatch, columns):
    return pl.pallas_call(
        unpack_kernel,
        out_shape=jax.ShapeDtypeStruct((nbatch, columns, columns), BF16),
        in_specs=[VMEM],
        out_specs=VMEM,
        scratch_shapes=[pltpu.VMEM((padded_rows(nbatch), columns), F32)],
        compiler_params=params(),
        cost_estimate=pl.CostEstimate(
            flops=nbatch * columns * columns * 4,
            bytes_accessed=nbatch * columns * columns * 3,
            transcendentals=0,
        ),
    )(packed)


def row_places(block_ref, b, rows):
    return [
        pl.ds(pl.multiple_of(block_ref[b, j] * rows, rows), rows) for j in range(block_ref.shape[1])
    ]


def apply_kernel(starts, rows, *refs):
    pieces = len(starts)
    block_refs, ham_refs = refs[:pieces], refs[pieces : 2 * pieces]
    window_refs = refs[2 * pieces : 2 * pieces + 3]
    out_before, out_own, out_after = refs[2 * pieces + 3 : 2 * pieces + 6]
    window, total = refs[2 * pieces + 6 :]
    region = window_refs[0].shape[0]
    for side, ref in enumerate(window_refs):
        window[side * region : (side + 1) * region] = ref[...]
    total[...] = jnp.zeros_like(total)

    def steps(members, count):
        def step(b, carry):
            places, products = [], []
            for p, first in members:
                place = row_places(block_refs[p], starts[p] + first + b, rows)
                picked = jnp.concatenate([window[at, :] for at in place], axis=0)
                products.append(jnp.dot(ham_refs[p][first + b], picked, preferred_element_type=F32))
                places.append(place)
            for place, product in zip(places, products):
                for j, at in enumerate(place):
                    total[at, :] += product[j * rows : (j + 1) * rows]
            return carry

        lax.fori_loop(0, count, step, 0, unroll=2)

    shares = {}
    smallest = min(ref.shape[0] for ref in ham_refs)
    for p, ref in enumerate(ham_refs):
        for first in range(0, ref.shape[0], smallest):
            count = min(smallest, ref.shape[0] - first)
            shares.setdefault(count, []).append((p, first))
    for count, members in shares.items():
        steps(members, count)
    out_before[...] = total[:region].astype(BF16)
    out_own[...] = total[region : 2 * region]
    out_after[...] = total[2 * region :].astype(BF16)


def apply_window(blocks, hams, starts, before, own, after):
    pieces, per_batch = len(hams), blocks[0].shape[1]
    columns = hams[0].shape[1]
    region, width = own.shape
    work = sum(ham.shape[0] for ham in hams)
    return pl.pallas_call(
        functools.partial(apply_kernel, starts, columns // per_batch),
        out_shape=[
            jax.ShapeDtypeStruct((region, width), BF16),
            jax.ShapeDtypeStruct((region, width), F32),
            jax.ShapeDtypeStruct((region, width), BF16),
        ],
        in_specs=[SMEM] * pieces + [VMEM] * (pieces + 3),
        out_specs=[VMEM] * 3,
        scratch_shapes=[
            pltpu.VMEM((3 * region, width), BF16),
            pltpu.VMEM((3 * region, width), F32),
        ],
        compiler_params=params(6),
        cost_estimate=pl.CostEstimate(
            flops=2 * work * columns * columns * width,
            bytes_accessed=work * columns * columns * 2 + 14 * region * width,
            transcendentals=0,
        ),
    )(
        *blocks,
        *hams,
        *[place_in(array, pltpu.VMEM) for array in (before, own, after)],
    )


def expand_kernel(first_ref, part_ref, coming_ref, *refs):
    sources, (out_ref, held, semaphores) = refs[:2], refs[-3:]
    blocks = semaphores.shape[0] // 2
    rows = held.shape[1] // blocks
    copies = []
    for i in range(blocks):
        place = pl.ds(i * rows, rows)
        for share, source in enumerate(sources):
            copies.append((source.at[place], held.at[share, place]))
    waits = fetch(copies, semaphores)
    low = first_ref[0] == 0
    rotations = []
    for share in range(2):
        part, coming = part_ref[share], coming_ref[share]
        halves = [jnp.where(low, part, coming), jnp.where(low, coming, part)]
        rotations.append(jnp.concatenate(halves, axis=0))
    for i in range(blocks):
        at = slice(i * rows, (i + 1) * rows)
        total = None
        for share in range(2):
            waits[2 * i + share].wait()
            product = lax.dot_general(
                held[share, at], rotations[share], NT, preferred_element_type=F32
            )
            total = product if total is None else total + product
        out_ref[at] = total.astype(out_ref.dtype)


def expand(first, part, coming, virtuals, kind, ahead):
    region, virt = virtuals[0].shape
    width = 2 * part.shape[1]
    blocks = 4 if region % 64 == 0 and region > 64 else 1
    return pl.pallas_call(
        expand_kernel,
        out_shape=jax.ShapeDtypeStruct((region, width), kind),
        in_specs=[SMEM, VMEM, VMEM, HBM, HBM] + [HBM] * len(ahead),
        out_specs=VMEM,
        scratch_shapes=[
            pltpu.VMEM((2, region, virt), BF16),
            pltpu.SemaphoreType.DMA((2 * blocks,)),
        ],
        compiler_params=params(14),
        cost_estimate=pl.CostEstimate(
            flops=4 * region * width * virt if kind == BF16 else 0,
            bytes_accessed=4 * region * virt if kind == BF16 else 0,
            transcendentals=0,
        ),
    )(first.reshape(1), part, coming, place_in(virtuals[0], pltpu.HBM), virtuals[1], *ahead)


def overlap_steps(block_ref, occ_ref, resp_ref, out_ref, rows):
    def step(b, carry):
        place = row_places(block_ref, b, rows)
        left = jnp.concatenate([resp_ref[at, :] for at in place], axis=0)
        right = jnp.concatenate([occ_ref[at, :] for at in place], axis=0)
        product = lax.dot_general(left, right, NT, preferred_element_type=F32)
        out_ref[b] = product.astype(out_ref.dtype)
        return carry

    lax.fori_loop(0, out_ref.shape[0], step, 0, unroll=8)


def gather_kernel(rows, block_ref, *refs):
    sources, (out_ref, occ_ref, resp_ref, semaphores) = refs[:12], refs[12:]
    region, width = sources[0].shape
    copies = []
    for i, source in enumerate(sources):
        target, side, part = (occ_ref, resp_ref)[i // 6], i % 6 // 2, i % 2
        place = (pl.ds(side * region, region), pl.ds(part * width, width))
        copies.append((source, target.at[place]))
    for copy in fetch(copies, semaphores):
        copy.wait()
    overlap_steps(block_ref, occ_ref, resp_ref, out_ref, rows)


def gather_overlaps(blocks, columns, occ_parts, resp_parts):
    nbatch, per_batch = blocks.shape
    region, width = occ_parts[0].shape
    return pl.pallas_call(
        functools.partial(gather_kernel, columns // per_batch),
        out_shape=[jax.ShapeDtypeStruct((nbatch, columns, columns), BF16)]
        + [pltpu.VMEM((3 * region, 2 * width), BF16)] * 2,
        in_specs=[SMEM] + [HBM] * 12,
        out_specs=[VMEM] * 3,
        scratch_shapes=[pltpu.SemaphoreType.DMA((12,))],
        compiler_params=params(),
        cost_estimate=pl.CostEstimate(
            flops=4 * nbatch * columns * columns * width,
            bytes_accessed=24 * region * width + nbatch * columns * columns * 2,
            transcendentals=0,
        ),
    )(blocks, *occ_parts, *resp_parts)


def overlap_kernel(rows, block_ref, occ_ref, resp_ref, out_ref):
    overlap_steps(block_ref, occ_ref, resp_ref, out_ref, rows)


def overlaps(blocks, columns, occ_window, resp_window):
    nbatch, per_batch = blocks.shape
    return pl.pallas_call(
        functools.partial(overlap_kernel, columns // per_batch),
        out_shape=pltpu.VMEM((nbatch, columns, columns), F32),
        in_specs=[SMEM, VMEM, VMEM],
        out_specs=VMEM,
        compiler_params=params(),
        cost_estimate=pl.CostEstimate(
            flops=2 * nbatch * columns * columns * occ_window.shape[1],
            bytes_accessed=nbatch * columns * columns * 4,
            transcendentals=0,
        ),
    )(blocks, place_in(occ_window, pltpu.VMEM), place_in(resp_window, pltpu.VMEM))


def density_kernel(
    core_ref, counts_ref, basis_ref, first_ref, second_ref, scale_ref, half_ref, near_ref,
    out_ref, coef_ref, semaphores,
):
    width = half_ref.shape[1]
    copies = []
    for source, place in ((half_ref, core_ref[0]), (near_ref, 1 - core_ref[0])):
        columns = pl.ds(pl.multiple_of(place * width, width), width)
        copies.append((source, coef_ref.at[:, columns]))
    waits = fetch(copies, semaphores)
    for b in range(basis_ref.shape[0]):
        values = basis_ref[b]
        overlap = first_ref[b] + second_ref[b].astype(F32)
        product = split_dot(overlap, values, NT)
        density = 4.0 * jnp.sum(product * values.astype(F32).T, axis=0, keepdims=True)
        out_ref[b : b + 1, :] = live_row(scale_ref, counts_ref, b) * density
    for copy in waits:
        copy.wait()


def density(core, basis_values, counts, first, second, scale, half, half_near):
    nbatch, points, columns = basis_values.shape
    region, width = half.shape
    return pl.pallas_call(
        density_kernel,
        out_shape=[
            jax.ShapeDtypeStruct((nbatch, points), F32),
            jax.ShapeDtypeStruct((region, 2 * width), BF16),
        ],
        in_specs=[SMEM] * 2 + [VMEM] * 4 + [HBM] * 2,
        out_specs=[VMEM, HBM],
        scratch_shapes=[pltpu.SemaphoreType.DMA((2,))],
        compiler_params=params(),
        cost_estimate=pl.CostEstimate(
            flops=4 * nbatch * points * columns * columns,
            bytes_accessed=basis_values.size * 2 + nbatch * columns * columns * 6,
            transcendentals=0,
        ),
    )(core.reshape(1), counts, basis_values, place_in(first, pltpu.VMEM), second, scale, half, half_near)


def flip(array, axis, mask):
    return lax.ppermute(array, axis, [(i, i ^ mask) for i in range(lax.axis_size(axis))])


def neighbours(array):
    size = lax.axis_size("grid")
    before = lax.ppermute(array, "grid", [(i, (i + 1) % size) for i in range(size)])
    after = lax.ppermute(array, "grid", [((i + 1) % size, i) for i in range(size)])
    return before, after


def column_part(array, index, width):
    return lax.dynamic_slice_in_dim(array, index * width, width, 1)


def trade(array, rows, choice):
    keep = lax.dynamic_slice_in_dim(array, choice * rows, rows, 1)
    return keep, lax.dynamic_slice_in_dim(array, (1 - choice) * rows, rows, 1).astype(BF16)


def join(own, other, choice):
    low, high = jnp.where(choice == 0, own, other), jnp.where(choice == 0, other, own)
    return jnp.concatenate([low, high], axis=1)


def swap(array, masks):
    size, tiles = lax.axis_size("grid"), lax.axis_size("tile")
    pairs = [
        (g * tiles + t, (g ^ masks[t % 2]) * tiles + t) for g in range(size) for t in range(tiles)
    ]
    return lax.ppermute(array, ("grid", "tile"), pairs)


def together(*arrays):
    return lax.optimization_barrier(arrays)


def divide_kernel(place_ref, energy_ref, *refs):
    chunks = len(refs) // 4
    rows = refs[0].shape[1]
    place = pl.multiple_of(place_ref[0], rows)
    for c in range(chunks):
        total_ref, coming_ref, level_ref, out_ref = refs[3 * c : 3 * c + 3] + (refs[3 * chunks + c],)
        level = level_ref[pl.ds(place, rows), :]
        for share in range(total_ref.shape[0]):
            total = total_ref[share] + coming_ref[share].astype(F32)
            gap = level - energy_ref[share : share + 1, :]
            out_ref[share] = (total / gap).astype(out_ref.dtype)


def divide(place, energies, chunks):
    shape = chunks[0].total.shape
    operands = []
    for chunk in chunks:
        operands += [chunk.total, chunk.coming, chunk.level[:, None]]
    return pl.pallas_call(
        divide_kernel,
        out_shape=[pltpu.VMEM(shape, BF16)] * len(chunks),
        in_specs=[SMEM] + [VMEM] * (1 + len(operands)),
        out_specs=[VMEM] * len(chunks),
        compiler_params=params(),
        cost_estimate=pl.CostEstimate(
            flops=len(chunks) * math.prod(shape) * 8, bytes_accessed=0, transcendentals=0
        ),
    )(place.reshape(1), energies, *operands)


class Reduction:
    def __init__(self, part, level):
        grid, core = lax.axis_index("grid"), lax.axis_index("tile") % 2
        self.masks = (1, 2), (2, 1)
        self.first, self.second = (grid >> core) & 1, (grid >> (1 - core)) & 1
        self.level = level
        self.half = part.shape[1] // 2
        self.keep, send = trade(part, self.half, self.first)
        self.coming = swap(send, self.masks[0])

    def narrow(self):
        total = self.keep + self.coming.astype(F32)
        self.keep, send = trade(total, self.half // 2, self.second)
        self.total = self.keep + swap(send, self.masks[1]).astype(F32)
        self.total, self.across = together(self.total, self.total.astype(BF16))

    def cross(self):
        self.coming = flip(self.across, "grid", 4)

    def place(self):
        return self.first * self.half + self.second * (self.half // 2)

    def widen(self, own):
        self.part = join(own, swap(own, self.masks[1]), self.second)
        self.coming = swap(self.part, self.masks[0])

    def result(self, virtuals, kind, *ahead):
        return expand(self.first, self.part, self.coming, virtuals, kind, ahead)


def per_device(
    basis_values,
    blocks,
    counts,
    weighted_potential,
    xc_kernel,
    occ_coef,
    virt_coef,
    occ_energy,
    virt_energy,
):
    nbatch, _, columns = basis_values.shape
    region, occ_count = occ_coef.shape
    width = occ_count // lax.axis_size("tile")
    tile = lax.axis_index("tile")
    chip, core = tile // 2, tile % 2
    quarter = 2 * core + chip

    occ_own = column_part(occ_coef, quarter, width)

    lists = [blocks, flip(blocks, "tile", 1), flip(blocks, "tile", 2)]
    occ_before, occ_after = neighbours(occ_own)
    sizes, fulls, arrived = groups(nbatch), [], []
    for i, size in enumerate(sizes):
        full, packed = integrate(basis_values, counts, weighted_potential, sum(sizes[:i]), size)
        fulls.append(full)
        arrived.append(flip(packed, "tile", 2))
    arrived[0], occ_before, occ_after = together(arrived[0], occ_before, occ_after)
    far = [unpack(array, size, columns) for array, size in zip(arrived, sizes)]
    far[-1], lists[2] = together(far[-1], lists[2])
    lists.append(flip(lists[2], "tile", 1))
    hams = []
    for full, other in zip(fulls, far):
        hams += [full, flip(full, "tile", 1), other, flip(other, "tile", 1)]
    places, blocks_near = lists * len(sizes), lists[1]
    starts = [sum(sizes[:i]) for i in range(len(sizes)) for _ in range(4)]
    virtuals = [virt_coef, flip(virt_coef, "tile", 1)]
    energies = jnp.stack([virt_energy, flip(virt_energy, "tile", 1)])

    to_before, own_sum, to_after = apply_window(
        places,
        hams,
        starts,
        occ_before,
        occ_own,
        occ_after,
    )
    levels = [
        lax.dynamic_slice_in_dim(occ_energy, place * width, width, 0)
        for place in (quarter, quarter ^ 1)
    ]
    loaded = [load(array) for array in virtuals]
    own_sum, energies, levels, loaded = together(own_sum, energies, levels, loaded)
    size = lax.axis_size("grid")
    from_before = lax.ppermute(to_after, "grid", [(i, (i + 1) % size) for i in range(size)])
    from_after = lax.ppermute(to_before, "grid", [((i + 1) % size, i) for i in range(size)])
    ham_own = (own_sum + from_before.astype(F32) + from_after.astype(F32)).astype(BF16)

    def products(ham_sum):
        dots = [
            lax.dot_general(ham_sum, virt, (((0,), (0,)), ((), ())), preferred_element_type=F32)
            for virt in loaded
        ]
        return jnp.stack(dots)

    own_part, far_part = products(ham_own), products(flip(ham_own, "tile", 2))
    occ_far = column_part(occ_coef, quarter ^ 1, width)
    if lax.axis_size("grid") == 8:
        own = Reduction(own_part, levels[0])
        far = Reduction(far_part, levels[1])
        own.narrow()
        far.narrow()
        far.cross()
        own.across, occ_before, occ_after = together(own.across, occ_before, occ_after)
        own.cross()
        before_far, after_far = flip(occ_before, "tile", 2), flip(occ_after, "tile", 2)
        own.coming, before_far, after_far = together(own.coming, before_far, after_far)
        own_rotation, far_rotation = divide(own.place(), energies, [own, far])
        own.widen(own_rotation)
        far.widen(far_rotation)
        coef_far = far.result(virtuals, BF16)
        coef_own = own.result(virtuals, F32, coef_far)
    else:
        before_far, after_far = flip(occ_before, "tile", 2), flip(occ_after, "tile", 2)
        coefs = []
        for part, level in ((own_part, levels[0]), (far_part, levels[1])):
            total = lax.psum(part, "grid")
            rotation = (total / (level[None, :, None] - energies[:, None, :])).astype(BF16)
            terms = [
                lax.dot_general(virt, rotation[i], NT, preferred_element_type=F32)
                for i, virt in enumerate(virtuals)
            ]
            coefs.append(terms[0] + terms[1])
        coef_own, coef_far = coefs[0], coefs[1].astype(BF16)
    coef_own, coef_far = together(coef_own, flip(coef_far, "tile", 2))
    resp_own = (coef_own + coef_far.astype(F32)).astype(BF16)

    resp_before, resp_after = neighbours(resp_own)
    resp_before_far = flip(resp_before, "tile", 2)
    resp_after, resp_far = together(resp_after, flip(resp_own, "tile", 2))
    resp_after_far = flip(resp_after, "tile", 2)
    first = chip == 0
    half = jnp.concatenate(
        [jnp.where(first, resp_own, resp_far), jnp.where(first, resp_far, resp_own)], axis=1
    )
    overlap_near, occ_window, resp_window = gather_overlaps(
        blocks_near,
        columns,
        [occ_before, before_far, occ_own, occ_far, occ_after, after_far],
        [resp_before, resp_before_far, resp_own, resp_far, resp_after, resp_after_far],
    )
    response_potential, response_coef = density(
        core,
        basis_values,
        counts,
        overlaps(blocks, columns, occ_window, resp_window),
        flip(overlap_near, "tile", 1),
        xc_kernel,
        half,
        flip(half, "tile", 1),
    )
    return (response_coef, response_potential)


def solution(mesh):
    in_specs = (
        P(("grid", "tile"), None, None),
        P(("grid", "tile"), None),
        P(("grid", "tile")),
        P(("grid", "tile"), None),
        P(("grid", "tile"), None),
        P("grid", None),
        P("grid", "tile"),
        P(),
        P("tile"),
    )
    out_specs = (P("grid", None), P(("grid", "tile"), None))
    return jax.shard_map(
        per_device, mesh=mesh, in_specs=in_specs, out_specs=out_specs, check_vma=False
    )
```

```python
import functools
import math

import jax
import jax.numpy as jnp
from jax import lax
from jax.experimental import pallas as pl
from jax.experimental.pallas import tpu as pltpu
from jax.sharding import PartitionSpec as P

VMEM = pl.BlockSpec(memory_space=pltpu.VMEM)
SMEM = pl.BlockSpec(memory_space=pltpu.SMEM)
HBM = pl.BlockSpec(memory_space=pl.ANY)
MIB = 1024 * 1024
F32 = jnp.float32
BF16 = jnp.bfloat16
NT = (((1,), (1,)), ((), ()))


def params(mib=4):
    return pltpu.CompilerParams(vmem_limit_bytes=mib * MIB)


def place_in(array, space):
    return pltpu.with_memory_space_constraint(array, space)


def fetch(copies, semaphores):
    started = [
        pltpu.make_async_copy(source, target, semaphores.at[i])
        for i, (source, target) in enumerate(copies)
    ]
    for copy in started:
        copy.start()
    return started


def load_kernel(source_ref, out_ref, semaphores):
    rows = source_ref.shape[0] // semaphores.shape[0]
    places = [pl.ds(i * rows, rows) for i in range(semaphores.shape[0])]
    for copy in fetch([(source_ref.at[at], out_ref.at[at]) for at in places], semaphores):
        copy.wait()


def load(array):
    parts = 4 if array.shape[0] % 64 == 0 else 1
    return pl.pallas_call(
        load_kernel,
        out_shape=pltpu.VMEM(array.shape, array.dtype),
        in_specs=[HBM],
        out_specs=VMEM,
        scratch_shapes=[pltpu.SemaphoreType.DMA((parts,))],
        compiler_params=params(),
        cost_estimate=pl.CostEstimate(
            flops=0, bytes_accessed=2 * array.size * array.dtype.itemsize, transcendentals=0
        ),
    )(place_in(array, pltpu.HBM))


def split_dot(full, other, dims):
    high = full.astype(BF16)
    low = (full - high.astype(F32)).astype(BF16)
    return lax.dot_general(high, other, dims, preferred_element_type=F32) + lax.dot_general(
        low, other, dims, preferred_element_type=F32
    )


def triangle(size):
    rows = lax.broadcasted_iota(jnp.int32, (size, size), 0)
    return rows, lax.broadcasted_iota(jnp.int32, (size, size), 1)


def live_row(values_ref, counts_ref, b):
    row = values_ref[b : b + 1, :]
    points = lax.broadcasted_iota(jnp.int32, row.shape, 1)
    return jnp.where(points < counts_ref[b], row, 0.0)


def integrate_kernel(start, counts_hbm, basis_hbm, weights_hbm, full_ref, packed_ref, *scratch):
    diagonal, basis_ref, weights_ref, counts_ref, semaphores = scratch
    size = full_ref.shape[0]
    half = full_ref.shape[2] // 2
    row, column = triangle(half)
    cut = -(-size // 2)
    copies = [(counts_hbm, counts_ref), (weights_hbm, weights_ref)]
    for place in (pl.ds(0, cut), pl.ds(cut, size - cut)):
        copies.append((basis_hbm.at[pl.ds(start + place.start, place.size)], basis_ref.at[place]))
    waits = fetch(copies if cut < size else copies[:3], semaphores)
    diagonal[...] = jnp.zeros_like(diagonal)
    for b in range(size):
        if b == 0:
            for copy in waits[:3]:
                copy.wait()
        elif b == cut:
            waits[3].wait()
        values = basis_ref[b]
        weighted = values.astype(F32).T * live_row(weights_ref, counts_ref, start + b)
        ham = split_dot(weighted, values, (((1,), (0,)), ((), ())))
        full_ref[b] = ham.astype(BF16)
        last = ham[half:, half:]
        mixed = jnp.where(row >= column, ham[:half, :half], last)
        packed = jnp.concatenate([ham[:half, half:], mixed], axis=1)
        packed_ref[b * half : (b + 1) * half, :] = packed.astype(BF16)
        line = jnp.sum(jnp.where(row == column, last, 0.0), axis=0, keepdims=True)
        diagonal[b : b + 1, :] = jnp.concatenate([line, jnp.zeros_like(line)], axis=1)
    packed_ref[size * half :, :] = diagonal[...].astype(BF16)


def groups(nbatch):
    first = -(-nbatch // 2)
    return [first, nbatch - first] if nbatch > first else [first]


def padded_rows(nbatch):
    return -(-nbatch // 32) * 32


def integrate(basis_values, counts, weights, start, size):
    _, points, columns = basis_values.shape
    extra = padded_rows(size)
    return pl.pallas_call(
        functools.partial(integrate_kernel, start),
        out_shape=[
            pltpu.VMEM((size, columns, columns), BF16),
            jax.ShapeDtypeStruct((size * columns // 2 + extra, columns), BF16),
        ],
        in_specs=[HBM, HBM, HBM],
        out_specs=[VMEM, VMEM],
        scratch_shapes=[
            pltpu.VMEM((extra, columns), F32),
            pltpu.VMEM((size, points, columns), BF16),
            pltpu.VMEM(weights.shape, F32),
            pltpu.SMEM(counts.shape, jnp.int32),
            pltpu.SemaphoreType.DMA((4,)),
        ],
        compiler_params=params(6),
        cost_estimate=pl.CostEstimate(
            flops=4 * size * points * columns * columns,
            bytes_accessed=size * columns * (points * 2 + columns * 3),
            transcendentals=0,
        ),
    )(*[place_in(array, pltpu.HBM) for array in (counts, basis_values, weights)])


def unpack_kernel(packed_ref, full_ref, diagonal):
    nbatch = full_ref.shape[0]
    half = full_ref.shape[1] // 2
    row, column = triangle(half)
    diagonal[...] = packed_ref[nbatch * half :, :].astype(F32)

    def step(b, carry):
        packed = packed_ref[pl.ds(pl.multiple_of(b * half, half), half), :].astype(F32)
        turned = packed.T
        mixed, mixed_turned = packed[:, half:], turned[half:]
        first = jnp.where(row >= column, mixed, mixed_turned)
        last = jnp.where(row < column, mixed, mixed_turned)
        last = jnp.where(row == column, diagonal[pl.ds(b, 1), :][:, :half], last)
        upper = jnp.concatenate([first, packed[:, :half]], axis=1)
        lower = jnp.concatenate([turned[:half], last], axis=1)
        full_ref[b] = jnp.concatenate([upper, lower], axis=0).astype(BF16)
        return carry

    lax.fori_loop(0, nbatch, step, 0, unroll=4)


def unpack(packed, nbatch, columns):
    return pl.pallas_call(
        unpack_kernel,
        out_shape=jax.ShapeDtypeStruct((nbatch, columns, columns), BF16),
        in_specs=[VMEM],
        out_specs=VMEM,
        scratch_shapes=[pltpu.VMEM((padded_rows(nbatch), columns), F32)],
        compiler_params=params(),
        cost_estimate=pl.CostEstimate(
            flops=nbatch * columns * columns * 4,
            bytes_accessed=nbatch * columns * columns * 3,
            transcendentals=0,
        ),
    )(packed)


def row_places(block_ref, b, rows):
    return [
        pl.ds(pl.multiple_of(block_ref[b, j] * rows, rows), rows) for j in range(block_ref.shape[1])
    ]


def apply_kernel(starts, rows, *refs):
    pieces, lists = len(starts), len(refs) - len(starts) - 8
    block_refs, refs = refs[:lists] * (pieces // lists), refs[lists:]
    ham_refs, window_refs = refs[:pieces], refs[pieces : pieces + 3]
    out_before, out_own, out_after, window, total = refs[pieces + 3 :]
    region = window_refs[0].shape[0]
    for side, ref in enumerate(window_refs):
        window[side * region : (side + 1) * region] = ref[...]
    total[...] = jnp.zeros_like(total)

    def steps(members, count):
        def step(b, carry):
            places, products = [], []
            for p, first in members:
                place = row_places(block_refs[p], starts[p] + first + b, rows)
                picked = jnp.concatenate([window[at, :] for at in place], axis=0)
                products.append(jnp.dot(ham_refs[p][first + b], picked, preferred_element_type=F32))
                places.append(place)
            for place, product in zip(places, products):
                for j, at in enumerate(place):
                    total[at, :] += product[j * rows : (j + 1) * rows]
            return carry

        lax.fori_loop(0, count, step, 0, unroll=6)

    shares = {}
    smallest = min(ref.shape[0] for ref in ham_refs)
    for p, ref in enumerate(ham_refs):
        for first in range(0, ref.shape[0], smallest):
            count = min(smallest, ref.shape[0] - first)
            shares.setdefault(count, []).append((p, first))
    for count, members in shares.items():
        steps(members, count)
    out_before[...] = total[:region].astype(BF16)
    out_own[...] = total[region : 2 * region]
    out_after[...] = total[2 * region :].astype(BF16)


def apply_window(blocks, hams, starts, before, own, after):
    pieces, per_batch = len(hams), blocks[0].shape[1]
    columns = hams[0].shape[1]
    region, width = own.shape
    work = sum(ham.shape[0] for ham in hams)
    return pl.pallas_call(
        functools.partial(apply_kernel, starts, columns // per_batch),
        out_shape=[
            jax.ShapeDtypeStruct((region, width), BF16),
            jax.ShapeDtypeStruct((region, width), F32),
            jax.ShapeDtypeStruct((region, width), BF16),
        ],
        in_specs=[SMEM] * len(blocks) + [VMEM] * (pieces + 3),
        out_specs=[VMEM] * 3,
        scratch_shapes=[
            pltpu.VMEM((3 * region, width), BF16),
            pltpu.VMEM((3 * region, width), F32),
        ],
        compiler_params=params(6),
        cost_estimate=pl.CostEstimate(
            flops=2 * work * columns * columns * width,
            bytes_accessed=work * columns * columns * 2 + 14 * region * width,
            transcendentals=0,
        ),
    )(
        *blocks,
        *hams,
        *[place_in(array, pltpu.VMEM) for array in (before, own, after)],
    )


def expand_kernel(first_ref, part_ref, coming_ref, *refs):
    sources, (out_ref, held, semaphores) = refs[:2], refs[-3:]
    blocks = semaphores.shape[0] // 2
    rows = held.shape[1] // blocks
    copies = []
    for i in range(blocks):
        place = pl.ds(i * rows, rows)
        for share, source in enumerate(sources):
            copies.append((source.at[place], held.at[share, place]))
    waits = fetch(copies, semaphores)
    low = first_ref[0] == 0
    rotations = []
    for share in range(2):
        part, coming = part_ref[share], coming_ref[share]
        halves = [jnp.where(low, part, coming), jnp.where(low, coming, part)]
        rotations.append(jnp.concatenate(halves, axis=0))
    for i in range(blocks):
        at = slice(i * rows, (i + 1) * rows)
        total = None
        for share in range(2):
            waits[2 * i + share].wait()
            product = lax.dot_general(
                held[share, at], rotations[share], NT, preferred_element_type=F32
            )
            total = product if total is None else total + product
        out_ref[at] = total.astype(out_ref.dtype)


def expand(first, part, coming, virtuals, kind, ahead):
    region, virt = virtuals[0].shape
    width = 2 * part.shape[1]
    blocks = 4 if region % 64 == 0 and region > 64 else 1
    return pl.pallas_call(
        expand_kernel,
        out_shape=jax.ShapeDtypeStruct((region, width), kind),
        in_specs=[SMEM, VMEM, VMEM, HBM, HBM] + [HBM] * len(ahead),
        out_specs=VMEM,
        scratch_shapes=[
            pltpu.VMEM((2, region, virt), BF16),
            pltpu.SemaphoreType.DMA((2 * blocks,)),
        ],
        compiler_params=params(14),
        cost_estimate=pl.CostEstimate(
            flops=4 * region * width * virt if kind == BF16 else 0,
            bytes_accessed=4 * region * virt if kind == BF16 else 0,
            transcendentals=0,
        ),
    )(first.reshape(1), part, coming, place_in(virtuals[0], pltpu.HBM), virtuals[1], *ahead)


def overlap_steps(block_ref, occ_ref, resp_ref, out_ref, rows):
    def step(b, carry):
        place = row_places(block_ref, b, rows)
        left = jnp.concatenate([resp_ref[at, :] for at in place], axis=0)
        right = jnp.concatenate([occ_ref[at, :] for at in place], axis=0)
        product = lax.dot_general(left, right, NT, preferred_element_type=F32)
        out_ref[b] = product.astype(out_ref.dtype)
        return carry

    lax.fori_loop(0, out_ref.shape[0], step, 0, unroll=8)


def gather_kernel(rows, block_ref, *refs):
    sources, (out_ref, occ_ref, resp_ref, semaphores) = refs[:12], refs[12:]
    region, width = sources[0].shape
    copies = []
    for i, source in enumerate(sources):
        target, side, part = (occ_ref, resp_ref)[i // 6], i % 6 // 2, i % 2
        place = (pl.ds(side * region, region), pl.ds(part * width, width))
        copies.append((source, target.at[place]))
    for copy in fetch(copies, semaphores):
        copy.wait()
    overlap_steps(block_ref, occ_ref, resp_ref, out_ref, rows)


def gather_overlaps(blocks, columns, occ_parts, resp_parts):
    nbatch, per_batch = blocks.shape
    region, width = occ_parts[0].shape
    return pl.pallas_call(
        functools.partial(gather_kernel, columns // per_batch),
        out_shape=[jax.ShapeDtypeStruct((nbatch, columns, columns), BF16)]
        + [pltpu.VMEM((3 * region, 2 * width), BF16)] * 2,
        in_specs=[SMEM] + [HBM] * 12,
        out_specs=[VMEM] * 3,
        scratch_shapes=[pltpu.SemaphoreType.DMA((12,))],
        compiler_params=params(),
        cost_estimate=pl.CostEstimate(
            flops=4 * nbatch * columns * columns * width,
            bytes_accessed=24 * region * width + nbatch * columns * columns * 2,
            transcendentals=0,
        ),
    )(blocks, *occ_parts, *resp_parts)


def overlap_kernel(rows, block_ref, occ_ref, resp_ref, out_ref):
    overlap_steps(block_ref, occ_ref, resp_ref, out_ref, rows)


def overlaps(blocks, columns, occ_window, resp_window):
    nbatch, per_batch = blocks.shape
    return pl.pallas_call(
        functools.partial(overlap_kernel, columns // per_batch),
        out_shape=pltpu.VMEM((nbatch, columns, columns), F32),
        in_specs=[SMEM, VMEM, VMEM],
        out_specs=VMEM,
        compiler_params=params(),
        cost_estimate=pl.CostEstimate(
            flops=2 * nbatch * columns * columns * occ_window.shape[1],
            bytes_accessed=nbatch * columns * columns * 4,
            transcendentals=0,
        ),
    )(blocks, place_in(occ_window, pltpu.VMEM), place_in(resp_window, pltpu.VMEM))


def density_kernel(
    core_ref, basis_ref, first_ref, second_ref, scale_ref, half_ref, near_ref,
    out_ref, coef_ref, semaphores,
):
    width = half_ref.shape[1]
    copies = []
    for source, place in ((half_ref, core_ref[0]), (near_ref, 1 - core_ref[0])):
        columns = pl.ds(pl.multiple_of(place * width, width), width)
        copies.append((source, coef_ref.at[:, columns]))
    waits = fetch(copies, semaphores)
    for b in range(basis_ref.shape[0]):
        values = basis_ref[b]
        overlap = first_ref[b] + second_ref[b].astype(F32)
        product = split_dot(overlap, values, NT)
        density = jnp.sum(product * values.astype(F32).T, axis=0, keepdims=True)
        out_ref[b : b + 1, :] = scale_ref[b : b + 1, :] * density
    for copy in waits:
        copy.wait()


def density(core, basis_values, first, second, scale, half, half_near):
    nbatch, points, columns = basis_values.shape
    region, width = half.shape
    return pl.pallas_call(
        density_kernel,
        out_shape=[
            jax.ShapeDtypeStruct((nbatch, points), F32),
            jax.ShapeDtypeStruct((region, 2 * width), BF16),
        ],
        in_specs=[SMEM] + [VMEM] * 4 + [HBM] * 2,
        out_specs=[VMEM, HBM],
        scratch_shapes=[pltpu.SemaphoreType.DMA((2,))],
        compiler_params=params(),
        cost_estimate=pl.CostEstimate(
            flops=4 * nbatch * points * columns * columns,
            bytes_accessed=basis_values.size * 2 + nbatch * columns * columns * 6,
            transcendentals=0,
        ),
    )(core.reshape(1), basis_values, place_in(first, pltpu.VMEM), second, scale, half, half_near)


def flip(array, axis, mask):
    return lax.ppermute(array, axis, [(i, i ^ mask) for i in range(lax.axis_size(axis))])


def neighbours(array):
    size = lax.axis_size("grid")
    before = lax.ppermute(array, "grid", [(i, (i + 1) % size) for i in range(size)])
    after = lax.ppermute(array, "grid", [((i + 1) % size, i) for i in range(size)])
    return before, after


def column_part(array, index, width):
    return lax.dynamic_slice_in_dim(array, index * width, width, 1)


def trade(array, rows, choice):
    keep = lax.dynamic_slice_in_dim(array, choice * rows, rows, 1)
    return keep, lax.dynamic_slice_in_dim(array, (1 - choice) * rows, rows, 1).astype(BF16)


def join(own, other, choice):
    low, high = jnp.where(choice == 0, own, other), jnp.where(choice == 0, other, own)
    return jnp.concatenate([low, high], axis=1)


def swap(array, masks):
    size, tiles = lax.axis_size("grid"), lax.axis_size("tile")
    pairs = [
        (g * tiles + t, (g ^ masks[t % 2]) * tiles + t) for g in range(size) for t in range(tiles)
    ]
    return lax.ppermute(array, ("grid", "tile"), pairs)


def together(*arrays):
    return lax.optimization_barrier(arrays)


def divide_kernel(place_ref, energy_ref, *refs):
    chunks = len(refs) // 4
    rows = refs[0].shape[1]
    place = pl.multiple_of(place_ref[0], rows)
    for c in range(chunks):
        total_ref, coming_ref, level_ref, out_ref = refs[3 * c : 3 * c + 3] + (refs[3 * chunks + c],)
        level = level_ref[pl.ds(place, rows), :]
        for share in range(total_ref.shape[0]):
            total = total_ref[share] + coming_ref[share].astype(F32)
            gap = level - energy_ref[share : share + 1, :]
            out_ref[share] = (total / gap).astype(out_ref.dtype)


def divide(place, energies, chunks):
    shape = chunks[0].total.shape
    operands = []
    for chunk in chunks:
        operands += [chunk.total, chunk.coming, chunk.level[:, None]]
    return pl.pallas_call(
        divide_kernel,
        out_shape=[pltpu.VMEM(shape, BF16)] * len(chunks),
        in_specs=[SMEM] + [VMEM] * (1 + len(operands)),
        out_specs=[VMEM] * len(chunks),
        compiler_params=params(),
        cost_estimate=pl.CostEstimate(
            flops=len(chunks) * math.prod(shape) * 8, bytes_accessed=0, transcendentals=0
        ),
    )(place.reshape(1), energies, *operands)


class Reduction:
    def __init__(self, part, level):
        grid, core = lax.axis_index("grid"), lax.axis_index("tile") % 2
        self.masks = (1, 2), (2, 1)
        self.first, self.second = (grid >> core) & 1, (grid >> (1 - core)) & 1
        self.level = level
        self.half = part.shape[1] // 2
        self.keep, send = trade(part, self.half, self.first)
        self.coming = swap(send, self.masks[0])

    def narrow(self):
        total = self.keep + self.coming.astype(F32)
        self.keep, send = trade(total, self.half // 2, self.second)
        self.total = self.keep + swap(send, self.masks[1]).astype(F32)
        self.total, self.across = together(self.total, self.total.astype(BF16))

    def cross(self):
        self.coming = flip(self.across, "grid", 4)

    def place(self):
        return self.first * self.half + self.second * (self.half // 2)

    def widen(self, own):
        self.part = join(own, swap(own, self.masks[1]), self.second)
        self.coming = swap(self.part, self.masks[0])

    def result(self, virtuals, kind, *ahead):
        return expand(self.first, self.part, self.coming, virtuals, kind, ahead)


def per_device(
    basis_values,
    blocks,
    counts,
    weighted_potential,
    xc_kernel,
    occ_coef,
    virt_coef,
    occ_energy,
    virt_energy,
):
    nbatch, _, columns = basis_values.shape
    region, occ_count = occ_coef.shape
    width = occ_count // lax.axis_size("tile")
    tile = lax.axis_index("tile")
    chip, core = tile // 2, tile % 2
    quarter = 2 * core + chip

    occ_own = column_part(occ_coef, quarter, width)

    lists = [blocks, flip(blocks, "tile", 1), flip(blocks, "tile", 2)]
    occ_before, occ_after = neighbours(occ_own)
    sizes, fulls, arrived = groups(nbatch), [], []
    for i, size in enumerate(sizes):
        full, packed = integrate(basis_values, counts, weighted_potential, sum(sizes[:i]), size)
        fulls.append(full)
        arrived.append(flip(packed, "tile", 2))
    arrived[0], occ_before, occ_after = together(arrived[0], occ_before, occ_after)
    far = [unpack(array, size, columns) for array, size in zip(arrived, sizes)]
    far[0], lists[2] = together(far[0], lists[2])
    lists.append(flip(lists[2], "tile", 1))
    hams = []
    for full, other in zip(fulls, far):
        hams += [full, flip(full, "tile", 1), other, flip(other, "tile", 1)]
    blocks_near = lists[1]
    starts = [sum(sizes[:i]) for i in range(len(sizes)) for _ in range(4)]
    virtuals = [virt_coef, flip(virt_coef, "tile", 1)]
    energies = jnp.stack([virt_energy, flip(virt_energy, "tile", 1)])

    to_before, own_sum, to_after = apply_window(
        lists,
        hams,
        starts,
        occ_before,
        occ_own,
        occ_after,
    )
    levels = [
        lax.dynamic_slice_in_dim(occ_energy, place * width, width, 0)
        for place in (quarter, quarter ^ 1)
    ]
    loaded = [load(array) for array in virtuals]
    points = lax.broadcasted_iota(jnp.int32, xc_kernel.shape, 1)
    scale = jnp.where(points < counts[:, None], 4.0 * xc_kernel, 0.0)
    own_sum, energies, levels, loaded, scale = together(own_sum, energies, levels, loaded, scale)
    size = lax.axis_size("grid")
    from_before = lax.ppermute(to_after, "grid", [(i, (i + 1) % size) for i in range(size)])
    from_after = lax.ppermute(to_before, "grid", [((i + 1) % size, i) for i in range(size)])
    ham_own = (own_sum + from_before.astype(F32) + from_after.astype(F32)).astype(BF16)

    def products(ham_sum):
        dots = [
            lax.dot_general(ham_sum, virt, (((0,), (0,)), ((), ())), preferred_element_type=F32)
            for virt in loaded
        ]
        return jnp.stack(dots)

    own_part, far_part = products(ham_own), products(flip(ham_own, "tile", 2))
    occ_far = column_part(occ_coef, quarter ^ 1, width)
    if lax.axis_size("grid") == 8:
        own = Reduction(own_part, levels[0])
        far = Reduction(far_part, levels[1])
        own.narrow()
        far.narrow()
        far.cross()
        own.across, occ_before, occ_after = together(own.across, occ_before, occ_after)
        own.cross()
        before_far, after_far = flip(occ_before, "tile", 2), flip(occ_after, "tile", 2)
        own.coming, before_far, after_far = together(own.coming, before_far, after_far)
        own_rotation, far_rotation = divide(own.place(), energies, [own, far])
        own.widen(own_rotation)
        far.widen(far_rotation)
        coef_far = far.result(virtuals, BF16)
        coef_own = own.result(virtuals, F32, coef_far)
    else:
        before_far, after_far = flip(occ_before, "tile", 2), flip(occ_after, "tile", 2)
        coefs = []
        for part, level in ((own_part, levels[0]), (far_part, levels[1])):
            total = lax.psum(part, "grid")
            rotation = (total / (level[None, :, None] - energies[:, None, :])).astype(BF16)
            terms = [
                lax.dot_general(virt, rotation[i], NT, preferred_element_type=F32)
                for i, virt in enumerate(virtuals)
            ]
            coefs.append(terms[0] + terms[1])
        coef_own, coef_far = coefs[0], coefs[1].astype(BF16)
    coef_own, coef_far = together(coef_own, flip(coef_far, "tile", 2))
    resp_own = (coef_own + coef_far.astype(F32)).astype(BF16)

    resp_before, resp_after = neighbours(resp_own)
    resp_before_far = flip(resp_before, "tile", 2)
    resp_far, resp_after = together(flip(resp_own, "tile", 2), resp_after)
    resp_after_far = flip(resp_after, "tile", 2)
    first = chip == 0
    half = jnp.concatenate(
        [jnp.where(first, resp_own, resp_far), jnp.where(first, resp_far, resp_own)], axis=1
    )
    overlap_near, occ_window, resp_window = gather_overlaps(
        blocks_near,
        columns,
        [occ_before, before_far, occ_own, occ_far, occ_after, after_far],
        [resp_before, resp_before_far, resp_own, resp_far, resp_after, resp_after_far],
    )
    response_potential, response_coef = density(
        core,
        basis_values,
        overlaps(blocks, columns, occ_window, resp_window),
        flip(overlap_near, "tile", 1),
        scale,
        half,
        flip(half, "tile", 1),
    )
    return (response_coef, response_potential)


def solution(mesh):
    in_specs = (
        P(("grid", "tile"), None, None),
        P(("grid", "tile"), None),
        P(("grid", "tile")),
        P(("grid", "tile"), None),
        P(("grid", "tile"), None),
        P("grid", None),
        P("grid", "tile"),
        P(),
        P("tile"),
    )
    out_specs = (P("grid", None), P(("grid", "tile"), None))
    return jax.shard_map(
        per_device, mesh=mesh, in_specs=in_specs, out_specs=out_specs, check_vma=False
    )
```

```python
import functools
import math

import jax
import jax.numpy as jnp
from jax import lax
from jax.experimental import pallas as pl
from jax.experimental.pallas import tpu as pltpu
from jax.sharding import PartitionSpec as P

VMEM = pl.BlockSpec(memory_space=pltpu.VMEM)
SMEM = pl.BlockSpec(memory_space=pltpu.SMEM)
HBM = pl.BlockSpec(memory_space=pl.ANY)
MIB = 1024 * 1024
F32 = jnp.float32
BF16 = jnp.bfloat16
NT = (((1,), (1,)), ((), ()))


def params(mib=4):
    return pltpu.CompilerParams(vmem_limit_bytes=mib * MIB)


def place_in(array, space):
    return pltpu.with_memory_space_constraint(array, space)


def fetch(copies, semaphores):
    started = [
        pltpu.make_async_copy(source, target, semaphores.at[i])
        for i, (source, target) in enumerate(copies)
    ]
    for copy in started:
        copy.start()
    return started


def load_kernel(source_ref, out_ref, semaphores):
    rows = source_ref.shape[0] // semaphores.shape[0]
    places = [pl.ds(i * rows, rows) for i in range(semaphores.shape[0])]
    for copy in fetch([(source_ref.at[at], out_ref.at[at]) for at in places], semaphores):
        copy.wait()


def load(array):
    parts = 4 if array.shape[0] % 64 == 0 else 1
    return pl.pallas_call(
        load_kernel,
        out_shape=pltpu.VMEM(array.shape, array.dtype),
        in_specs=[HBM],
        out_specs=VMEM,
        scratch_shapes=[pltpu.SemaphoreType.DMA((parts,))],
        compiler_params=params(),
        cost_estimate=pl.CostEstimate(
            flops=0, bytes_accessed=2 * array.size * array.dtype.itemsize, transcendentals=0
        ),
    )(place_in(array, pltpu.HBM))


def split_dot(full, other, dims):
    high = full.astype(BF16)
    low = (full - high.astype(F32)).astype(BF16)
    return lax.dot_general(high, other, dims, preferred_element_type=F32) + lax.dot_general(
        low, other, dims, preferred_element_type=F32
    )


def triangle(size):
    rows = lax.broadcasted_iota(jnp.int32, (size, size), 0)
    return rows, lax.broadcasted_iota(jnp.int32, (size, size), 1)


def live_row(values_ref, counts_ref, b):
    row = values_ref[b : b + 1, :]
    points = lax.broadcasted_iota(jnp.int32, row.shape, 1)
    return jnp.where(points < counts_ref[b], row, 0.0)


def integrate_kernel(start, counts_hbm, basis_hbm, weights_hbm, full_ref, packed_ref, *scratch):
    diagonal, basis_ref, weights_ref, counts_ref, semaphores = scratch
    size = full_ref.shape[0]
    half = full_ref.shape[2] // 2
    row, column = triangle(half)
    cut = -(-size // 2)
    copies = [(counts_hbm, counts_ref), (weights_hbm, weights_ref)]
    for place in (pl.ds(0, cut), pl.ds(cut, size - cut)):
        copies.append((basis_hbm.at[pl.ds(start + place.start, place.size)], basis_ref.at[place]))
    waits = fetch(copies if cut < size else copies[:3], semaphores)
    diagonal[...] = jnp.zeros_like(diagonal)
    for b in range(size):
        if b == 0:
            for copy in waits[:3]:
                copy.wait()
        elif b == cut:
            waits[3].wait()
        values = basis_ref[b]
        weighted = values.astype(F32).T * live_row(weights_ref, counts_ref, start + b)
        ham = split_dot(weighted, values, (((1,), (0,)), ((), ())))
        full_ref[b] = ham.astype(BF16)
        last = ham[half:, half:]
        mixed = jnp.where(row >= column, ham[:half, :half], last)
        packed = jnp.concatenate([ham[:half, half:], mixed], axis=1)
        packed_ref[b * half : (b + 1) * half, :] = packed.astype(BF16)
        line = jnp.sum(jnp.where(row == column, last, 0.0), axis=0, keepdims=True)
        diagonal[b : b + 1, :] = jnp.concatenate([line, jnp.zeros_like(line)], axis=1)
    packed_ref[size * half :, :] = diagonal[...].astype(BF16)


def groups(nbatch):
    first = -(-nbatch // 2)
    return [first, nbatch - first] if nbatch > first else [first]


def padded_rows(nbatch):
    return -(-nbatch // 32) * 32


def integrate(basis_values, counts, weights, start, size):
    _, points, columns = basis_values.shape
    extra = padded_rows(size)
    return pl.pallas_call(
        functools.partial(integrate_kernel, start),
        out_shape=[
            pltpu.VMEM((size, columns, columns), BF16),
            jax.ShapeDtypeStruct((size * columns // 2 + extra, columns), BF16),
        ],
        in_specs=[HBM, HBM, HBM],
        out_specs=[VMEM, VMEM],
        scratch_shapes=[
            pltpu.VMEM((extra, columns), F32),
            pltpu.VMEM((size, points, columns), BF16),
            pltpu.VMEM(weights.shape, F32),
            pltpu.SMEM(counts.shape, jnp.int32),
            pltpu.SemaphoreType.DMA((4,)),
        ],
        compiler_params=params(6),
        cost_estimate=pl.CostEstimate(
            flops=4 * size * points * columns * columns,
            bytes_accessed=size * columns * (points * 2 + columns * 3),
            transcendentals=0,
        ),
    )(*[place_in(array, pltpu.HBM) for array in (counts, basis_values, weights)])


def unpack_kernel(packed_ref, full_ref, diagonal):
    nbatch = full_ref.shape[0]
    half = full_ref.shape[1] // 2
    row, column = triangle(half)
    diagonal[...] = packed_ref[nbatch * half :, :].astype(F32)

    def step(b, carry):
        packed = packed_ref[pl.ds(pl.multiple_of(b * half, half), half), :].astype(F32)
        turned = packed.T
        mixed, mixed_turned = packed[:, half:], turned[half:]
        first = jnp.where(row >= column, mixed, mixed_turned)
        last = jnp.where(row < column, mixed, mixed_turned)
        last = jnp.where(row == column, diagonal[pl.ds(b, 1), :][:, :half], last)
        upper = jnp.concatenate([first, packed[:, :half]], axis=1)
        lower = jnp.concatenate([turned[:half], last], axis=1)
        full_ref[b] = jnp.concatenate([upper, lower], axis=0).astype(BF16)
        return carry

    lax.fori_loop(0, nbatch, step, 0, unroll=4)


def unpack(packed, nbatch, columns):
    return pl.pallas_call(
        unpack_kernel,
        out_shape=jax.ShapeDtypeStruct((nbatch, columns, columns), BF16),
        in_specs=[VMEM],
        out_specs=VMEM,
        scratch_shapes=[pltpu.VMEM((padded_rows(nbatch), columns), F32)],
        compiler_params=params(),
        cost_estimate=pl.CostEstimate(
            flops=nbatch * columns * columns * 4,
            bytes_accessed=nbatch * columns * columns * 3,
            transcendentals=0,
        ),
    )(packed)


def row_places(block_ref, b, rows):
    return [
        pl.ds(pl.multiple_of(block_ref[b, j] * rows, rows), rows) for j in range(block_ref.shape[1])
    ]


def apply_kernel(starts, rows, *refs):
    pieces, lists = len(starts), len(refs) - len(starts) - 8
    block_refs, refs = refs[:lists] * (pieces // lists), refs[lists:]
    ham_refs, window_refs = refs[:pieces], refs[pieces : pieces + 3]
    out_before, out_own, out_after, window, total = refs[pieces + 3 :]
    region = window_refs[0].shape[0]
    for side, ref in enumerate(window_refs):
        window[side * region : (side + 1) * region] = ref[...]
    total[...] = jnp.zeros_like(total)

    def steps(members, count):
        def step(b, carry):
            places, products = [], []
            for p, first in members:
                place = row_places(block_refs[p], starts[p] + first + b, rows)
                picked = jnp.concatenate([window[at, :] for at in place], axis=0)
                products.append(jnp.dot(ham_refs[p][first + b], picked, preferred_element_type=F32))
                places.append(place)
            for place, product in zip(places, products):
                for j, at in enumerate(place):
                    total[at, :] += product[j * rows : (j + 1) * rows]
            return carry

        lax.fori_loop(0, count, step, 0, unroll=12)

    shares = {}
    smallest = min(ref.shape[0] for ref in ham_refs)
    for p, ref in enumerate(ham_refs):
        for first in range(0, ref.shape[0], smallest):
            count = min(smallest, ref.shape[0] - first)
            shares.setdefault(count, []).append((p, first))
    for count, members in shares.items():
        steps(members, count)
    out_before[...] = total[:region].astype(BF16)
    out_own[...] = total[region : 2 * region]
    out_after[...] = total[2 * region :].astype(BF16)


def apply_window(blocks, hams, starts, before, own, after):
    pieces, per_batch = len(hams), blocks[0].shape[1]
    columns = hams[0].shape[1]
    region, width = own.shape
    work = sum(ham.shape[0] for ham in hams)
    return pl.pallas_call(
        functools.partial(apply_kernel, starts, columns // per_batch),
        out_shape=[
            jax.ShapeDtypeStruct((region, width), BF16),
            jax.ShapeDtypeStruct((region, width), F32),
            jax.ShapeDtypeStruct((region, width), BF16),
        ],
        in_specs=[SMEM] * len(blocks) + [VMEM] * (pieces + 3),
        out_specs=[VMEM] * 3,
        scratch_shapes=[
            pltpu.VMEM((3 * region, width), BF16),
            pltpu.VMEM((3 * region, width), F32),
        ],
        compiler_params=params(6),
        cost_estimate=pl.CostEstimate(
            flops=2 * work * columns * columns * width,
            bytes_accessed=work * columns * columns * 2 + 14 * region * width,
            transcendentals=0,
        ),
    )(
        *blocks,
        *hams,
        *[place_in(array, pltpu.VMEM) for array in (before, own, after)],
    )


def expand_kernel(fetched, first_ref, part_ref, coming_ref, *refs):
    sources, (out_ref, held, semaphores) = refs[:2], refs[-3:]
    blocks = semaphores.shape[0] // fetched
    rows = held.shape[1] // blocks
    copies = []
    for i in range(blocks):
        place = pl.ds(i * rows, rows)
        for share in range(fetched):
            copies.append((sources[share].at[place], held.at[share, place]))
    waits = fetch(copies, semaphores)
    places = [held.at[share] if share < fetched else sources[share] for share in range(2)]
    low = first_ref[0] == 0
    rotations = []
    for share in range(2):
        part, coming = part_ref[share], coming_ref[share]
        halves = [jnp.where(low, part, coming), jnp.where(low, coming, part)]
        rotations.append(jnp.concatenate(halves, axis=0))
    for i in range(blocks):
        at = slice(i * rows, (i + 1) * rows)
        total = None
        for share in reversed(range(2)):
            if share < fetched:
                waits[fetched * i + share].wait()
            product = lax.dot_general(
                places[share][at], rotations[share], NT, preferred_element_type=F32
            )
            total = product if total is None else total + product
        out_ref[at] = total.astype(out_ref.dtype)


def expand(first, part, coming, virtuals, kind, ahead, fetched):
    region, virt = virtuals[0].shape
    width = 2 * part.shape[1]
    blocks = 4 if region % 64 == 0 and region > 64 else 1
    near = virtuals[1] if fetched == 2 else place_in(virtuals[1], pltpu.VMEM)
    return pl.pallas_call(
        functools.partial(expand_kernel, fetched),
        out_shape=jax.ShapeDtypeStruct((region, width), kind),
        in_specs=[SMEM, VMEM, VMEM, HBM, HBM if fetched == 2 else VMEM] + [HBM] * len(ahead),
        out_specs=VMEM,
        scratch_shapes=[
            pltpu.VMEM((fetched, region, virt), BF16),
            pltpu.SemaphoreType.DMA((fetched * blocks,)),
        ],
        compiler_params=params(6 + 4 * fetched),
        cost_estimate=pl.CostEstimate(
            flops=4 * region * width * virt if kind == BF16 else 0,
            bytes_accessed=4 * region * virt if kind == BF16 else 0,
            transcendentals=0,
        ),
    )(first.reshape(1), part, coming, place_in(virtuals[0], pltpu.HBM), near, *ahead)


def overlap_steps(block_ref, occ_ref, resp_ref, out_ref, rows):
    def step(b, carry):
        place = row_places(block_ref, b, rows)
        left = jnp.concatenate([resp_ref[at, :] for at in place], axis=0)
        right = jnp.concatenate([occ_ref[at, :] for at in place], axis=0)
        product = lax.dot_general(left, right, NT, preferred_element_type=F32)
        out_ref[b] = product.astype(out_ref.dtype)
        return carry

    lax.fori_loop(0, out_ref.shape[0], step, 0, unroll=24)


def gather_kernel(rows, block_ref, *refs):
    sources, (out_ref, occ_ref, resp_ref, semaphores) = refs[:12], refs[12:]
    region, width = sources[0].shape
    copies = []
    for i, source in enumerate(sources):
        target, side, part = (occ_ref, resp_ref)[i // 6], i % 6 // 2, i % 2
        place = (pl.ds(side * region, region), pl.ds(part * width, width))
        copies.append((source, target.at[place]))
    for copy in fetch(copies, semaphores):
        copy.wait()
    overlap_steps(block_ref, occ_ref, resp_ref, out_ref, rows)


def gather_overlaps(blocks, columns, occ_parts, resp_parts):
    nbatch, per_batch = blocks.shape
    region, width = occ_parts[0].shape
    return pl.pallas_call(
        functools.partial(gather_kernel, columns // per_batch),
        out_shape=[jax.ShapeDtypeStruct((nbatch, columns, columns), BF16)]
        + [pltpu.VMEM((3 * region, 2 * width), BF16)] * 2,
        in_specs=[SMEM] + [HBM] * 12,
        out_specs=[VMEM] * 3,
        scratch_shapes=[pltpu.SemaphoreType.DMA((12,))],
        compiler_params=params(),
        cost_estimate=pl.CostEstimate(
            flops=4 * nbatch * columns * columns * width,
            bytes_accessed=24 * region * width + nbatch * columns * columns * 2,
            transcendentals=0,
        ),
    )(blocks, *occ_parts, *resp_parts)


def overlap_kernel(rows, block_ref, occ_ref, resp_ref, out_ref):
    overlap_steps(block_ref, occ_ref, resp_ref, out_ref, rows)


def overlaps(blocks, columns, occ_window, resp_window):
    nbatch, per_batch = blocks.shape
    return pl.pallas_call(
        functools.partial(overlap_kernel, columns // per_batch),
        out_shape=pltpu.VMEM((nbatch, columns, columns), F32),
        in_specs=[SMEM, VMEM, VMEM],
        out_specs=VMEM,
        compiler_params=params(),
        cost_estimate=pl.CostEstimate(
            flops=2 * nbatch * columns * columns * occ_window.shape[1],
            bytes_accessed=nbatch * columns * columns * 4,
            transcendentals=0,
        ),
    )(blocks, place_in(occ_window, pltpu.VMEM), place_in(resp_window, pltpu.VMEM))


def density_kernel(
    core_ref, basis_ref, first_ref, second_ref, scale_ref, half_ref, near_ref,
    out_ref, coef_ref, semaphores,
):
    width = half_ref.shape[1]
    copies = []
    for source, place in ((half_ref, core_ref[0]), (near_ref, 1 - core_ref[0])):
        columns = pl.ds(pl.multiple_of(place * width, width), width)
        copies.append((source, coef_ref.at[:, columns]))
    waits = fetch(copies, semaphores)
    for b in range(basis_ref.shape[0]):
        values = basis_ref[b]
        overlap = first_ref[b] + second_ref[b].astype(F32)
        product = split_dot(overlap, values, NT)
        density = jnp.sum(product * values.astype(F32).T, axis=0, keepdims=True)
        out_ref[b : b + 1, :] = scale_ref[b : b + 1, :] * density
    for copy in waits:
        copy.wait()


def density(core, basis_values, first, second, scale, half, half_near):
    nbatch, points, columns = basis_values.shape
    region, width = half.shape
    return pl.pallas_call(
        density_kernel,
        out_shape=[
            jax.ShapeDtypeStruct((nbatch, points), F32),
            jax.ShapeDtypeStruct((region, 2 * width), BF16),
        ],
        in_specs=[SMEM] + [VMEM] * 4 + [HBM] * 2,
        out_specs=[VMEM, HBM],
        scratch_shapes=[pltpu.SemaphoreType.DMA((2,))],
        compiler_params=params(),
        cost_estimate=pl.CostEstimate(
            flops=4 * nbatch * points * columns * columns,
            bytes_accessed=basis_values.size * 2 + nbatch * columns * columns * 6,
            transcendentals=0,
        ),
    )(core.reshape(1), basis_values, place_in(first, pltpu.VMEM), second, scale, half, half_near)


def flip(array, axis, mask):
    return lax.ppermute(array, axis, [(i, i ^ mask) for i in range(lax.axis_size(axis))])


def neighbours(array):
    size = lax.axis_size("grid")
    before = lax.ppermute(array, "grid", [(i, (i + 1) % size) for i in range(size)])
    after = lax.ppermute(array, "grid", [((i + 1) % size, i) for i in range(size)])
    return before, after


def column_part(array, index, width):
    return lax.dynamic_slice_in_dim(array, index * width, width, 1)


def trade(array, rows, choice):
    keep = lax.dynamic_slice_in_dim(array, choice * rows, rows, 1)
    return keep, lax.dynamic_slice_in_dim(array, (1 - choice) * rows, rows, 1).astype(BF16)


def join(own, other, choice):
    low, high = jnp.where(choice == 0, own, other), jnp.where(choice == 0, other, own)
    return jnp.concatenate([low, high], axis=1)


def swap(array, masks):
    size, tiles = lax.axis_size("grid"), lax.axis_size("tile")
    pairs = [
        (g * tiles + t, (g ^ masks[t % 2]) * tiles + t) for g in range(size) for t in range(tiles)
    ]
    return lax.ppermute(array, ("grid", "tile"), pairs)


def together(*arrays):
    return lax.optimization_barrier(arrays)


def divide_kernel(place_ref, energy_ref, *refs):
    chunks = len(refs) // 4
    rows = refs[0].shape[1]
    place = pl.multiple_of(place_ref[0], rows)
    for c in range(chunks):
        total_ref, coming_ref, level_ref, out_ref = refs[3 * c : 3 * c + 3] + (refs[3 * chunks + c],)
        level = level_ref[pl.ds(place, rows), :]
        for share in range(total_ref.shape[0]):
            total = total_ref[share] + coming_ref[share].astype(F32)
            gap = level - energy_ref[share : share + 1, :]
            out_ref[share] = (total / gap).astype(out_ref.dtype)


def divide(place, energies, chunks):
    shape = chunks[0].total.shape
    operands = []
    for chunk in chunks:
        operands += [chunk.total, chunk.coming, chunk.level[:, None]]
    return pl.pallas_call(
        divide_kernel,
        out_shape=[pltpu.VMEM(shape, BF16)] * len(chunks),
        in_specs=[SMEM] + [VMEM] * (1 + len(operands)),
        out_specs=[VMEM] * len(chunks),
        compiler_params=params(),
        cost_estimate=pl.CostEstimate(
            flops=len(chunks) * math.prod(shape) * 8, bytes_accessed=0, transcendentals=0
        ),
    )(place.reshape(1), energies, *operands)


class Reduction:
    def __init__(self, part, level):
        grid, core = lax.axis_index("grid"), lax.axis_index("tile") % 2
        self.masks = (1, 2), (2, 1)
        self.first, self.second = (grid >> core) & 1, (grid >> (1 - core)) & 1
        self.level = level
        self.half = part.shape[1] // 2
        self.keep, send = trade(part, self.half, self.first)
        self.coming = swap(send, self.masks[0])

    def narrow(self):
        total = self.keep + self.coming.astype(F32)
        self.keep, send = trade(total, self.half // 2, self.second)
        self.total = self.keep + swap(send, self.masks[1]).astype(F32)
        self.total, self.across = together(self.total, self.total.astype(BF16))

    def cross(self):
        self.coming = flip(self.across, "grid", 4)

    def place(self):
        return self.first * self.half + self.second * (self.half // 2)

    def widen(self, own):
        self.part = join(own, swap(own, self.masks[1]), self.second)
        self.coming = swap(self.part, self.masks[0])

    def result(self, virtuals, kind, *ahead, fetched=2):
        return expand(self.first, self.part, self.coming, virtuals, kind, ahead, fetched)


def per_device(
    basis_values,
    blocks,
    counts,
    weighted_potential,
    xc_kernel,
    occ_coef,
    virt_coef,
    occ_energy,
    virt_energy,
):
    nbatch, _, columns = basis_values.shape
    region, occ_count = occ_coef.shape
    width = occ_count // lax.axis_size("tile")
    tile = lax.axis_index("tile")
    chip, core = tile // 2, tile % 2
    quarter = 2 * core + chip

    occ_own = column_part(occ_coef, quarter, width)

    lists = [blocks, flip(blocks, "tile", 1), flip(blocks, "tile", 2)]
    occ_before, occ_after = neighbours(occ_own)
    sizes, fulls, arrived = groups(nbatch), [], []
    for i, size in enumerate(sizes):
        full, packed = integrate(basis_values, counts, weighted_potential, sum(sizes[:i]), size)
        fulls.append(full)
        arrived.append(flip(packed, "tile", 2))
    arrived[0], occ_before, occ_after = together(arrived[0], occ_before, occ_after)
    far = [unpack(array, size, columns) for array, size in zip(arrived, sizes)]
    far[0], lists[2] = together(far[0], lists[2])
    lists.append(flip(lists[2], "tile", 1))
    hams = []
    for full, other in zip(fulls, far):
        hams += [full, flip(full, "tile", 1), other, flip(other, "tile", 1)]
    blocks_near = lists[1]
    starts = [sum(sizes[:i]) for i in range(len(sizes)) for _ in range(4)]
    virtuals = [virt_coef, flip(virt_coef, "tile", 1)]
    energies = jnp.stack([virt_energy, flip(virt_energy, "tile", 1)])

    to_before, own_sum, to_after = apply_window(
        lists,
        hams,
        starts,
        occ_before,
        occ_own,
        occ_after,
    )
    levels = [
        lax.dynamic_slice_in_dim(occ_energy, place * width, width, 0)
        for place in (quarter, quarter ^ 1)
    ]
    loaded = [load(array) for array in virtuals]
    points = lax.broadcasted_iota(jnp.int32, xc_kernel.shape, 1)
    scale = jnp.where(points < counts[:, None], 4.0 * xc_kernel, 0.0)
    own_sum, energies, levels, loaded, scale = together(own_sum, energies, levels, loaded, scale)
    size = lax.axis_size("grid")
    from_before = lax.ppermute(to_after, "grid", [(i, (i + 1) % size) for i in range(size)])
    from_after = lax.ppermute(to_before, "grid", [((i + 1) % size, i) for i in range(size)])
    ham_own = (own_sum + from_before.astype(F32) + from_after.astype(F32)).astype(BF16)

    def products(ham_sum):
        dots = [
            lax.dot_general(ham_sum, virt, (((0,), (0,)), ((), ())), preferred_element_type=F32)
            for virt in loaded
        ]
        return jnp.stack(dots)

    own_part, far_part = products(ham_own), products(flip(ham_own, "tile", 2))
    occ_far = column_part(occ_coef, quarter ^ 1, width)
    if lax.axis_size("grid") == 8:
        own = Reduction(own_part, levels[0])
        far = Reduction(far_part, levels[1])
        own.narrow()
        far.narrow()
        far.cross()
        own.across, occ_before, occ_after = together(own.across, occ_before, occ_after)
        own.cross()
        before_far, after_far = flip(occ_before, "tile", 2), flip(occ_after, "tile", 2)
        own.coming, before_far, after_far = together(own.coming, before_far, after_far)
        own_rotation, far_rotation = divide(own.place(), energies, [own, far])
        own.widen(own_rotation)
        far.widen(far_rotation)
        far.part, near = together(far.part, virtuals[1])
        coef_far = far.result([virt_coef, load(near)], BF16, fetched=1)
        coef_own = own.result(virtuals, F32, coef_far)
    else:
        before_far, after_far = flip(occ_before, "tile", 2), flip(occ_after, "tile", 2)
        coefs = []
        for part, level in ((own_part, levels[0]), (far_part, levels[1])):
            total = lax.psum(part, "grid")
            rotation = (total / (level[None, :, None] - energies[:, None, :])).astype(BF16)
            terms = [
                lax.dot_general(virt, rotation[i], NT, preferred_element_type=F32)
                for i, virt in enumerate(virtuals)
            ]
            coefs.append(terms[0] + terms[1])
        coef_own, coef_far = coefs[0], coefs[1].astype(BF16)
    coef_own, coef_far = together(coef_own, flip(coef_far, "tile", 2))
    resp_own = (coef_own + coef_far.astype(F32)).astype(BF16)

    resp_before, resp_after = neighbours(resp_own)
    resp_before_far = flip(resp_before, "tile", 2)
    resp_far, resp_after = together(flip(resp_own, "tile", 2), resp_after)
    resp_after_far = flip(resp_after, "tile", 2)
    first = chip == 0
    half = jnp.concatenate(
        [jnp.where(first, resp_own, resp_far), jnp.where(first, resp_far, resp_own)], axis=1
    )
    overlap_near, occ_window, resp_window = gather_overlaps(
        blocks_near,
        columns,
        [occ_before, before_far, occ_own, occ_far, occ_after, after_far],
        [resp_before, resp_before_far, resp_own, resp_far, resp_after, resp_after_far],
    )
    response_potential, response_coef = density(
        core,
        basis_values,
        overlaps(blocks, columns, occ_window, resp_window),
        flip(overlap_near, "tile", 1),
        scale,
        half,
        flip(half, "tile", 1),
    )
    return (response_coef, response_potential)


def solution(mesh):
    in_specs = (
        P(("grid", "tile"), None, None),
        P(("grid", "tile"), None),
        P(("grid", "tile")),
        P(("grid", "tile"), None),
        P(("grid", "tile"), None),
        P("grid", None),
        P("grid", "tile"),
        P(),
        P("tile"),
    )
    out_specs = (P("grid", None), P(("grid", "tile"), None))
    return jax.shard_map(
        per_device, mesh=mesh, in_specs=in_specs, out_specs=out_specs, check_vma=False
    )
```

```python
import functools
import math

import jax
import jax.numpy as jnp
from jax import lax
from jax.experimental import pallas as pl
from jax.experimental.pallas import tpu as pltpu
from jax.sharding import PartitionSpec as P

VMEM = pl.BlockSpec(memory_space=pltpu.VMEM)
SMEM = pl.BlockSpec(memory_space=pltpu.SMEM)
HBM = pl.BlockSpec(memory_space=pl.ANY)
MIB = 1024 * 1024
F32 = jnp.float32
BF16 = jnp.bfloat16
NT = (((1,), (1,)), ((), ()))


def params(mib=4):
    return pltpu.CompilerParams(vmem_limit_bytes=mib * MIB)


def place_in(array, space):
    return pltpu.with_memory_space_constraint(array, space)


def fetch(copies, semaphores):
    started = [
        pltpu.make_async_copy(source, target, semaphores.at[i])
        for i, (source, target) in enumerate(copies)
    ]
    for copy in started:
        copy.start()
    return started


def load_kernel(source_ref, out_ref, semaphores):
    rows = source_ref.shape[0] // semaphores.shape[0]
    places = [pl.ds(i * rows, rows) for i in range(semaphores.shape[0])]
    for copy in fetch([(source_ref.at[at], out_ref.at[at]) for at in places], semaphores):
        copy.wait()


def load(array):
    parts = 4 if array.shape[0] % 64 == 0 else 1
    return pl.pallas_call(
        load_kernel,
        out_shape=pltpu.VMEM(array.shape, array.dtype),
        in_specs=[HBM],
        out_specs=VMEM,
        scratch_shapes=[pltpu.SemaphoreType.DMA((parts,))],
        compiler_params=params(),
        cost_estimate=pl.CostEstimate(
            flops=0, bytes_accessed=2 * array.size * array.dtype.itemsize, transcendentals=0
        ),
    )(place_in(array, pltpu.HBM))


def load_both_kernel(first_ref, second_ref, first_out, second_out, semaphores):
    copies = [(first_ref, first_out), (second_ref, second_out)]
    for copy in fetch(copies, semaphores):
        copy.wait()


def load_both(arrays):
    return pl.pallas_call(
        load_both_kernel,
        out_shape=[pltpu.VMEM(array.shape, array.dtype) for array in arrays],
        in_specs=[HBM] * 2,
        out_specs=[VMEM] * 2,
        scratch_shapes=[pltpu.SemaphoreType.DMA((2,))],
        compiler_params=params(),
        cost_estimate=pl.CostEstimate(
            flops=0,
            bytes_accessed=2 * sum(array.size * array.dtype.itemsize for array in arrays),
            transcendentals=0,
        ),
    )(place_in(arrays[0], pltpu.HBM), arrays[1])


def split_dot(full, other, dims):
    high = full.astype(BF16)
    low = (full - high.astype(F32)).astype(BF16)
    return lax.dot_general(high, other, dims, preferred_element_type=F32) + lax.dot_general(
        low, other, dims, preferred_element_type=F32
    )


def triangle(size):
    rows = lax.broadcasted_iota(jnp.int32, (size, size), 0)
    return rows, lax.broadcasted_iota(jnp.int32, (size, size), 1)


def live_row(values_ref, counts_ref, b):
    row = values_ref[b : b + 1, :]
    points = lax.broadcasted_iota(jnp.int32, row.shape, 1)
    return jnp.where(points < counts_ref[b], row, 0.0)


def integrate_kernel(start, counts_hbm, basis_hbm, weights_hbm, full_ref, packed_ref, *scratch):
    diagonal, basis_ref, weights_ref, counts_ref, semaphores = scratch
    size = full_ref.shape[0]
    half = full_ref.shape[2] // 2
    row, column = triangle(half)
    cut = -(-size // 2)
    copies = [(counts_hbm, counts_ref), (weights_hbm, weights_ref)]
    for place in (pl.ds(0, cut), pl.ds(cut, size - cut)):
        copies.append((basis_hbm.at[pl.ds(start + place.start, place.size)], basis_ref.at[place]))
    waits = fetch(copies if cut < size else copies[:3], semaphores)
    diagonal[...] = jnp.zeros_like(diagonal)
    for b in range(size):
        if b == 0:
            for copy in waits[:3]:
                copy.wait()
        elif b == cut:
            waits[3].wait()
        values = basis_ref[b]
        weighted = values.astype(F32).T * live_row(weights_ref, counts_ref, start + b)
        ham = split_dot(weighted, values, (((1,), (0,)), ((), ())))
        full_ref[b] = ham.astype(BF16)
        last = ham[half:, half:]
        mixed = jnp.where(row >= column, ham[:half, :half], last)
        packed = jnp.concatenate([ham[:half, half:], mixed], axis=1)
        packed_ref[b * half : (b + 1) * half, :] = packed.astype(BF16)
        line = jnp.sum(jnp.where(row == column, last, 0.0), axis=0, keepdims=True)
        diagonal[b : b + 1, :] = jnp.concatenate([line, jnp.zeros_like(line)], axis=1)
    packed_ref[size * half :, :] = diagonal[...].astype(BF16)


def groups(nbatch):
    first = -(-nbatch // 2)
    return [first, nbatch - first] if nbatch > first else [first]


def padded_rows(nbatch):
    return -(-nbatch // 32) * 32


def integrate(basis_values, counts, weights, start, size):
    _, points, columns = basis_values.shape
    extra = padded_rows(size)
    return pl.pallas_call(
        functools.partial(integrate_kernel, start),
        out_shape=[
            pltpu.VMEM((size, columns, columns), BF16),
            jax.ShapeDtypeStruct((size * columns // 2 + extra, columns), BF16),
        ],
        in_specs=[HBM, HBM, HBM],
        out_specs=[VMEM, VMEM],
        scratch_shapes=[
            pltpu.VMEM((extra, columns), F32),
            pltpu.VMEM((size, points, columns), BF16),
            pltpu.VMEM(weights.shape, F32),
            pltpu.SMEM(counts.shape, jnp.int32),
            pltpu.SemaphoreType.DMA((4,)),
        ],
        compiler_params=params(6),
        cost_estimate=pl.CostEstimate(
            flops=4 * size * points * columns * columns,
            bytes_accessed=size * columns * (points * 2 + columns * 3),
            transcendentals=0,
        ),
    )(*[place_in(array, pltpu.HBM) for array in (counts, basis_values, weights)])


def unpack_kernel(packed_ref, full_ref, diagonal):
    nbatch = full_ref.shape[0]
    half = full_ref.shape[1] // 2
    row, column = triangle(half)
    diagonal[...] = packed_ref[nbatch * half :, :].astype(F32)

    def step(b, carry):
        packed = packed_ref[pl.ds(pl.multiple_of(b * half, half), half), :].astype(F32)
        turned = packed.T
        mixed, mixed_turned = packed[:, half:], turned[half:]
        first = jnp.where(row >= column, mixed, mixed_turned)
        last = jnp.where(row < column, mixed, mixed_turned)
        last = jnp.where(row == column, diagonal[pl.ds(b, 1), :][:, :half], last)
        upper = jnp.concatenate([first, packed[:, :half]], axis=1)
        lower = jnp.concatenate([turned[:half], last], axis=1)
        full_ref[b] = jnp.concatenate([upper, lower], axis=0).astype(BF16)
        return carry

    lax.fori_loop(0, nbatch, step, 0, unroll=4)


def unpack(packed, nbatch, columns):
    return pl.pallas_call(
        unpack_kernel,
        out_shape=jax.ShapeDtypeStruct((nbatch, columns, columns), BF16),
        in_specs=[VMEM],
        out_specs=VMEM,
        scratch_shapes=[pltpu.VMEM((padded_rows(nbatch), columns), F32)],
        compiler_params=params(),
        cost_estimate=pl.CostEstimate(
            flops=nbatch * columns * columns * 4,
            bytes_accessed=nbatch * columns * columns * 3,
            transcendentals=0,
        ),
    )(packed)


def row_places(block_ref, b, rows):
    return [
        pl.ds(pl.multiple_of(block_ref[b, j] * rows, rows), rows) for j in range(block_ref.shape[1])
    ]


def apply_kernel(starts, rows, *refs):
    pieces, lists = len(starts), len(refs) - len(starts) - 8
    block_refs, refs = refs[:lists] * (pieces // lists), refs[lists:]
    ham_refs, window_refs = refs[:pieces], refs[pieces : pieces + 3]
    out_before, out_own, out_after, window, total = refs[pieces + 3 :]
    region = window_refs[0].shape[0]
    for side, ref in enumerate(window_refs):
        window[side * region : (side + 1) * region] = ref[...]
    total[...] = jnp.zeros_like(total)

    def steps(members, count):
        def step(b, carry):
            places, products = [], []
            for p, first in members:
                place = row_places(block_refs[p], starts[p] + first + b, rows)
                picked = jnp.concatenate([window[at, :] for at in place], axis=0)
                products.append(jnp.dot(ham_refs[p][first + b], picked, preferred_element_type=F32))
                places.append(place)
            for place, product in zip(places, products):
                for j, at in enumerate(place):
                    total[at, :] += product[j * rows : (j + 1) * rows]
            return carry

        lax.fori_loop(0, count, step, 0, unroll=12)

    shares = {}
    smallest = min(ref.shape[0] for ref in ham_refs)
    for p, ref in enumerate(ham_refs):
        for first in range(0, ref.shape[0], smallest):
            count = min(smallest, ref.shape[0] - first)
            shares.setdefault(count, []).append((p, first))
    for count, members in shares.items():
        steps(members, count)
    out_before[...] = total[:region].astype(BF16)
    out_own[...] = total[region : 2 * region]
    out_after[...] = total[2 * region :].astype(BF16)


def apply_window(blocks, hams, starts, before, own, after):
    pieces, per_batch = len(hams), blocks[0].shape[1]
    columns = hams[0].shape[1]
    region, width = own.shape
    work = sum(ham.shape[0] for ham in hams)
    return pl.pallas_call(
        functools.partial(apply_kernel, starts, columns // per_batch),
        out_shape=[
            jax.ShapeDtypeStruct((region, width), BF16),
            jax.ShapeDtypeStruct((region, width), F32),
            jax.ShapeDtypeStruct((region, width), BF16),
        ],
        in_specs=[SMEM] * len(blocks) + [VMEM] * (pieces + 3),
        out_specs=[VMEM] * 3,
        scratch_shapes=[
            pltpu.VMEM((3 * region, width), BF16),
            pltpu.VMEM((3 * region, width), F32),
        ],
        compiler_params=params(6),
        cost_estimate=pl.CostEstimate(
            flops=2 * work * columns * columns * width,
            bytes_accessed=work * columns * columns * 2 + 14 * region * width,
            transcendentals=0,
        ),
    )(
        *blocks,
        *hams,
        *[place_in(array, pltpu.VMEM) for array in (before, own, after)],
    )


def expand_kernel(fetched, first_ref, part_ref, coming_ref, *refs):
    sources, (out_ref, held, semaphores) = refs[:2], refs[-3:]
    blocks = semaphores.shape[0] // max(fetched, 1)
    rows = out_ref.shape[0] // blocks
    copies = []
    for i in range(blocks):
        place = pl.ds(i * rows, rows)
        for share in range(fetched):
            copies.append((sources[share].at[place], held.at[share, place]))
    waits = fetch(copies, semaphores)
    places = [held.at[share] if share < fetched else sources[share] for share in range(2)]
    low = first_ref[0] == 0
    rotations = []
    for share in range(2):
        part, coming = part_ref[share], coming_ref[share]
        halves = [jnp.where(low, part, coming), jnp.where(low, coming, part)]
        rotations.append(jnp.concatenate(halves, axis=0))
    for i in range(blocks):
        at = slice(i * rows, (i + 1) * rows)
        total = None
        for share in reversed(range(2)):
            if share < fetched:
                waits[fetched * i + share].wait()
            product = lax.dot_general(
                places[share][at], rotations[share], NT, preferred_element_type=F32
            )
            total = product if total is None else total + product
        out_ref[at] = total.astype(out_ref.dtype)


def expand(first, part, coming, virtuals, kind, ahead, fetched):
    region, virt = virtuals[0].shape
    width = 2 * part.shape[1]
    blocks = 4 if region % 64 == 0 and region > 64 else 1
    near = virtuals[1] if fetched == 2 else place_in(virtuals[1], pltpu.VMEM)
    own = place_in(virtuals[0], pltpu.HBM if fetched else pltpu.VMEM)
    return pl.pallas_call(
        functools.partial(expand_kernel, fetched),
        out_shape=jax.ShapeDtypeStruct((region, width), kind),
        in_specs=[SMEM, VMEM, VMEM, HBM if fetched else VMEM, HBM if fetched == 2 else VMEM]
        + [HBM] * len(ahead),
        out_specs=VMEM,
        scratch_shapes=[
            pltpu.VMEM((fetched, region, virt) if fetched else (16, 128), BF16),
            pltpu.SemaphoreType.DMA((max(fetched, 1) * blocks,)),
        ],
        compiler_params=params(6 + 4 * fetched),
        cost_estimate=pl.CostEstimate(
            flops=4 * region * width * virt if kind == BF16 else 0,
            bytes_accessed=4 * region * virt if kind == BF16 else 0,
            transcendentals=0,
        ),
    )(first.reshape(1), part, coming, own, near, *ahead)


def overlap_steps(block_ref, occ_ref, resp_ref, out_ref, rows):
    def step(b, carry):
        place = row_places(block_ref, b, rows)
        left = jnp.concatenate([resp_ref[at, :] for at in place], axis=0)
        right = jnp.concatenate([occ_ref[at, :] for at in place], axis=0)
        product = lax.dot_general(left, right, NT, preferred_element_type=F32)
        out_ref[b] = product.astype(out_ref.dtype)
        return carry

    lax.fori_loop(0, out_ref.shape[0], step, 0, unroll=24)


def gather_kernel(rows, block_ref, *refs):
    sources, (out_ref, occ_ref, resp_ref, semaphores) = refs[:12], refs[12:]
    region, width = sources[0].shape
    copies = []
    for i, source in enumerate(sources):
        target, side, part = (occ_ref, resp_ref)[i // 6], i % 6 // 2, i % 2
        place = (pl.ds(side * region, region), pl.ds(part * width, width))
        copies.append((source, target.at[place]))
    for copy in fetch(copies, semaphores):
        copy.wait()
    overlap_steps(block_ref, occ_ref, resp_ref, out_ref, rows)


def gather_overlaps(blocks, columns, occ_parts, resp_parts):
    nbatch, per_batch = blocks.shape
    region, width = occ_parts[0].shape
    return pl.pallas_call(
        functools.partial(gather_kernel, columns // per_batch),
        out_shape=[jax.ShapeDtypeStruct((nbatch, columns, columns), BF16)]
        + [pltpu.VMEM((3 * region, 2 * width), BF16)] * 2,
        in_specs=[SMEM] + [HBM] * 12,
        out_specs=[VMEM] * 3,
        scratch_shapes=[pltpu.SemaphoreType.DMA((12,))],
        compiler_params=params(),
        cost_estimate=pl.CostEstimate(
            flops=4 * nbatch * columns * columns * width,
            bytes_accessed=24 * region * width + nbatch * columns * columns * 2,
            transcendentals=0,
        ),
    )(blocks, *occ_parts, *resp_parts)


def overlap_kernel(rows, block_ref, occ_ref, resp_ref, out_ref):
    overlap_steps(block_ref, occ_ref, resp_ref, out_ref, rows)


def overlaps(blocks, columns, occ_window, resp_window):
    nbatch, per_batch = blocks.shape
    return pl.pallas_call(
        functools.partial(overlap_kernel, columns // per_batch),
        out_shape=pltpu.VMEM((nbatch, columns, columns), F32),
        in_specs=[SMEM, VMEM, VMEM],
        out_specs=VMEM,
        compiler_params=params(),
        cost_estimate=pl.CostEstimate(
            flops=2 * nbatch * columns * columns * occ_window.shape[1],
            bytes_accessed=nbatch * columns * columns * 4,
            transcendentals=0,
        ),
    )(blocks, place_in(occ_window, pltpu.VMEM), place_in(resp_window, pltpu.VMEM))


def density_kernel(
    core_ref, basis_ref, first_ref, second_ref, scale_ref, half_ref, near_ref,
    out_ref, coef_ref, semaphores,
):
    width = half_ref.shape[1]
    copies = []
    for source, place in ((half_ref, core_ref[0]), (near_ref, 1 - core_ref[0])):
        columns = pl.ds(pl.multiple_of(place * width, width), width)
        copies.append((source, coef_ref.at[:, columns]))
    waits = fetch(copies, semaphores)
    for b in range(basis_ref.shape[0]):
        values = basis_ref[b]
        overlap = first_ref[b] + second_ref[b].astype(F32)
        product = split_dot(overlap, values, NT)
        density = jnp.sum(product * values.astype(F32).T, axis=0, keepdims=True)
        out_ref[b : b + 1, :] = scale_ref[b : b + 1, :] * density
    for copy in waits:
        copy.wait()


def density(core, basis_values, first, second, scale, half, half_near):
    nbatch, points, columns = basis_values.shape
    region, width = half.shape
    return pl.pallas_call(
        density_kernel,
        out_shape=[
            jax.ShapeDtypeStruct((nbatch, points), F32),
            jax.ShapeDtypeStruct((region, 2 * width), BF16),
        ],
        in_specs=[SMEM] + [VMEM] * 4 + [HBM] * 2,
        out_specs=[VMEM, HBM],
        scratch_shapes=[pltpu.SemaphoreType.DMA((2,))],
        compiler_params=params(),
        cost_estimate=pl.CostEstimate(
            flops=4 * nbatch * points * columns * columns,
            bytes_accessed=basis_values.size * 2 + nbatch * columns * columns * 6,
            transcendentals=0,
        ),
    )(core.reshape(1), basis_values, place_in(first, pltpu.VMEM), second, scale, half, half_near)


def flip(array, axis, mask):
    return lax.ppermute(array, axis, [(i, i ^ mask) for i in range(lax.axis_size(axis))])


def neighbours(array):
    size = lax.axis_size("grid")
    before = lax.ppermute(array, "grid", [(i, (i + 1) % size) for i in range(size)])
    after = lax.ppermute(array, "grid", [((i + 1) % size, i) for i in range(size)])
    return before, after


def column_part(array, index, width):
    return lax.dynamic_slice_in_dim(array, index * width, width, 1)


def trade(array, rows, choice):
    keep = lax.dynamic_slice_in_dim(array, choice * rows, rows, 1)
    return keep, lax.dynamic_slice_in_dim(array, (1 - choice) * rows, rows, 1).astype(BF16)


def join(own, other, choice):
    low, high = jnp.where(choice == 0, own, other), jnp.where(choice == 0, other, own)
    return jnp.concatenate([low, high], axis=1)


def swap(array, masks):
    size, tiles = lax.axis_size("grid"), lax.axis_size("tile")
    pairs = [
        (g * tiles + t, (g ^ masks[t % 2]) * tiles + t) for g in range(size) for t in range(tiles)
    ]
    return lax.ppermute(array, ("grid", "tile"), pairs)


def together(*arrays):
    return lax.optimization_barrier(arrays)


def divide_kernel(place_ref, energy_ref, *refs):
    chunks = len(refs) // 4
    rows = refs[0].shape[1]
    place = pl.multiple_of(place_ref[0], rows)
    for c in range(chunks):
        total_ref, coming_ref, level_ref, out_ref = refs[3 * c : 3 * c + 3] + (refs[3 * chunks + c],)
        level = level_ref[pl.ds(place, rows), :]
        for share in range(total_ref.shape[0]):
            total = total_ref[share] + coming_ref[share].astype(F32)
            gap = level - energy_ref[share : share + 1, :]
            out_ref[share] = (total / gap).astype(out_ref.dtype)


def divide(place, energies, chunks):
    shape = chunks[0].total.shape
    operands = []
    for chunk in chunks:
        operands += [chunk.total, chunk.coming, chunk.level[:, None]]
    return pl.pallas_call(
        divide_kernel,
        out_shape=[pltpu.VMEM(shape, BF16)] * len(chunks),
        in_specs=[SMEM] + [VMEM] * (1 + len(operands)),
        out_specs=[VMEM] * len(chunks),
        compiler_params=params(),
        cost_estimate=pl.CostEstimate(
            flops=len(chunks) * math.prod(shape) * 8, bytes_accessed=0, transcendentals=0
        ),
    )(place.reshape(1), energies, *operands)


class Reduction:
    def __init__(self, part, level):
        grid, core = lax.axis_index("grid"), lax.axis_index("tile") % 2
        self.masks = (1, 2), (2, 1)
        self.first, self.second = (grid >> core) & 1, (grid >> (1 - core)) & 1
        self.level = level
        self.half = part.shape[1] // 2
        self.keep, send = trade(part, self.half, self.first)
        self.coming = swap(send, self.masks[0])

    def narrow(self):
        total = self.keep + self.coming.astype(F32)
        self.keep, send = trade(total, self.half // 2, self.second)
        self.total = self.keep + swap(send, self.masks[1]).astype(F32)
        self.total, self.across = together(self.total, self.total.astype(BF16))

    def cross(self):
        self.coming = flip(self.across, "grid", 4)

    def place(self):
        return self.first * self.half + self.second * (self.half // 2)

    def widen(self, own):
        self.part = join(own, swap(own, self.masks[1]), self.second)
        self.coming = swap(self.part, self.masks[0])

    def result(self, virtuals, kind, *ahead, fetched=2):
        return expand(self.first, self.part, self.coming, virtuals, kind, ahead, fetched)


def per_device(
    basis_values,
    blocks,
    counts,
    weighted_potential,
    xc_kernel,
    occ_coef,
    virt_coef,
    occ_energy,
    virt_energy,
):
    nbatch, _, columns = basis_values.shape
    region, occ_count = occ_coef.shape
    width = occ_count // lax.axis_size("tile")
    tile = lax.axis_index("tile")
    chip, core = tile // 2, tile % 2
    quarter = 2 * core + chip

    occ_own = column_part(occ_coef, quarter, width)

    lists = [blocks, flip(blocks, "tile", 1), flip(blocks, "tile", 2)]
    occ_before, occ_after = neighbours(occ_own)
    sizes, fulls, arrived = groups(nbatch), [], []
    for i, size in enumerate(sizes):
        full, packed = integrate(basis_values, counts, weighted_potential, sum(sizes[:i]), size)
        fulls.append(full)
        arrived.append(flip(packed, "tile", 2))
    arrived[0], occ_before, occ_after = together(arrived[0], occ_before, occ_after)
    far = [unpack(array, size, columns) for array, size in zip(arrived, sizes)]
    far[0], lists[2] = together(far[0], lists[2])
    lists.append(flip(lists[2], "tile", 1))
    hams = []
    for full, other in zip(fulls, far):
        hams += [full, flip(full, "tile", 1), other, flip(other, "tile", 1)]
    blocks_near = lists[1]
    starts = [sum(sizes[:i]) for i in range(len(sizes)) for _ in range(4)]
    virtuals = [virt_coef, flip(virt_coef, "tile", 1)]
    energies = jnp.stack([virt_energy, flip(virt_energy, "tile", 1)])

    to_before, own_sum, to_after = apply_window(
        lists,
        hams,
        starts,
        occ_before,
        occ_own,
        occ_after,
    )
    levels = [
        lax.dynamic_slice_in_dim(occ_energy, place * width, width, 0)
        for place in (quarter, quarter ^ 1)
    ]
    loaded = [load(array) for array in virtuals]
    points = lax.broadcasted_iota(jnp.int32, xc_kernel.shape, 1)
    scale = jnp.where(points < counts[:, None], 4.0 * xc_kernel, 0.0)
    own_sum, energies, levels, loaded, scale = together(own_sum, energies, levels, loaded, scale)
    size = lax.axis_size("grid")
    from_before = lax.ppermute(to_after, "grid", [(i, (i + 1) % size) for i in range(size)])
    from_after = lax.ppermute(to_before, "grid", [((i + 1) % size, i) for i in range(size)])
    ham_own = (own_sum + from_before.astype(F32) + from_after.astype(F32)).astype(BF16)

    def products(ham_sum):
        dots = [
            lax.dot_general(ham_sum, virt, (((0,), (0,)), ((), ())), preferred_element_type=F32)
            for virt in loaded
        ]
        return jnp.stack(dots)

    own_part, far_part = products(ham_own), products(flip(ham_own, "tile", 2))
    occ_far = column_part(occ_coef, quarter ^ 1, width)
    if lax.axis_size("grid") == 8:
        own = Reduction(own_part, levels[0])
        far = Reduction(far_part, levels[1])
        own.narrow()
        far.narrow()
        far.cross()
        own.across, occ_before, occ_after = together(own.across, occ_before, occ_after)
        own.cross()
        before_far, after_far = flip(occ_before, "tile", 2), flip(occ_after, "tile", 2)
        own.coming, before_far, after_far = together(own.coming, before_far, after_far)
        own_rotation, far_rotation = divide(own.place(), energies, [own, far])
        own.widen(own_rotation)
        far.widen(far_rotation)
        far.part, near = together(far.part, virtuals[1])
        coef_far = far.result(load_both([virt_coef, near]), BF16, fetched=0)
        coef_own = own.result(virtuals, F32, coef_far)
    else:
        before_far, after_far = flip(occ_before, "tile", 2), flip(occ_after, "tile", 2)
        coefs = []
        for part, level in ((own_part, levels[0]), (far_part, levels[1])):
            total = lax.psum(part, "grid")
            rotation = (total / (level[None, :, None] - energies[:, None, :])).astype(BF16)
            terms = [
                lax.dot_general(virt, rotation[i], NT, preferred_element_type=F32)
                for i, virt in enumerate(virtuals)
            ]
            coefs.append(terms[0] + terms[1])
        coef_own, coef_far = coefs[0], coefs[1].astype(BF16)
    coef_own, coef_far = together(coef_own, flip(coef_far, "tile", 2))
    resp_own = (coef_own + coef_far.astype(F32)).astype(BF16)

    resp_before, resp_after = neighbours(resp_own)
    resp_before_far = flip(resp_before, "tile", 2)
    resp_far, resp_after = together(flip(resp_own, "tile", 2), resp_after)
    resp_after_far = flip(resp_after, "tile", 2)
    first = chip == 0
    half = jnp.concatenate(
        [jnp.where(first, resp_own, resp_far), jnp.where(first, resp_far, resp_own)], axis=1
    )
    overlap_near, occ_window, resp_window = gather_overlaps(
        blocks_near,
        columns,
        [occ_before, before_far, occ_own, occ_far, occ_after, after_far],
        [resp_before, resp_before_far, resp_own, resp_far, resp_after, resp_after_far],
    )
    response_potential, response_coef = density(
        core,
        basis_values,
        overlaps(blocks, columns, occ_window, resp_window),
        flip(overlap_near, "tile", 1),
        scale,
        half,
        flip(half, "tile", 1),
    )
    return (response_coef, response_potential)


def solution(mesh):
    in_specs = (
        P(("grid", "tile"), None, None),
        P(("grid", "tile"), None),
        P(("grid", "tile")),
        P(("grid", "tile"), None),
        P(("grid", "tile"), None),
        P("grid", None),
        P("grid", "tile"),
        P(),
        P("tile"),
    )
    out_specs = (P("grid", None), P(("grid", "tile"), None))
    return jax.shard_map(
        per_device, mesh=mesh, in_specs=in_specs, out_specs=out_specs, check_vma=False
    )
```
